32 devices in a mesh: expert: 4 (over x, core), dp: 8 (over z, y).
Axes of the slice: x: 2, y: 2, z: 4, core: 2. Of those that a mesh axis runs over, the one named last changes fastest.
Arguments:
- out_grad: bfloat16 [2048, 3072], P(('expert', 'dp')), may hold values from -6 to 6
- gate_saved: bfloat16 [2048, 2, 8192], P('expert', None, 'dp'), may hold values from -6 to 6
- up_saved: bfloat16 [2048, 2, 8192], P('expert', None, 'dp'), may hold values from -6 to 6
- routing: int32 [2048, 2], P('expert'), may hold values from 0 to 3, all different within a row; in each aligned block of 512 rows (0 to 511, 512 to 1023, ...) at most 512 rows name the same one
- down_weight: bfloat16 [4, 3072, 8192], P('expert', None, 'dp'), may hold values from -0.0625 to 0.0625
- momentum: bfloat16 [4, 3072, 8192], P('expert', 'dp'), may hold values from -60 to 60
Outputs:
- d_gate: bfloat16 [2048, 2, 8192], P('expert', None, 'dp')
- d_up: bfloat16 [2048, 2, 8192], P('expert', None, 'dp')
- new_weight: float32 [4, 3072, 8192], P('expert', 'dp')
- new_momentum: bfloat16 [4, 3072, 8192], P('expert', 'dp')
The draws below stay inside these ranges and needn't reach their ends.
Inputs may be any that keep to these rules, and one draw needn't show every extreme that they name: `routing`: in each aligned block of 512 tokens (one group), the 2 experts of a token differ, no expert is named by more than 512 tokens, a bound that some block reaches.
All inputs are finite; a program needn't handle non-finite values.
Results may differ from the reference program's by a relative error of at most 0.0015.
Values may be sent and summed in bfloat16 or wider, within the bound.
No kernel may reach another device: no remote copies, remote signals or barrier semaphores. Data moves between devices by JAX's collectives and lax.ppermute only.
A program may use at most 128 MiB of HBM per device.

```python
import math
import jax
import jax.numpy as jnp
import numpy as np

D = 3072
FF = 8192
TOPK = 2
GROUP_TOK = 512
EXPERTS = 4
TOKENS = 2048
CAP = 512


def level_of(rng, dims, cuts, low, high):
    def one(dim, blocks):
        steps = jax.random.uniform(jax.random.fold_in(jax.random.fold_in(rng, 6), dim), (blocks,), jnp.float32, low / len(cuts), high / len(cuts))
        return jnp.repeat(jnp.exp(steps), dims[dim] // blocks).reshape((-1,) + (1,) * (len(dims) - dim - 1))

    loudness = one(*cuts[0])
    for cut in cuts[1:]:
        loudness = loudness * one(*cut)
    return loudness


def routed_block(rng, own, number, rows, number_of, top, bound, skew):
    order = jax.random.permutation(rng, number_of)
    heavy_load, common = portions_of(number_of, rows * top, bound, skew, True), portions_of(number_of, rows * top, bound, skew, False)
    places = jnp.arange(number_of)

    def named(tallies, rotation):
        used = int((tallies > 0).sum())
        fixed = max(1, used // 4)
        passed = fixed + (places - fixed + rotation * (used - fixed)) % max(1, number_of - fixed)
        return jnp.zeros((number_of,), jnp.int32).at[order[jnp.where(places < fixed, places, passed)]].set(jnp.asarray(tallies, jnp.int32))

    tallies = jnp.where(number % 4 == 0, named(heavy_load, number // 4), named(common, number - number // 4 - 1))
    mixed = jax.random.permutation(jax.random.fold_in(own, 3), number_of)
    giver, receiver = mixed[0:number_of // 2 * 2:2], mixed[1:number_of // 2 * 2:2]
    slack = jnp.minimum(tallies[giver] - 1, bound - tallies[receiver]) // 2
    slack = jnp.where((giver == order[0]) | (receiver == order[0]) | (tallies[receiver] == 0), 0, jnp.maximum(slack, 0))
    passed = jax.random.randint(jax.random.fold_in(own, 4), (number_of // 2,), 0, 1 << 20) % (slack + 1)
    tallies = tallies.at[giver].add(-passed).at[receiver].add(passed)
    labels = jnp.searchsorted(jnp.cumsum(tallies), jnp.arange(rows * top), side="right").astype(jnp.int32)
    table = labels.reshape(top, rows).T
    table = table[jax.random.permutation(jax.random.fold_in(own, 1), rows)]
    rotation = jax.random.randint(jax.random.fold_in(own, 2), (rows, 1), 0, top)
    return jnp.take_along_axis(table, (jnp.arange(top)[None, :] + rotation) % top, axis=1)


def portions_of(count, total, most, slope, full):
    portions = [(1 << 20) // math.isqrt(standing ** slope) + 1 for standing in range(1, count + 1)]
    largest = most if full else min(most, max(-(-total // count), total * portions[0] // sum(portions)))
    least = 1 if total - largest >= count - 1 else 0
    counts, surplus = [largest] + [least] * (count - 1), total - largest - least * (count - 1)
    while surplus > 0:
        movable = [i for i in range(1, count) if counts[i] < largest] or [i for i in range(1, count) if counts[i] < most]
        mass, left = sum([portions[i] for i in movable]), surplus
        for i in movable:
            extra = min(most - counts[i], max(1, left * portions[i] // mass), surplus)
            counts[i] = counts[i] + extra
            surplus = surplus - extra
    return np.array(counts)


def centred(own_key, extent, spread, limit, pieces=(), held_as=jnp.bfloat16):
    array = jax.random.normal(own_key, extent, jnp.float32) * spread
    if len(pieces) > 0:
        array = level_of(own_key, extent, pieces, -0.22, 0.18) * array
    return jnp.clip(array, min=-limit, max=limit).astype(held_as)


def setup_inputs(seed: int = 0) -> dict:
    splits = jax.random.split(jax.random.key(seed), 7)
    out_grad = centred(splits[0], (TOKENS, D), 1.0, 6.0, ((0, 32),))
    gate_saved = centred(splits[1], (TOKENS, TOPK, FF), 1.0, 6.0, ((0, 4), (2, 8)))
    up_saved = centred(splits[2], (TOKENS, TOPK, FF), 1.0, 6.0, ((0, 4), (2, 8)))
    routing_keys = jax.random.split(jax.random.fold_in(splits[3], 1), TOKENS // GROUP_TOK)
    routing_turns = jax.random.permutation(jax.random.fold_in(splits[3], 3), TOKENS // GROUP_TOK)
    routing = jax.vmap(lambda own, number: routed_block(jax.random.fold_in(splits[3], 2), own, number, GROUP_TOK, EXPERTS, TOPK, CAP, 2))(routing_keys, routing_turns).reshape((TOKENS, TOPK))
    down_weight = centred(splits[4], (EXPERTS, D, FF), FF ** -0.5, 0.0625, ((0, 4), (2, 8)))
    momentum = centred(splits[5], (EXPERTS, D, FF), 10.0, 60.0, ((0, 4), (1, 8)))
    return dict(out_grad=out_grad, gate_saved=gate_saved, up_saved=up_saved, routing=routing, down_weight=down_weight, momentum=momentum)


beta_first = 0.9
beta_second = 0.99
step_rate = 0.01
decay_rate = 1.0
sign_width = 10.0


def slot_table(flat_route, experts, capacity):
    count_rows = flat_route.shape[0]
    onehot = (flat_route[:, None] == jnp.arange(experts, dtype=jnp.int32)[None, :]).astype(jnp.int32)
    before = jnp.cumsum(onehot, axis=0) - onehot
    place = jnp.sum(before * onehot, axis=1).astype(jnp.int32)
    table = jnp.full((experts, capacity), count_rows, jnp.int32)
    table = table.at[flat_route, place].set(jnp.arange(count_rows, dtype=jnp.int32))
    return table, jnp.sum(onehot, axis=0)


def reference(out_grad, gate_saved, up_saved, routing, down_weight, momentum):
    group_tok = GROUP_TOK
    count_rows = group_tok * TOPK
    gate_all = gate_saved.reshape(EXPERTS, count_rows, FF).astype(jnp.float32)
    up_all = up_saved.reshape(EXPERTS, count_rows, FF).astype(jnp.float32)
    sigma = jax.nn.sigmoid(gate_all)
    hidden = (gate_all * sigma * up_all).astype(jnp.bfloat16)
    grads = out_grad.reshape(EXPERTS, group_tok, D)
    route = routing.reshape(EXPERTS, count_rows).astype(jnp.int32)
    tables = []
    grads_pad = []
    hidden_pad = []
    for group in range(EXPERTS):
        tables.append(slot_table(route[group], EXPERTS, CAP)[0])
        grads_pad.append(jnp.concatenate([grads[group], jnp.zeros((1, D), jnp.bfloat16)], axis=0))
        hidden_pad.append(jnp.concatenate([hidden[group], jnp.zeros((1, FF), jnp.bfloat16)], axis=0))
    deriv = [jnp.zeros((count_rows + 1, FF), jnp.float32) for group in range(EXPERTS)]
    weights_out = []
    moments_out = []
    for expert in range(EXPERTS):
        carried = jnp.zeros((D, FF), jnp.bfloat16)
        for step in range(EXPERTS):
            group = (expert + step) % EXPERTS
            index = tables[group][expert]
            upstream = grads_pad[group][index // TOPK]
            picked = hidden_pad[group][index]
            deriv[group] = deriv[group].at[index].set(jnp.dot(upstream, down_weight[expert], preferred_element_type=jnp.float32))
            term = jnp.dot(upstream.T, picked, preferred_element_type=jnp.float32)
            carried = (carried.astype(jnp.float32) + term).astype(jnp.bfloat16)
        grad = carried.astype(jnp.float32)
        moment = momentum[expert].astype(jnp.float32)
        mix = beta_first * moment + (1.0 - beta_first) * grad
        weights_out.append(down_weight[expert].astype(jnp.float32) * (1.0 - step_rate * decay_rate) - step_rate * jnp.tanh(mix / sign_width))
        moments_out.append((beta_second * moment + (1.0 - beta_second) * grad).astype(jnp.bfloat16))
    dh = jnp.stack([deriv[group][:count_rows] for group in range(EXPERTS)])
    d_up = (dh * gate_all * sigma).astype(jnp.bfloat16).reshape(TOKENS, TOPK, FF)
    d_gate = (dh * up_all * sigma * (1.0 + gate_all * (1.0 - sigma))).astype(jnp.bfloat16).reshape(TOKENS, TOPK, FF)
    return d_gate, d_up, jnp.stack(weights_out), jnp.stack(moments_out)
```

```python
import functools

import jax
import jax.numpy as jnp
from jax import lax
from jax.experimental import pallas as pl
from jax.experimental.pallas import tpu as pltpu
from jax.sharding import PartitionSpec as P

beta_first = 0.9
beta_second = 0.99
step_rate = 0.01
decay_rate = 1.0
sign_width = 10.0


def swapped(array, axis, mask):
    size = lax.axis_size(axis)
    return lax.ppermute(array, axis, [(i, i ^ mask) for i in range(size)])


def update_kernel(grad_ref, weight_ref, momentum_ref, new_weight_ref, new_momentum_ref):
    grad = grad_ref[0].astype(jnp.float32)
    moment = momentum_ref[0].astype(jnp.float32)
    weight = weight_ref[0].astype(jnp.float32)
    mix = beta_first * moment + (1.0 - beta_first) * grad
    new_weight_ref[0] = weight * (1.0 - step_rate * decay_rate) - step_rate * jnp.tanh(
        mix / sign_width
    )
    new_momentum_ref[0] = (beta_second * moment + (1.0 - beta_second) * grad).astype(
        jnp.bfloat16
    )


def update(grad, weight, momentum):
    sources, rows, cols = grad.shape
    block = pl.BlockSpec((1, rows, cols), lambda s: (s, 0, 0))
    wide = pl.BlockSpec((1, rows, cols), lambda s: (0, 0, s))
    return pl.pallas_call(
        update_kernel,
        grid=(sources,),
        in_specs=[block, block, wide],
        out_specs=[wide, wide],
        out_shape=[
            jax.ShapeDtypeStruct(momentum.shape, jnp.float32),
            jax.ShapeDtypeStruct(momentum.shape, jnp.bfloat16),
        ],
        compiler_params=pltpu.CompilerParams(vmem_limit_bytes=32 * 1024 * 1024),
        cost_estimate=pl.CostEstimate(
            flops=10 * momentum.size, bytes_accessed=12 * momentum.size, transcendentals=momentum.size
        ),
        name="lion_step",
    )(grad, weight, momentum)


def body(out_grad, gate_saved, up_saved, routing, down_weight, momentum):
    experts = lax.axis_size("expert")
    shards = lax.axis_size("dp")
    group_tok, topk, cols = gate_saved.shape
    width = out_grad.shape[1]
    rows = momentum.shape[1]
    mine = lax.axis_index("expert")

    weight_shards = lax.all_to_all(
        down_weight.reshape(shards, rows, cols), "dp", split_axis=0, concat_axis=0, tiled=True
    )

    tokens = {0: lax.all_gather(out_grad, "dp", axis=0, tiled=True)}
    for m in sorted(range(1, experts), key=lambda m: (bin(m).count("1"), -m)):
        low = m & -m
        tokens[m] = swapped(tokens[m ^ low], "expert", low)

    gate = gate_saved.astype(jnp.float32)
    up = up_saved.astype(jnp.float32)
    sigma = jax.nn.sigmoid(gate)
    hidden = (gate * sigma * up).astype(jnp.bfloat16)

    rows_of = {}
    for m in range(experts):
        chosen = (routing == (mine ^ m))[:, :, None]
        picked = jnp.sum(jnp.where(chosen, hidden, jnp.zeros_like(hidden)), axis=1)
        rows_of[m] = swapped(picked, "expert", m) if m else picked

    weight = down_weight[0]
    deriv = jnp.zeros(gate.shape, jnp.float32)
    term = jnp.zeros((width, cols), jnp.float32)
    for m in range(experts):
        part = jnp.dot(tokens[m], weight, preferred_element_type=jnp.float32)
        back = swapped(part, "expert", m) if m else part
        chosen = (routing == (mine ^ m))[:, :, None]
        deriv = jnp.where(chosen, back[:, None, :], deriv)
        term = term + lax.dot_general(
            tokens[m], rows_of[m], (((0,), (0,)), ((), ())), preferred_element_type=jnp.float32
        )

    grad_shards = lax.all_to_all(
        term.astype(jnp.bfloat16).reshape(shards, rows, cols),
        "dp",
        split_axis=0,
        concat_axis=0,
        tiled=True,
    )
    d_up = (deriv * gate * sigma).astype(jnp.bfloat16)
    d_gate = (deriv * up * sigma * (1.0 + gate * (1.0 - sigma))).astype(jnp.bfloat16)
    new_weight, new_momentum = update(grad_shards, weight_shards, momentum)
    return (d_gate, d_up, new_weight, new_momentum)


def solution(mesh):
    placed = (
        P(("expert", "dp"), None),
        P("expert", None, "dp"),
        P("expert", None, "dp"),
        P("expert", None),
        P("expert", None, "dp"),
        P("expert", "dp", None),
    )
    return jax.shard_map(
        body,
        mesh=mesh,
        in_specs=placed,
        out_specs=(
            P("expert", None, "dp"),
            P("expert", None, "dp"),
            P("expert", "dp", None),
            P("expert", "dp", None),
        ),
        check_vma=False,
    )
```

```python
import functools

import jax
import jax.numpy as jnp
from jax import lax
from jax.experimental import pallas as pl
from jax.experimental.pallas import tpu as pltpu
from jax.sharding import PartitionSpec as P

beta_first = 0.9
beta_second = 0.99
step_rate = 0.01
decay_rate = 1.0
sign_width = 10.0


def swapped(array, axis, mask):
    size = lax.axis_size(axis)
    return lax.ppermute(array, axis, [(i, i ^ mask) for i in range(size)])


def update_kernel(grad_ref, weight_ref, momentum_ref, *refs):
    new_weight_ref, new_momentum_ref = refs[-2:]
    grad = grad_ref[0].astype(jnp.float32)
    moment = momentum_ref[0].astype(jnp.float32)
    weight = weight_ref[0].astype(jnp.float32)
    mix = beta_first * moment + (1.0 - beta_first) * grad
    new_weight_ref[0] = weight * (1.0 - step_rate * decay_rate) - step_rate * jnp.tanh(
        mix / sign_width
    )
    new_momentum_ref[0] = (beta_second * moment + (1.0 - beta_second) * grad).astype(
        jnp.bfloat16
    )


def update(part, parts, grad, weight, momentum, done):
    sources, rows, cols = grad.shape
    own = pl.BlockSpec((1, rows, cols), lambda s: (s, 0, 0))
    half = pl.BlockSpec((1, rows, cols), lambda s: (s, 0, part))
    wide = pl.BlockSpec((1, rows, cols), lambda s: (0, 0, s * parts + part))
    size = grad.size
    return pl.pallas_call(
        update_kernel,
        grid=(sources,),
        in_specs=[own, half, wide] + [pl.BlockSpec(memory_space=pl.ANY)] * len(done),
        out_specs=[wide, wide],
        out_shape=[
            jax.ShapeDtypeStruct(momentum.shape, jnp.float32),
            jax.ShapeDtypeStruct(momentum.shape, jnp.bfloat16),
        ],
        input_output_aliases={3 + i: i for i in range(len(done))},
        compiler_params=pltpu.CompilerParams(vmem_limit_bytes=32 * 1024 * 1024),
        cost_estimate=pl.CostEstimate(flops=10 * size, bytes_accessed=12 * size, transcendentals=size),
        name="lion_step",
    )(grad, weight, momentum, *done)


def term_kernel(count, *refs):
    tokens, hidden, out_ref = refs[:count], refs[count : 2 * count], refs[-1]
    total = None
    for token_ref, hidden_ref in zip(tokens, hidden):
        one = lax.dot_general(
            token_ref[...],
            hidden_ref[...],
            (((0,), (0,)), ((), ())),
            preferred_element_type=jnp.float32,
        )
        total = one if total is None else total + one
    out_ref[...] = total.astype(jnp.bfloat16)


def term_of(part, parts, tokens, hidden):
    group_tok, width = tokens[0].shape
    cols = hidden[0].shape[1] // parts
    tall = width // 8
    count = len(tokens)
    return pl.pallas_call(
        functools.partial(term_kernel, count),
        grid=(width // tall,),
        in_specs=[pl.BlockSpec((group_tok, tall), lambda i: (0, i))] * count
        + [pl.BlockSpec((group_tok, cols), lambda i: (0, part))] * count,
        out_specs=pl.BlockSpec((tall, cols), lambda i: (i, 0)),
        out_shape=jax.ShapeDtypeStruct((width, cols), jnp.bfloat16),
        compiler_params=pltpu.CompilerParams(vmem_limit_bytes=40 * 1024 * 1024),
        cost_estimate=pl.CostEstimate(
            flops=2 * count * group_tok * width * cols,
            bytes_accessed=2 * (count * group_tok * (width + cols) + width * cols),
            transcendentals=0,
        ),
        name="group_terms",
    )(*tokens, *hidden)


def deriv_kernel(tokens_ref, weight_ref, out_ref):
    out_ref[...] = jnp.dot(
        tokens_ref[...], weight_ref[...], preferred_element_type=jnp.float32
    )


def deriv_of(tokens, weight):
    group_tok, width = tokens.shape
    cols = weight.shape[1]
    wide = 256 if cols % 256 == 0 else cols
    return pl.pallas_call(
        deriv_kernel,
        grid=(cols // wide,),
        in_specs=[
            pl.BlockSpec((group_tok, width), lambda i: (0, 0)),
            pl.BlockSpec((width, wide), lambda i: (0, i)),
        ],
        out_specs=pl.BlockSpec((group_tok, wide), lambda i: (0, i)),
        out_shape=jax.ShapeDtypeStruct((group_tok, cols), jnp.float32),
        compiler_params=pltpu.CompilerParams(vmem_limit_bytes=32 * 1024 * 1024),
        cost_estimate=pl.CostEstimate(
            flops=2 * group_tok * width * cols,
            bytes_accessed=2 * (group_tok + cols) * width + 4 * group_tok * cols,
            transcendentals=0,
        ),
        name="hidden_deriv",
    )(tokens, weight)


def body(out_grad, gate_saved, up_saved, routing, down_weight, momentum):
    experts = lax.axis_size("expert")
    shards = lax.axis_size("dp")
    group_tok, topk, cols = gate_saved.shape
    width = out_grad.shape[1]
    rows = momentum.shape[1]
    mine = lax.axis_index("expert")

    weight_shards = lax.all_to_all(
        down_weight.reshape(shards, rows, cols), "dp", split_axis=0, concat_axis=0, tiled=True
    )

    tokens = {0: lax.all_gather(out_grad, "dp", axis=0, tiled=True)}
    for m in sorted(range(1, experts), key=lambda m: (bin(m).count("1"), -m)):
        low = m & -m
        tokens[m] = swapped(tokens[m ^ low], "expert", low)

    gate = gate_saved.astype(jnp.float32)
    up = up_saved.astype(jnp.float32)
    sigma = jax.nn.sigmoid(gate)
    hidden = (gate * sigma * up).astype(jnp.bfloat16)

    rows_of = {}
    for m in range(experts):
        chosen = (routing == (mine ^ m))[:, :, None]
        picked = jnp.sum(jnp.where(chosen, hidden, jnp.zeros_like(hidden)), axis=1)
        rows_of[m] = swapped(picked, "expert", m) if m else picked

    weight_shards, rows_of = lax.optimization_barrier((weight_shards, rows_of))
    each = range(experts)
    parts = 2 if cols % 256 == 0 else 1
    terms = [
        term_of(part, parts, [tokens[m] for m in each], [rows_of[m] for m in each])
        for part in range(parts)
    ]

    weight, gate_saved, up_saved, first = lax.optimization_barrier(
        (down_weight[0], gate_saved, up_saved, terms[0])
    )
    gate = gate_saved.astype(jnp.float32)
    up = up_saved.astype(jnp.float32)
    sigma = jax.nn.sigmoid(gate)
    deriv = jnp.zeros(gate.shape, jnp.float32)
    for m in each:
        part = deriv_of(tokens[m], weight)
        back = swapped(part, "expert", m) if m else part
        chosen = (routing == (mine ^ m))[:, :, None]
        deriv = jnp.where(chosen, back[:, None, :], deriv)
    d_up = (deriv * gate * sigma).astype(jnp.bfloat16)
    d_gate = (deriv * up * sigma * (1.0 + gate * (1.0 - sigma))).astype(jnp.bfloat16)

    done = ()
    for part, term in enumerate([first] + terms[1:]):
        grad_shards = lax.all_to_all(
            term.reshape(shards, rows, cols // parts), "dp", split_axis=0, concat_axis=0, tiled=True
        )
        done = update(part, parts, grad_shards, weight_shards, momentum, done)
    new_weight, new_momentum = done
    return (d_gate, d_up, new_weight, new_momentum)


def solution(mesh):
    placed = (
        P(("expert", "dp"), None),
        P("expert", None, "dp"),
        P("expert", None, "dp"),
        P("expert", None),
        P("expert", None, "dp"),
        P("expert", "dp", None),
    )
    return jax.shard_map(
        body,
        mesh=mesh,
        in_specs=placed,
        out_specs=(
            P("expert", None, "dp"),
            P("expert", None, "dp"),
            P("expert", "dp", None),
            P("expert", "dp", None),
        ),
        check_vma=False,
    )
```

```python
import functools

import jax
import jax.numpy as jnp
from jax import lax
from jax.experimental import pallas as pl
from jax.experimental.pallas import tpu as pltpu
from jax.sharding import PartitionSpec as P

beta_first = 0.9
beta_second = 0.99
step_rate = 0.01
decay_rate = 1.0
sign_width = 10.0
MIB = 1024 * 1024


def swapped(array, axis, mask):
    if mask == 0:
        return array
    size = lax.axis_size(axis)
    return lax.ppermute(array, axis, [(i, i ^ mask) for i in range(size)])


def after(value, *others):
    return lax.optimization_barrier((value, *others))[0]


def order_kernel(place_ref, mine_ref, theirs_ref, out_ref):
    out_ref[0, place_ref[0]] = mine_ref[0]
    out_ref[0, 1 - place_ref[0]] = theirs_ref[0]


def in_order(mine, theirs, bit):
    count, some, width = mine.shape
    one = pl.BlockSpec((1, some, width), lambda i, place: (i, 0, 0))
    both = pl.pallas_call(
        order_kernel,
        grid_spec=pltpu.PrefetchScalarGridSpec(
            num_scalar_prefetch=1,
            grid=(count,),
            in_specs=[one, one],
            out_specs=pl.BlockSpec((1, 2, some, width), lambda i, place: (i, 0, 0, 0)),
        ),
        out_shape=jax.ShapeDtypeStruct((count, 2, some, width), mine.dtype),
        cost_estimate=pl.CostEstimate(flops=0, bytes_accessed=8 * mine.size, transcendentals=0),
        name="side_by_side",
    )(bit.astype(jnp.int32).reshape(1), mine, theirs)
    return both.reshape(2 * count, some, width)


def pick(hidden, named_ref, out_refs):
    count_rows = hidden.shape[0]
    tokens = out_refs[0].shape[0]
    topk = count_rows // tokens
    token = lax.broadcasted_iota(jnp.int32, (tokens, count_rows), 0)
    row = lax.broadcasted_iota(jnp.int32, (tokens, count_rows), 1)
    here = (row >= token * topk) & (row < token * topk + topk)
    for m, out_ref in enumerate(out_refs):
        chosen = jnp.where(here & (named_ref[...] == m), 1.0, 0.0).astype(jnp.bfloat16)
        out_ref[...] = jnp.dot(chosen, hidden, preferred_element_type=jnp.float32).astype(
            jnp.bfloat16
        )


def hidden_kernel(gate_ref, up_ref, named_ref, hidden_ref, *out_refs):
    gate = gate_ref[...].astype(jnp.float32)
    up = up_ref[...].astype(jnp.float32)
    hidden = (gate * jax.nn.sigmoid(gate) * up).astype(jnp.bfloat16)
    hidden_ref[...] = hidden
    pick(hidden, named_ref, out_refs)


def pick_kernel(hidden_ref, named_ref, *out_refs):
    pick(hidden_ref[...], named_ref, out_refs)


def picked_rows(kernel, arrays, named, experts, topk, with_hidden):
    count_rows, cols = arrays[0].shape
    group_tok = count_rows // topk
    some = 128 if group_tok % 128 == 0 else group_tok
    row_block = pl.BlockSpec((some * topk, cols), lambda i: (i, 0))
    out_shape = [jax.ShapeDtypeStruct((group_tok, cols), jnp.bfloat16)] * experts
    out_specs = [pl.BlockSpec((some, cols), lambda i: (i, 0))] * experts
    if with_hidden:
        out_shape = [jax.ShapeDtypeStruct((count_rows, cols), jnp.bfloat16)] + out_shape
        out_specs = [row_block] + out_specs
    return pl.pallas_call(
        kernel,
        grid=(group_tok // some,),
        in_specs=[row_block] * len(arrays) + [pl.BlockSpec((1, some * topk), lambda i: (0, i))],
        out_specs=out_specs,
        out_shape=out_shape,
        compiler_params=pltpu.CompilerParams(vmem_limit_bytes=32 * MIB),
        cost_estimate=pl.CostEstimate(
            flops=2 * experts * count_rows * some * cols,
            bytes_accessed=2 * cols * (count_rows * (len(arrays) + 1) + experts * group_tok),
            transcendentals=count_rows * cols,
        ),
        name="hidden_rows",
    )(*arrays, named)


def term_kernel(count, place_ref, *refs):
    tokens, hidden, out_ref = refs[:count], refs[count : 2 * count], refs[-1]
    total = None
    for token_ref, hidden_ref in zip(tokens, hidden):
        one = lax.dot_general(
            token_ref[...],
            hidden_ref[...],
            (((0,), (0,)), ((), ())),
            preferred_element_type=jnp.float32,
        )
        total = one if total is None else total + one
    out_ref[...] = total.astype(jnp.bfloat16)


def terms(tokens, hidden, tall, first, steps):
    group_tok, width = tokens[0].shape
    cols = hidden[0].shape[1]
    count = len(tokens)
    return pl.pallas_call(
        functools.partial(term_kernel, count),
        grid_spec=pltpu.PrefetchScalarGridSpec(
            num_scalar_prefetch=1,
            grid=(steps,),
            in_specs=[pl.BlockSpec((group_tok, tall), lambda i, place: (0, place[0] + i))] * count
            + [pl.BlockSpec((group_tok, cols), lambda i, place: (0, 0))] * count,
            out_specs=pl.BlockSpec((tall, cols), lambda i, place: (i, 0)),
        ),
        out_shape=jax.ShapeDtypeStruct((steps * tall, cols), jnp.bfloat16),
        compiler_params=pltpu.CompilerParams(vmem_limit_bytes=40 * MIB),
        cost_estimate=pl.CostEstimate(
            flops=2 * count * group_tok * steps * tall * cols,
            bytes_accessed=2 * (count * group_tok * (steps * tall + cols) + steps * tall * cols),
            transcendentals=0,
        ),
        name="group_terms",
    )(first.reshape(1), *tokens, *hidden)


def deriv_kernel(place_ref, near_ref, far_ref, near_weight_ref, far_weight_ref, out_ref):
    out_ref[...] = jnp.dot(
        near_ref[...], near_weight_ref[...], preferred_element_type=jnp.float32
    ) + jnp.dot(far_ref[...], far_weight_ref[...], preferred_element_type=jnp.float32)


def deriv_of(near, far, weight, half):
    group_tok, width = near.shape
    cols = weight.shape[1]
    wide = 256 if cols % 256 == 0 else cols
    whole = pl.BlockSpec((group_tok, width), lambda i, place: (0, 0))
    return pl.pallas_call(
        deriv_kernel,
        grid_spec=pltpu.PrefetchScalarGridSpec(
            num_scalar_prefetch=1,
            grid=(cols // wide,),
            in_specs=[
                whole,
                whole,
                pl.BlockSpec((width, wide), lambda i, place: (place[0], i)),
                pl.BlockSpec((width, wide), lambda i, place: (1 - place[0], i)),
            ],
            out_specs=pl.BlockSpec((group_tok, wide), lambda i, place: (0, i)),
        ),
        out_shape=jax.ShapeDtypeStruct((group_tok, cols), jnp.float32),
        compiler_params=pltpu.CompilerParams(vmem_limit_bytes=32 * MIB),
        cost_estimate=pl.CostEstimate(
            flops=4 * group_tok * width * cols,
            bytes_accessed=4 * (group_tok + cols) * width + 4 * group_tok * cols,
            transcendentals=0,
        ),
        name="hidden_deriv",
    )(half.reshape(1), near, far, weight, weight)


def update_kernel(place_ref, grad_ref, weight_ref, momentum_ref, *refs):
    new_weight_ref, new_momentum_ref = refs[-2:]
    grad = grad_ref[...].astype(jnp.float32)
    moment = momentum_ref[0].astype(jnp.float32)
    weight = weight_ref[...].astype(jnp.float32)
    mix = beta_first * moment + (1.0 - beta_first) * grad
    new_weight_ref[0] = weight * (1.0 - step_rate * decay_rate) - step_rate * jnp.tanh(
        mix / sign_width
    )
    new_momentum_ref[0] = (beta_second * moment + (1.0 - beta_second) * grad).astype(
        jnp.bfloat16
    )


def update(source, grad, weight, momentum, done):
    rows, cols = grad.shape
    steps = 3 if rows % 48 == 0 else 1
    some = rows // steps
    own = pl.BlockSpec((some, cols), lambda i, place: (i, 0))
    wide = pl.BlockSpec((1, some, cols), lambda i, place: (0, i, place[0]))
    size = grad.size
    return pl.pallas_call(
        update_kernel,
        grid_spec=pltpu.PrefetchScalarGridSpec(
            num_scalar_prefetch=1,
            grid=(steps,),
            in_specs=[own, own, wide] + [pl.BlockSpec(memory_space=pl.ANY)] * len(done),
            out_specs=[wide, wide],
        ),
        out_shape=[
            jax.ShapeDtypeStruct(momentum.shape, jnp.float32),
            jax.ShapeDtypeStruct(momentum.shape, jnp.bfloat16),
        ],
        input_output_aliases={4 + i: i for i in range(len(done))},
        compiler_params=pltpu.CompilerParams(vmem_limit_bytes=32 * MIB),
        cost_estimate=pl.CostEstimate(flops=10 * size, bytes_accessed=12 * size, transcendentals=size),
        name="lion_step",
    )(source.reshape(1), grad, weight, momentum, *done)


def gathered(keep, give, experts, shards, place, mine):
    bit = shards // 2
    held = in_order(keep[None], swapped(give, "dp", bit)[None], (place & bit) != 0)
    while bit > 2:
        bit //= 2
        held = in_order(held, swapped(held, "dp", bit), (place & bit) != 0)
    groups = {0: held}
    for m in sorted(range(2, experts, 2), key=lambda m: (bin(m).count("1"), -m)):
        groups[m] = swapped(groups[m & (m - 1)], "expert", m & -m)
    if bit > 1:
        for m in groups:
            groups[m] = in_order(groups[m], swapped(groups[m], "dp", 1), (place & 1) != 0)
    for m in list(groups):
        groups[m] = groups[m].reshape(-1, keep.shape[1])
        if experts > 1:
            groups[m + 1] = swapped(groups[m], "expert", 1)
    return groups


def body(out_grad, gate_saved, up_saved, routing, down_weight, momentum):
    experts = lax.axis_size("expert")
    shards = lax.axis_size("dp")
    group_tok, topk, cols = gate_saved.shape
    width = out_grad.shape[1]
    rows = momentum.shape[1]
    mine = lax.axis_index("expert")
    place = lax.axis_index("dp")
    span = shards // 2
    half = place // span
    within = place % span
    each = range(experts)

    low, high = out_grad[:, : width // 2], out_grad[:, width // 2 :]
    near = jnp.where(half == 0, low, high)
    far = jnp.where(half == 0, high, low)
    near_tokens = gathered(near, far, experts, shards, place, mine)
    far_tokens = gathered(far, near, experts, shards, place, mine)

    named = (routing ^ mine).reshape(1, group_tok * topk)
    hidden, *own_rows = picked_rows(
        hidden_kernel,
        [gate_saved.reshape(-1, cols), up_saved.reshape(-1, cols)],
        named,
        experts,
        topk,
        True,
    )
    other_hidden = swapped(hidden, "dp", span)
    own_rows = [swapped(own_rows[m], "expert", m) for m in each]
    other_rows = picked_rows(pick_kernel, [other_hidden], named, experts, topk, False)
    other_rows = [swapped(other_rows[m], "expert", m) for m in each]

    near_list = [near_tokens[m] for m in each]

    def shard_terms(hidden_rows):
        if rows % 128 == 0:
            return [terms(near_list, hidden_rows, rows, within ^ m, 1) for m in range(span)]
        tall = width // 8
        total = terms(near_list, hidden_rows, tall, 0 * within, width // 2 // tall)
        return [
            lax.dynamic_slice_in_dim(total, (within ^ m) * rows, rows, axis=0) for m in range(span)
        ]

    own_terms = shard_terms(own_rows)
    other_terms = shard_terms(other_rows)
    grads = {}
    for m in range(span):
        grads[m] = swapped(own_terms[m], "dp", m)
        grads[m ^ span] = swapped(other_terms[m], "dp", m)

    weight = down_weight[0]
    late_weight = after(weight, other_hidden)
    weights = {}
    for m in range(shards):
        block = lax.dynamic_slice_in_dim(
            weight if m < span else late_weight, (place ^ m) * rows, rows, axis=0
        )
        weights[m] = swapped(block, "dp", m)

    back_weight, gate_saved, up_saved, _ = lax.optimization_barrier(
        (weight, gate_saved, up_saved, own_terms[0])
    )
    gate = gate_saved.astype(jnp.float32)
    up = up_saved.astype(jnp.float32)
    sigma = jax.nn.sigmoid(gate)
    deriv = jnp.zeros(gate.shape, jnp.float32)
    for m in [2 * i + j for j in range(2) for i in range(experts // 2)][::-1]:
        part = deriv_of(near_tokens[m], far_tokens[m], back_weight, half)
        chosen = (routing == (mine ^ m))[:, :, None]
        deriv = jnp.where(chosen, swapped(part, "expert", m)[:, None, :], deriv)
    d_up = (deriv * gate * sigma).astype(jnp.bfloat16)
    d_gate = (deriv * up * sigma * (1.0 + gate * (1.0 - sigma))).astype(jnp.bfloat16)

    done = ()
    for m in range(shards):
        done = update(place ^ m, grads[m], weights[m], momentum, done)
    new_weight, new_momentum = done
    return (d_gate, d_up, new_weight, new_momentum)


def solution(mesh):
    placed = (
        P(("expert", "dp"), None),
        P("expert", None, "dp"),
        P("expert", None, "dp"),
        P("expert", None),
        P("expert", None, "dp"),
        P("expert", "dp", None),
    )
    return jax.shard_map(
        body,
        mesh=mesh,
        in_specs=placed,
        out_specs=(
            P("expert", None, "dp"),
            P("expert", None, "dp"),
            P("expert", "dp", None),
            P("expert", "dp", None),
        ),
        check_vma=False,
    )
```

```python
import functools

import jax
import jax.numpy as jnp
from jax import lax
from jax.experimental import pallas as pl
from jax.experimental.pallas import tpu as pltpu
from jax.sharding import PartitionSpec as P

beta_first = 0.9
beta_second = 0.99
step_rate = 0.01
decay_rate = 1.0
sign_width = 10.0
MIB = 1024 * 1024


def swapped(array, axis, mask):
    if mask == 0:
        return array
    size = lax.axis_size(axis)
    return lax.ppermute(array, axis, [(i, i ^ mask) for i in range(size)])


def after(value, *others):
    return lax.optimization_barrier((value, *others))[0]


def order_kernel(place_ref, mine_ref, theirs_ref, out_ref):
    out_ref[0, place_ref[0]] = mine_ref[0]
    out_ref[0, 1 - place_ref[0]] = theirs_ref[0]


def in_order(mine, theirs, bit):
    count, some, width = mine.shape
    one = pl.BlockSpec((1, some, width), lambda i, place: (i, 0, 0))
    both = pl.pallas_call(
        order_kernel,
        grid_spec=pltpu.PrefetchScalarGridSpec(
            num_scalar_prefetch=1,
            grid=(count,),
            in_specs=[one, one],
            out_specs=pl.BlockSpec((1, 2, some, width), lambda i, place: (i, 0, 0, 0)),
        ),
        out_shape=jax.ShapeDtypeStruct((count, 2, some, width), mine.dtype),
        cost_estimate=pl.CostEstimate(flops=0, bytes_accessed=8 * mine.size, transcendentals=0),
        name="side_by_side",
    )(bit.astype(jnp.int32).reshape(1), mine, theirs)
    return both.reshape(2 * count, some, width)


def pick(hidden, named_ref, out_refs):
    count_rows = hidden.shape[0]
    tokens = out_refs[0].shape[0]
    topk = count_rows // tokens
    token = lax.broadcasted_iota(jnp.int32, (tokens, count_rows), 0)
    row = lax.broadcasted_iota(jnp.int32, (tokens, count_rows), 1)
    here = (row >= token * topk) & (row < token * topk + topk)
    for m, out_ref in enumerate(out_refs):
        chosen = jnp.where(here & (named_ref[...] == m), 1.0, 0.0).astype(jnp.bfloat16)
        out_ref[...] = jnp.dot(chosen, hidden, preferred_element_type=jnp.float32).astype(
            jnp.bfloat16
        )


def hidden_kernel(gate_ref, up_ref, named_ref, hidden_ref, *out_refs):
    gate = gate_ref[...].astype(jnp.float32)
    up = up_ref[...].astype(jnp.float32)
    hidden = (gate * jax.nn.sigmoid(gate) * up).astype(jnp.bfloat16)
    hidden_ref[...] = hidden
    pick(hidden, named_ref, out_refs)


def pick_kernel(hidden_ref, named_ref, *out_refs):
    pick(hidden_ref[...], named_ref, out_refs)


def picked_rows(kernel, arrays, named, experts, topk, with_hidden):
    count_rows, cols = arrays[0].shape
    group_tok = count_rows // topk
    some = 128 if group_tok % 128 == 0 else group_tok
    row_block = pl.BlockSpec((some * topk, cols), lambda i: (i, 0))
    out_shape = [jax.ShapeDtypeStruct((group_tok, cols), jnp.bfloat16)] * experts
    out_specs = [pl.BlockSpec((some, cols), lambda i: (i, 0))] * experts
    if with_hidden:
        out_shape = [jax.ShapeDtypeStruct((count_rows, cols), jnp.bfloat16)] + out_shape
        out_specs = [row_block] + out_specs
    return pl.pallas_call(
        kernel,
        grid=(group_tok // some,),
        in_specs=[row_block] * len(arrays) + [pl.BlockSpec((1, some * topk), lambda i: (0, i))],
        out_specs=out_specs,
        out_shape=out_shape,
        compiler_params=pltpu.CompilerParams(vmem_limit_bytes=32 * MIB),
        cost_estimate=pl.CostEstimate(
            flops=2 * experts * count_rows * some * cols,
            bytes_accessed=2 * cols * (count_rows * (len(arrays) + 1) + experts * group_tok),
            transcendentals=count_rows * cols,
        ),
        name="hidden_rows",
    )(*arrays, named)


def term_kernel(count, place_ref, *refs):
    tokens, hidden, out_ref = refs[:count], refs[count : 2 * count], refs[-1]
    total = None
    for token_ref, hidden_ref in zip(tokens, hidden):
        one = lax.dot_general(
            token_ref[...],
            hidden_ref[...],
            (((0,), (0,)), ((), ())),
            preferred_element_type=jnp.float32,
        )
        total = one if total is None else total + one
    out_ref[...] = total.astype(jnp.bfloat16)


def terms(tokens, hidden, tall, first, steps):
    group_tok, width = tokens[0].shape
    cols = hidden[0].shape[1]
    count = len(tokens)
    return pl.pallas_call(
        functools.partial(term_kernel, count),
        grid_spec=pltpu.PrefetchScalarGridSpec(
            num_scalar_prefetch=1,
            grid=(steps,),
            in_specs=[pl.BlockSpec((group_tok, tall), lambda i, place: (0, place[0] + i))] * count
            + [pl.BlockSpec((group_tok, cols), lambda i, place: (0, 0))] * count,
            out_specs=pl.BlockSpec((tall, cols), lambda i, place: (i, 0)),
        ),
        out_shape=jax.ShapeDtypeStruct((steps * tall, cols), jnp.bfloat16),
        compiler_params=pltpu.CompilerParams(vmem_limit_bytes=40 * MIB),
        cost_estimate=pl.CostEstimate(
            flops=2 * count * group_tok * steps * tall * cols,
            bytes_accessed=2 * (count * group_tok * (steps * tall + cols) + steps * tall * cols),
            transcendentals=0,
        ),
        name="group_terms",
    )(first.reshape(1), *tokens, *hidden)


def deriv_kernel(place_ref, near_ref, far_ref, near_weight_ref, far_weight_ref, out_ref):
    out_ref[...] = jnp.dot(
        near_ref[...], near_weight_ref[...], preferred_element_type=jnp.float32
    ) + jnp.dot(far_ref[...], far_weight_ref[...], preferred_element_type=jnp.float32)


def deriv_of(near, far, weight, half):
    group_tok, width = near.shape
    cols = weight.shape[1]
    wide = 256 if cols % 256 == 0 else cols
    whole = pl.BlockSpec((group_tok, width), lambda i, place: (0, 0))
    return pl.pallas_call(
        deriv_kernel,
        grid_spec=pltpu.PrefetchScalarGridSpec(
            num_scalar_prefetch=1,
            grid=(cols // wide,),
            in_specs=[
                whole,
                whole,
                pl.BlockSpec((width, wide), lambda i, place: (place[0], i)),
                pl.BlockSpec((width, wide), lambda i, place: (1 - place[0], i)),
            ],
            out_specs=pl.BlockSpec((group_tok, wide), lambda i, place: (0, i)),
        ),
        out_shape=jax.ShapeDtypeStruct((group_tok, cols), jnp.float32),
        compiler_params=pltpu.CompilerParams(vmem_limit_bytes=32 * MIB),
        cost_estimate=pl.CostEstimate(
            flops=4 * group_tok * width * cols,
            bytes_accessed=4 * (group_tok + cols) * width + 4 * group_tok * cols,
            transcendentals=0,
        ),
        name="hidden_deriv",
    )(half.reshape(1), near, far, weight, weight)


def update_kernel(count, place_ref, weight_ref, momentum_ref, *refs):
    grad_refs = refs[:count]
    new_weight_ref, new_momentum_ref = refs[-2:]
    for m, grad_ref in enumerate(grad_refs):

        @pl.when(pl.program_id(0) == m)
        def _():
            grad = grad_ref[...].astype(jnp.float32)
            moment = momentum_ref[0].astype(jnp.float32)
            weight = weight_ref[0].astype(jnp.float32)
            mix = beta_first * moment + (1.0 - beta_first) * grad
            new_weight_ref[0] = weight * (1.0 - step_rate * decay_rate) - step_rate * jnp.tanh(
                mix / sign_width
            )
            new_momentum_ref[0] = (beta_second * moment + (1.0 - beta_second) * grad).astype(
                jnp.bfloat16
            )


def update(part, place, grads, weight, momentum, done):
    count, rows, some = weight.shape
    parts = grads[0].shape[1] // some
    wide = pl.BlockSpec((1, rows, some), lambda m, place: (0, 0, (place[0] ^ m) * parts + part))
    size = weight.size
    return pl.pallas_call(
        functools.partial(update_kernel, count),
        grid_spec=pltpu.PrefetchScalarGridSpec(
            num_scalar_prefetch=1,
            grid=(count,),
            in_specs=[pl.BlockSpec((1, rows, some), lambda m, place: (place[0] ^ m, 0, 0)), wide]
            + [pl.BlockSpec((rows, some), lambda m, place: (0, part))] * count
            + [pl.BlockSpec(memory_space=pl.ANY)] * len(done),
            out_specs=[wide, wide],
        ),
        out_shape=[
            jax.ShapeDtypeStruct(momentum.shape, jnp.float32),
            jax.ShapeDtypeStruct(momentum.shape, jnp.bfloat16),
        ],
        input_output_aliases={3 + count + i: i for i in range(len(done))},
        compiler_params=pltpu.CompilerParams(vmem_limit_bytes=40 * MIB),
        cost_estimate=pl.CostEstimate(flops=10 * size, bytes_accessed=12 * size, transcendentals=size),
        name="lion_step",
    )(place.reshape(1), weight, momentum, *grads, *done)


def gathered(keep, give, experts, shards, place, first):
    bit = shards // 2
    theirs = after(swapped(give, "dp", bit), first)
    held = in_order(keep[None], theirs[None], (place & bit) != 0)
    while bit > 2:
        bit //= 2
        held = in_order(held, swapped(held, "dp", bit), (place & bit) != 0)
    groups = {0: held}
    for m in sorted(range(2, experts, 2), key=lambda m: (bin(m).count("1"), -m)):
        groups[m] = swapped(groups[m & (m - 1)], "expert", m & -m)
    if bit > 1:
        for m in groups:
            groups[m] = in_order(groups[m], swapped(groups[m], "dp", 1), (place & 1) != 0)
    for m in list(groups):
        groups[m] = groups[m].reshape(-1, keep.shape[1])
        if experts > 1:
            groups[m + 1] = swapped(groups[m], "expert", 1)
    return groups


def body(out_grad, gate_saved, up_saved, routing, down_weight, momentum):
    experts = lax.axis_size("expert")
    shards = lax.axis_size("dp")
    group_tok, topk, cols = gate_saved.shape
    width = out_grad.shape[1]
    rows = momentum.shape[1]
    mine = lax.axis_index("expert")
    place = lax.axis_index("dp")
    span = shards // 2
    half = place // span
    within = place % span
    each = range(experts)

    low, high = out_grad[:, : width // 2], out_grad[:, width // 2 :]
    near = jnp.where(half == 0, low, high)
    far = jnp.where(half == 0, high, low)
    named = (routing ^ mine).reshape(1, group_tok * topk)
    hidden, *own_rows = picked_rows(
        hidden_kernel,
        [gate_saved.reshape(-1, cols), up_saved.reshape(-1, cols)],
        named,
        experts,
        topk,
        True,
    )
    near_tokens = gathered(near, far, experts, shards, place, hidden)
    far_tokens = gathered(far, near, experts, shards, place, hidden)
    other_hidden = swapped(hidden, "dp", span)
    own_rows = [swapped(own_rows[m], "expert", m) for m in each]
    other_rows = picked_rows(pick_kernel, [other_hidden], named, experts, topk, False)
    other_picked = other_rows[0]
    other_rows = [swapped(other_rows[m], "expert", m) for m in each]

    near_list = [near_tokens[m] for m in each]

    def shard_terms(hidden_rows):
        if rows % 128 == 0:
            return [terms(near_list, hidden_rows, rows, within ^ m, 1) for m in range(span)]
        tall = width // 8
        total = terms(near_list, hidden_rows, tall, 0 * within, width // 2 // tall)
        return [
            lax.dynamic_slice_in_dim(total, (within ^ m) * rows, rows, axis=0) for m in range(span)
        ]

    own_terms = shard_terms(own_rows)
    other_terms = shard_terms(other_rows)
    grads = {}
    for m in range(span):
        grads[m] = swapped(own_terms[m], "dp", m)
        grads[m ^ span] = swapped(other_terms[m], "dp", m)

    weight = down_weight[0]
    parts = 2 if cols % 256 == 0 else 1
    late_weight = after(down_weight, other_hidden).reshape(shards, rows, cols)
    weights = [
        lax.all_to_all(piece, "dp", split_axis=0, concat_axis=0, tiled=True)
        for piece in jnp.split(late_weight, parts, axis=2)
    ]

    back_weight, gate_saved, up_saved, *_ = lax.optimization_barrier(
        (weight, gate_saved, up_saved, own_terms, other_picked)
    )
    gate = gate_saved.astype(jnp.float32)
    up = up_saved.astype(jnp.float32)
    sigma = jax.nn.sigmoid(gate)
    deriv = jnp.zeros(gate.shape, jnp.float32)
    for m in [2 * i + j for j in range(2) for i in range(experts // 2)][::-1]:
        part = deriv_of(near_tokens[m], far_tokens[m], back_weight, half)
        chosen = (routing == (mine ^ m))[:, :, None]
        deriv = jnp.where(chosen, swapped(part, "expert", m)[:, None, :], deriv)
    d_up = (deriv * gate * sigma).astype(jnp.bfloat16)
    d_gate = (deriv * up * sigma * (1.0 + gate * (1.0 - sigma))).astype(jnp.bfloat16)

    done = ()
    for part in range(parts):
        done = update(part, place, [grads[m] for m in range(shards)], weights[part], momentum, done)
    new_weight, new_momentum = done
    return (d_gate, d_up, new_weight, new_momentum)


def solution(mesh):
    placed = (
        P(("expert", "dp"), None),
        P("expert", None, "dp"),
        P("expert", None, "dp"),
        P("expert", None),
        P("expert", None, "dp"),
        P("expert", "dp", None),
    )
    return jax.shard_map(
        body,
        mesh=mesh,
        in_specs=placed,
        out_specs=(
            P("expert", None, "dp"),
            P("expert", None, "dp"),
            P("expert", "dp", None),
            P("expert", "dp", None),
        ),
        check_vma=False,
    )
```

```python
import functools

import jax
import jax.numpy as jnp
from jax import lax
from jax.experimental import pallas as pl
from jax.experimental.pallas import tpu as pltpu
from jax.sharding import PartitionSpec as P

beta_first = 0.9
beta_second = 0.99
step_rate = 0.01
decay_rate = 1.0
sign_width = 10.0
MIB = 1024 * 1024


def swapped(array, axis, mask):
    if mask == 0:
        return array
    size = lax.axis_size(axis)
    return lax.ppermute(array, axis, [(i, i ^ mask) for i in range(size)])


def after(value, *others):
    return lax.optimization_barrier((value, *others))[0]


def order_kernel(place_ref, mine_ref, theirs_ref, out_ref):
    out_ref[0, place_ref[0]] = mine_ref[0]
    out_ref[0, 1 - place_ref[0]] = theirs_ref[0]


def in_order(mine, theirs, bit):
    count, some, width = mine.shape
    one = pl.BlockSpec((1, some, width), lambda i, place: (i, 0, 0))
    both = pl.pallas_call(
        order_kernel,
        grid_spec=pltpu.PrefetchScalarGridSpec(
            num_scalar_prefetch=1,
            grid=(count,),
            in_specs=[one, one],
            out_specs=pl.BlockSpec((1, 2, some, width), lambda i, place: (i, 0, 0, 0)),
        ),
        out_shape=jax.ShapeDtypeStruct((count, 2, some, width), mine.dtype),
        cost_estimate=pl.CostEstimate(flops=0, bytes_accessed=8 * mine.size, transcendentals=0),
        name="side_by_side",
    )(bit.astype(jnp.int32).reshape(1), mine, theirs)
    return both.reshape(2 * count, some, width)


def pick(hidden, named_ref, out_refs):
    count_rows = hidden.shape[0]
    tokens = out_refs[0].shape[0]
    topk = count_rows // tokens
    token = lax.broadcasted_iota(jnp.int32, (tokens, count_rows), 0)
    row = lax.broadcasted_iota(jnp.int32, (tokens, count_rows), 1)
    here = (row >= token * topk) & (row < token * topk + topk)
    for m, out_ref in enumerate(out_refs):
        chosen = jnp.where(here & (named_ref[...] == m), 1.0, 0.0).astype(jnp.bfloat16)
        out_ref[...] = jnp.dot(chosen, hidden, preferred_element_type=jnp.float32).astype(
            jnp.bfloat16
        )


def hidden_kernel(gate_ref, up_ref, named_ref, hidden_ref, *out_refs):
    gate = gate_ref[...].astype(jnp.float32)
    up = up_ref[...].astype(jnp.float32)
    hidden = (gate * jax.nn.sigmoid(gate) * up).astype(jnp.bfloat16)
    hidden_ref[...] = hidden
    pick(hidden, named_ref, out_refs)


def pick_kernel(hidden_ref, named_ref, *out_refs):
    pick(hidden_ref[...], named_ref, out_refs)


def picked_rows(kernel, arrays, named, experts, topk, with_hidden):
    count_rows, cols = arrays[0].shape
    group_tok = count_rows // topk
    some = 128 if group_tok % 128 == 0 else group_tok
    row_block = pl.BlockSpec((some * topk, cols), lambda i: (i, 0))
    out_shape = [jax.ShapeDtypeStruct((group_tok, cols), jnp.bfloat16)] * experts
    out_specs = [pl.BlockSpec((some, cols), lambda i: (i, 0))] * experts
    if with_hidden:
        out_shape = [jax.ShapeDtypeStruct((count_rows, cols), jnp.bfloat16)] + out_shape
        out_specs = [row_block] + out_specs
    return pl.pallas_call(
        kernel,
        grid=(group_tok // some,),
        in_specs=[row_block] * len(arrays) + [pl.BlockSpec((1, some * topk), lambda i: (0, i))],
        out_specs=out_specs,
        out_shape=out_shape,
        compiler_params=pltpu.CompilerParams(vmem_limit_bytes=56 * MIB),
        cost_estimate=pl.CostEstimate(
            flops=2 * experts * count_rows * some * cols,
            bytes_accessed=2 * cols * (count_rows * (len(arrays) + 1) + experts * group_tok),
            transcendentals=count_rows * cols,
        ),
        name="hidden_rows",
    )(*arrays, named)


def term_kernel(count, place_ref, *refs):
    tokens, hidden, out_ref = refs[:count], refs[count : 2 * count], refs[-1]
    total = None
    for token_ref, hidden_ref in zip(tokens, hidden):
        one = lax.dot_general(
            token_ref[...],
            hidden_ref[...],
            (((0,), (0,)), ((), ())),
            preferred_element_type=jnp.float32,
        )
        total = one if total is None else total + one
    out_ref[...] = total.astype(jnp.bfloat16)


def terms(tokens, hidden, tall, first, steps):
    group_tok, width = tokens[0].shape
    cols = hidden[0].shape[1]
    count = len(tokens)
    return pl.pallas_call(
        functools.partial(term_kernel, count),
        grid_spec=pltpu.PrefetchScalarGridSpec(
            num_scalar_prefetch=1,
            grid=(steps,),
            in_specs=[pl.BlockSpec((group_tok, tall), lambda i, place: (0, place[0] + i))] * count
            + [pl.BlockSpec((group_tok, cols), lambda i, place: (0, 0))] * count,
            out_specs=pl.BlockSpec((tall, cols), lambda i, place: (i, 0)),
        ),
        out_shape=jax.ShapeDtypeStruct((steps * tall, cols), jnp.bfloat16),
        compiler_params=pltpu.CompilerParams(vmem_limit_bytes=56 * MIB),
        cost_estimate=pl.CostEstimate(
            flops=2 * count * group_tok * steps * tall * cols,
            bytes_accessed=2 * (count * group_tok * (steps * tall + cols) + steps * tall * cols),
            transcendentals=0,
        ),
        name="group_terms",
    )(first.reshape(1), *tokens, *hidden)


def deriv_kernel(place_ref, near_ref, far_ref, near_weight_ref, far_weight_ref, out_ref):
    out_ref[...] = jnp.dot(
        near_ref[...], near_weight_ref[...], preferred_element_type=jnp.float32
    ) + jnp.dot(far_ref[...], far_weight_ref[...], preferred_element_type=jnp.float32)


def deriv_of(near, far, weight, half):
    group_tok, width = near.shape
    cols = weight.shape[1]
    wide = 256 if cols % 256 == 0 else cols
    whole = pl.BlockSpec((group_tok, width), lambda i, place: (0, 0))
    return pl.pallas_call(
        deriv_kernel,
        grid_spec=pltpu.PrefetchScalarGridSpec(
            num_scalar_prefetch=1,
            grid=(cols // wide,),
            in_specs=[
                whole,
                whole,
                pl.BlockSpec((width, wide), lambda i, place: (place[0], i)),
                pl.BlockSpec((width, wide), lambda i, place: (1 - place[0], i)),
            ],
            out_specs=pl.BlockSpec((group_tok, wide), lambda i, place: (0, i)),
        ),
        out_shape=jax.ShapeDtypeStruct((group_tok, cols), jnp.float32),
        compiler_params=pltpu.CompilerParams(vmem_limit_bytes=56 * MIB),
        cost_estimate=pl.CostEstimate(
            flops=4 * group_tok * width * cols,
            bytes_accessed=4 * (group_tok + cols) * width + 4 * group_tok * cols,
            transcendentals=0,
        ),
        name="hidden_deriv",
    )(half.reshape(1), near, far, weight, weight)


def update_kernel(count, place_ref, weight_ref, momentum_ref, *refs):
    grad_refs = refs[:count]
    new_weight_ref, new_momentum_ref = refs[-2:]
    for m, grad_ref in enumerate(grad_refs):

        @pl.when(pl.program_id(0) == m)
        def _():
            grad = grad_ref[...].astype(jnp.float32)
            moment = momentum_ref[0].astype(jnp.float32)
            weight = weight_ref[0].astype(jnp.float32)
            mix = beta_first * moment + (1.0 - beta_first) * grad
            new_weight_ref[0] = weight * (1.0 - step_rate * decay_rate) - step_rate * jnp.tanh(
                mix / sign_width
            )
            new_momentum_ref[0] = (beta_second * moment + (1.0 - beta_second) * grad).astype(
                jnp.bfloat16
            )


def update(part, place, grads, weight, momentum, done):
    count, rows, some = weight.shape
    parts = grads[0].shape[1] // some
    wide = pl.BlockSpec((1, rows, some), lambda m, place: (0, 0, (place[0] ^ m) * parts + part))
    size = weight.size
    return pl.pallas_call(
        functools.partial(update_kernel, count),
        grid_spec=pltpu.PrefetchScalarGridSpec(
            num_scalar_prefetch=1,
            grid=(count,),
            in_specs=[pl.BlockSpec((1, rows, some), lambda m, place: (place[0] ^ m, 0, 0)), wide]
            + [pl.BlockSpec((rows, some), lambda m, place: (0, part))] * count
            + [pl.BlockSpec(memory_space=pl.ANY)] * len(done),
            out_specs=[wide, wide],
        ),
        out_shape=[
            jax.ShapeDtypeStruct(momentum.shape, jnp.float32),
            jax.ShapeDtypeStruct(momentum.shape, jnp.bfloat16),
        ],
        input_output_aliases={3 + count + i: i for i in range(len(done))},
        compiler_params=pltpu.CompilerParams(vmem_limit_bytes=56 * MIB),
        cost_estimate=pl.CostEstimate(flops=10 * size, bytes_accessed=12 * size, transcendentals=size),
        name="lion_step",
    )(place.reshape(1), weight, momentum, *grads, *done)


def first_step(keep, theirs, shards, place):
    return in_order(keep[None], theirs[None], (place & (shards // 2)) != 0)


def gathered(held, experts, shards, place):
    bit = shards // 2
    while bit > 2:
        bit //= 2
        held = in_order(held, swapped(held, "dp", bit), (place & bit) != 0)
    groups = {0: held}
    for m in sorted(range(2, experts, 2), key=lambda m: (bin(m).count("1"), -m)):
        groups[m] = swapped(groups[m & (m - 1)], "expert", m & -m)
    if bit > 1:
        for m in groups:
            groups[m] = in_order(groups[m], swapped(groups[m], "dp", 1), (place & 1) != 0)
    for m in list(groups):
        groups[m] = groups[m].reshape(-1, held.shape[2])
        if experts > 1:
            groups[m + 1] = swapped(groups[m], "expert", 1)
    return groups


def body(out_grad, gate_saved, up_saved, routing, down_weight, momentum):
    experts = lax.axis_size("expert")
    shards = lax.axis_size("dp")
    group_tok, topk, cols = gate_saved.shape
    width = out_grad.shape[1]
    rows = momentum.shape[1]
    mine = lax.axis_index("expert")
    place = lax.axis_index("dp")
    span = shards // 2
    half = place // span
    within = place % span
    each = range(experts)

    low, high = out_grad[:, : width // 2], out_grad[:, width // 2 :]
    near = jnp.where(half == 0, low, high)
    far = jnp.where(half == 0, high, low)
    near_theirs = swapped(far, "dp", span)
    far_theirs = swapped(near, "dp", span)

    named = (routing ^ mine).reshape(1, group_tok * topk)
    gate_rows, up_rows, *_ = lax.optimization_barrier(
        (gate_saved.reshape(-1, cols), up_saved.reshape(-1, cols), near, far)
    )
    hidden, *own_rows = picked_rows(
        hidden_kernel, [gate_rows, up_rows], named, experts, topk, True
    )
    near_held = first_step(near, after(near_theirs, hidden), shards, place)
    far_held = first_step(far, after(far_theirs, hidden), shards, place)
    near_tokens = gathered(near_held, experts, shards, place)
    far_tokens = gathered(far_held, experts, shards, place)
    other_hidden = swapped(after(hidden, near_held, far_held), "dp", span)
    own_rows = [swapped(own_rows[m], "expert", m) for m in each]
    other_rows = picked_rows(pick_kernel, [other_hidden], named, experts, topk, False)
    other_rows = [swapped(other_rows[m], "expert", m) for m in each]

    near_list = [near_tokens[m] for m in each]

    def shard_terms(hidden_rows):
        if rows % 128 == 0:
            return [terms(near_list, hidden_rows, rows, within ^ m, 1) for m in range(span)]
        tall = width // 8
        total = terms(near_list, hidden_rows, tall, 0 * within, width // 2 // tall)
        return [
            lax.dynamic_slice_in_dim(total, (within ^ m) * rows, rows, axis=0) for m in range(span)
        ]

    own_terms = shard_terms(own_rows)
    other_terms = shard_terms(other_rows)
    weight = down_weight[0]
    parts = 2 if cols % 256 == 0 else 1
    pieces = jnp.split(down_weight.reshape(shards, rows, cols), parts, axis=2)
    weights = []
    for part, piece in enumerate(pieces):
        begun = [other_hidden] if part == 0 else [weights[-1], other_terms]
        weights.append(
            lax.all_to_all(after(piece, *begun), "dp", split_axis=0, concat_axis=0, tiled=True)
        )

    other_terms = after(other_terms, weights[0])
    grads = {}
    for m in range(span):
        grads[m] = swapped(own_terms[m], "dp", m)
        grads[m ^ span] = swapped(other_terms[m], "dp", m)

    back_weight, gate_saved, up_saved, *_ = lax.optimization_barrier(
        (weight, gate_saved, up_saved, own_terms, other_rows[experts // 2])
    )
    gate = gate_saved.astype(jnp.float32)
    up = up_saved.astype(jnp.float32)
    sigma = jax.nn.sigmoid(gate)
    deriv = jnp.zeros(gate.shape, jnp.float32)
    for m in list(range(experts // 2, experts)) + list(range(experts // 2)):
        part = deriv_of(near_tokens[m], far_tokens[m], back_weight, half)
        chosen = (routing == (mine ^ m))[:, :, None]
        deriv = jnp.where(chosen, swapped(part, "expert", m)[:, None, :], deriv)
    d_up = (deriv * gate * sigma).astype(jnp.bfloat16)
    d_gate = (deriv * up * sigma * (1.0 + gate * (1.0 - sigma))).astype(jnp.bfloat16)

    done = ()
    for part in range(parts):
        done = update(part, place, [grads[m] for m in range(shards)], weights[part], momentum, done)
    new_weight, new_momentum = done
    return (d_gate, d_up, new_weight, new_momentum)


def solution(mesh):
    placed = (
        P(("expert", "dp"), None),
        P("expert", None, "dp"),
        P("expert", None, "dp"),
        P("expert", None),
        P("expert", None, "dp"),
        P("expert", "dp", None),
    )
    return jax.shard_map(
        body,
        mesh=mesh,
        in_specs=placed,
        out_specs=(
            P("expert", None, "dp"),
            P("expert", None, "dp"),
            P("expert", "dp", None),
            P("expert", "dp", None),
        ),
        check_vma=False,
    )
```

```python
import functools

import jax
import jax.numpy as jnp
from jax import lax
from jax.experimental import pallas as pl
from jax.experimental.pallas import tpu as pltpu
from jax.sharding import PartitionSpec as P

beta_first = 0.9
beta_second = 0.99
step_rate = 0.01
decay_rate = 1.0
sign_width = 10.0
MIB = 1024 * 1024


def swapped(array, axis, mask):
    if mask == 0:
        return array
    size = lax.axis_size(axis)
    return lax.ppermute(array, axis, [(i, i ^ mask) for i in range(size)])


def after(value, *others):
    return lax.optimization_barrier((value, *others))[0]


def order_kernel(place_ref, mine_ref, theirs_ref, out_ref):
    out_ref[0, place_ref[0]] = mine_ref[0]
    out_ref[0, 1 - place_ref[0]] = theirs_ref[0]


def in_order(mine, theirs, bit):
    count, some, width = mine.shape
    one = pl.BlockSpec((1, some, width), lambda i, place: (i, 0, 0))
    both = pl.pallas_call(
        order_kernel,
        grid_spec=pltpu.PrefetchScalarGridSpec(
            num_scalar_prefetch=1,
            grid=(count,),
            in_specs=[one, one],
            out_specs=pl.BlockSpec((1, 2, some, width), lambda i, place: (i, 0, 0, 0)),
        ),
        out_shape=jax.ShapeDtypeStruct((count, 2, some, width), mine.dtype),
        cost_estimate=pl.CostEstimate(flops=0, bytes_accessed=8 * mine.size, transcendentals=0),
        name="side_by_side",
    )(bit.astype(jnp.int32).reshape(1), mine, theirs)
    return both.reshape(2 * count, some, width)


def place_kernel(place_ref, *refs):
    for m, block_ref in enumerate(refs[:-1]):
        refs[-1][place_ref[0] ^ m] = block_ref[...]


def placed_blocks(blocks, place):
    count = len(blocks)
    return pl.pallas_call(
        place_kernel,
        grid_spec=pltpu.PrefetchScalarGridSpec(
            num_scalar_prefetch=1,
            grid=(1,),
            in_specs=[pl.BlockSpec(blocks[0].shape, lambda i, place: (0, 0))] * count,
            out_specs=pl.BlockSpec((count,) + blocks[0].shape, lambda i, place: (0, 0, 0)),
        ),
        out_shape=jax.ShapeDtypeStruct((count,) + blocks[0].shape, blocks[0].dtype),
        compiler_params=pltpu.CompilerParams(vmem_limit_bytes=56 * MIB),
        cost_estimate=pl.CostEstimate(
            flops=0, bytes_accessed=4 * count * blocks[0].size, transcendentals=0
        ),
        name="placed_blocks",
    )(place.reshape(1), *blocks)


def pick(hidden, named_ref, out_refs):
    count_rows = hidden.shape[0]
    tokens = out_refs[0].shape[1]
    topk = count_rows // tokens
    token = lax.broadcasted_iota(jnp.int32, (tokens, count_rows), 0)
    row = lax.broadcasted_iota(jnp.int32, (tokens, count_rows), 1)
    here = (row >= token * topk) & (row < token * topk + topk)
    m = 0
    for out_ref in out_refs:
        for i in range(out_ref.shape[0]):
            chosen = jnp.where(here & (named_ref[...] == m), 1.0, 0.0).astype(jnp.bfloat16)
            out_ref[i] = jnp.dot(chosen, hidden, preferred_element_type=jnp.float32).astype(
                jnp.bfloat16
            )
            m += 1


def hidden_kernel(gate_ref, up_ref, named_ref, hidden_ref, *out_refs):
    gate = gate_ref[...].astype(jnp.float32)
    up = up_ref[...].astype(jnp.float32)
    hidden = (gate * jax.nn.sigmoid(gate) * up).astype(jnp.bfloat16)
    hidden_ref[...] = hidden
    pick(hidden, named_ref, out_refs)


def pick_kernel(hidden_ref, named_ref, *out_refs):
    pick(hidden_ref[...], named_ref, out_refs)


def picked_rows(kernel, arrays, named, experts, topk, with_hidden):
    count_rows, cols = arrays[0].shape
    group_tok = count_rows // topk
    some = 128 if group_tok % 128 == 0 else group_tok
    row_block = pl.BlockSpec((some * topk, cols), lambda i: (i, 0))
    sizes = [1] + [1 << b for b in range(experts.bit_length() - 1)]
    out_shape = [jax.ShapeDtypeStruct((n, group_tok, cols), jnp.bfloat16) for n in sizes]
    out_specs = [pl.BlockSpec((n, some, cols), lambda i: (0, i, 0)) for n in sizes]
    if with_hidden:
        out_shape = [jax.ShapeDtypeStruct((count_rows, cols), jnp.bfloat16)] + out_shape
        out_specs = [row_block] + out_specs
    return pl.pallas_call(
        kernel,
        grid=(group_tok // some,),
        in_specs=[row_block] * len(arrays) + [pl.BlockSpec((1, some * topk), lambda i: (0, i))],
        out_specs=out_specs,
        out_shape=out_shape,
        compiler_params=pltpu.CompilerParams(vmem_limit_bytes=56 * MIB),
        cost_estimate=pl.CostEstimate(
            flops=2 * experts * count_rows * some * cols,
            bytes_accessed=2 * cols * (count_rows * (len(arrays) + 1) + experts * group_tok),
            transcendentals=count_rows * cols,
        ),
        name="hidden_rows",
    )(*arrays, named)


def spread(picked, experts):
    held = {0: {(1 << i) >> 1: rows for i, rows in enumerate(picked)}}
    bit = experts // 2
    while bit:
        for group in list(held):
            got = swapped(held[group][bit], "expert", bit)
            held[group ^ bit] = {0: got[:1]}
            for i in range(bit.bit_length() - 1):
                held[group ^ bit][1 << i] = got[1 << i : 2 << i]
        bit //= 2
    return [held[m][0][0] for m in range(experts)]


def term_kernel(count, place_ref, *refs):
    tokens, hidden, outs = refs[:count], refs[count : 2 * count], refs[2 * count :]
    total = None
    for token_ref, hidden_ref in zip(tokens, hidden):
        one = lax.dot_general(
            token_ref[...],
            hidden_ref[...],
            (((0,), (0,)), ((), ())),
            preferred_element_type=jnp.float32,
        )
        total = one if total is None else total + one
    total = total.astype(jnp.bfloat16)
    for m, out_ref in enumerate(outs):

        @pl.when(pl.program_id(0) == m)
        def _():
            out_ref[...] = total


def terms(tokens, hidden, tall, steps, block_of, place):
    group_tok, width = tokens[0].shape
    cols = hidden[0].shape[1]
    count = len(tokens)
    return pl.pallas_call(
        functools.partial(term_kernel, count),
        grid_spec=pltpu.PrefetchScalarGridSpec(
            num_scalar_prefetch=1,
            grid=(steps,),
            in_specs=[
                pl.BlockSpec((group_tok, tall), lambda m, place: (0, block_of(place[0], m)))
            ]
            * count
            + [pl.BlockSpec((group_tok, cols), lambda m, place: (0, 0))] * count,
            out_specs=[pl.BlockSpec((tall, cols), lambda m, place: (0, 0))] * steps,
        ),
        out_shape=[jax.ShapeDtypeStruct((tall, cols), jnp.bfloat16)] * steps,
        compiler_params=pltpu.CompilerParams(vmem_limit_bytes=56 * MIB),
        cost_estimate=pl.CostEstimate(
            flops=2 * count * group_tok * steps * tall * cols,
            bytes_accessed=2 * (count * group_tok * (steps * tall + cols) + steps * tall * cols),
            transcendentals=0,
        ),
        name="group_terms",
    )(place.reshape(1), *tokens, *hidden)


def deriv_kernel(tokens_ref, weight_ref, out_ref):
    out_ref[...] = jnp.dot(
        tokens_ref[...], weight_ref[...], preferred_element_type=jnp.float32
    )


def deriv_of(tokens, weight):
    group_tok, width = tokens.shape
    cols = weight.shape[1]
    wide = 256 if cols % 256 == 0 else cols
    return pl.pallas_call(
        deriv_kernel,
        grid=(cols // wide,),
        in_specs=[
            pl.BlockSpec((group_tok, width), lambda i: (0, 0)),
            pl.BlockSpec((width, wide), lambda i: (0, i)),
        ],
        out_specs=pl.BlockSpec((group_tok, wide), lambda i: (0, i)),
        out_shape=jax.ShapeDtypeStruct((group_tok, cols), jnp.float32),
        compiler_params=pltpu.CompilerParams(vmem_limit_bytes=56 * MIB),
        cost_estimate=pl.CostEstimate(
            flops=2 * group_tok * width * cols,
            bytes_accessed=2 * (group_tok + cols) * width + 4 * group_tok * cols,
            transcendentals=0,
        ),
        name="hidden_deriv",
    )(tokens, weight)


def update_kernel(count, place_ref, weight_ref, momentum_ref, *refs):
    grad_refs = refs[:count]
    new_weight_ref, new_momentum_ref = refs[-2:]
    for m, grad_ref in enumerate(grad_refs):

        @pl.when(pl.program_id(0) == m)
        def _():
            grad = grad_ref[...].astype(jnp.float32)
            moment = momentum_ref[0].astype(jnp.float32)
            weight = weight_ref[0].astype(jnp.float32)
            mix = beta_first * moment + (1.0 - beta_first) * grad
            new_weight_ref[0] = weight * (1.0 - step_rate * decay_rate) - step_rate * jnp.tanh(
                mix / sign_width
            )
            new_momentum_ref[0] = (beta_second * moment + (1.0 - beta_second) * grad).astype(
                jnp.bfloat16
            )


def update(part, place, grads, weight, momentum, done):
    count, rows, some = weight.shape
    parts = grads[0].shape[1] // some
    wide = pl.BlockSpec((1, rows, some), lambda m, place: (0, 0, (place[0] ^ m) * parts + part))
    size = weight.size
    return pl.pallas_call(
        functools.partial(update_kernel, count),
        grid_spec=pltpu.PrefetchScalarGridSpec(
            num_scalar_prefetch=1,
            grid=(count,),
            in_specs=[pl.BlockSpec((1, rows, some), lambda m, place: (place[0] ^ m, 0, 0)), wide]
            + [pl.BlockSpec((rows, some), lambda m, place: (0, part))] * count
            + [pl.BlockSpec(memory_space=pl.ANY)] * len(done),
            out_specs=[wide, wide],
        ),
        out_shape=[
            jax.ShapeDtypeStruct(momentum.shape, jnp.float32),
            jax.ShapeDtypeStruct(momentum.shape, jnp.bfloat16),
        ],
        input_output_aliases={3 + count + i: i for i in range(len(done))},
        compiler_params=pltpu.CompilerParams(vmem_limit_bytes=56 * MIB),
        cost_estimate=pl.CostEstimate(flops=10 * size, bytes_accessed=12 * size, transcendentals=size),
        name="lion_step",
    )(place.reshape(1), weight, momentum, *grads, *done)


def gathered(held, experts, shards, place):
    groups = {0: held}
    for m in sorted(range(2, experts, 2), key=lambda m: (bin(m).count("1"), -m)):
        groups[m] = swapped(groups[m & (m - 1)], "expert", m & -m)
    for m in list(groups):
        both = in_order(groups[m], swapped(groups[m], "dp", 1), (place & 1) != 0)
        groups[m] = both.reshape(-1, held.shape[2])
        groups[m + 1] = swapped(groups[m], "expert", 1)
    return [groups[m] for m in range(experts)]


def body(out_grad, gate_saved, up_saved, routing, down_weight, momentum):
    experts = lax.axis_size("expert")
    shards = lax.axis_size("dp")
    group_tok, topk, cols = gate_saved.shape
    width = out_grad.shape[1]
    rows = momentum.shape[1]
    mine = lax.axis_index("expert")
    place = lax.axis_index("dp")
    span = shards // 2
    each = range(experts)

    blocks = [swapped(out_grad, "dp", m) for m in range(0, shards, 2)]
    named = (routing ^ mine).reshape(1, group_tok * topk)
    hidden, *own_picked = picked_rows(
        hidden_kernel,
        [gate_saved.reshape(-1, cols), up_saved.reshape(-1, cols)],
        named,
        experts,
        topk,
        True,
    )
    held = placed_blocks([after(block, hidden) for block in blocks], place // 2)
    hidden, own_picked, _ = lax.optimization_barrier((hidden, own_picked, held))
    other_hidden = swapped(hidden, "dp", span)
    tokens = gathered(held, experts, shards, place)
    own_rows = spread(own_picked, experts)
    other_picked = picked_rows(
        pick_kernel, [after(other_hidden, tokens)], named, experts, topk, False
    )
    other_rows = spread(other_picked, experts)

    def shard_terms(hidden_rows):
        if rows % 128 == 0:
            return terms(tokens, hidden_rows, rows, span, lambda place, m: place ^ m, place)
        tall = width // 8
        total = terms(
            tokens, hidden_rows, tall, 4, lambda place, m: place // span * 4 + m, place
        )
        total = jnp.concatenate(total, axis=0)
        return [
            lax.dynamic_slice_in_dim(total, (place % span ^ m) * rows, rows, axis=0)
            for m in range(span)
        ]

    own_terms = shard_terms(own_rows)
    other_terms = shard_terms(other_rows)

    weight = down_weight[0]
    parts = 2 if cols % 256 == 0 else 1
    pieces = jnp.split(down_weight.reshape(shards, rows, cols), parts, axis=2)
    weights = []
    for part, piece in enumerate(pieces):
        begun = [other_hidden] if part == 0 else [weights[-1], other_terms]
        weights.append(
            lax.all_to_all(after(piece, *begun), "dp", split_axis=0, concat_axis=0, tiled=True)
        )

    other_terms = after(other_terms, weights[0])
    grads = {}
    for m in range(span):
        grads[m] = swapped(own_terms[m], "dp", m)
        grads[m ^ span] = swapped(other_terms[m], "dp", m)

    back_weight, gate_saved, up_saved, *_ = lax.optimization_barrier(
        (weight, gate_saved, up_saved, own_terms)
    )
    gate = gate_saved.astype(jnp.float32)
    up = up_saved.astype(jnp.float32)
    sigma = jax.nn.sigmoid(gate)
    deriv = jnp.zeros(gate.shape, jnp.float32)
    for m in list(range(experts // 2, experts)) + list(range(experts // 2)):
        part = deriv_of(tokens[m], back_weight)
        if m >= experts // 2:
            part = after(part, other_rows[experts // 2])
        chosen = (routing == (mine ^ m))[:, :, None]
        deriv = jnp.where(chosen, swapped(part, "expert", m)[:, None, :], deriv)
    d_up = (deriv * gate * sigma).astype(jnp.bfloat16)
    d_gate = (deriv * up * sigma * (1.0 + gate * (1.0 - sigma))).astype(jnp.bfloat16)

    done = ()
    for part in range(parts):
        done = update(part, place, [grads[m] for m in range(shards)], weights[part], momentum, done)
    new_weight, new_momentum = done
    return (d_gate, d_up, new_weight, new_momentum)


def solution(mesh):
    placed = (
        P(("expert", "dp"), None),
        P("expert", None, "dp"),
        P("expert", None, "dp"),
        P("expert", None),
        P("expert", None, "dp"),
        P("expert", "dp", None),
    )
    return jax.shard_map(
        body,
        mesh=mesh,
        in_specs=placed,
        out_specs=(
            P("expert", None, "dp"),
            P("expert", None, "dp"),
            P("expert", "dp", None),
            P("expert", "dp", None),
        ),
        check_vma=False,
    )
```

```python
import functools

import jax
import jax.numpy as jnp
from jax import lax
from jax.experimental import pallas as pl
from jax.experimental.pallas import tpu as pltpu
from jax.sharding import PartitionSpec as P

beta_first = 0.9
beta_second = 0.99
step_rate = 0.01
decay_rate = 1.0
sign_width = 10.0
MIB = 1024 * 1024
SMALL = pl.CostEstimate(flops=1024, bytes_accessed=1024, transcendentals=0)


def swapped(array, axis, mask):
    if mask == 0:
        return array
    size = lax.axis_size(axis)
    return lax.ppermute(array, axis, [(i, i ^ mask) for i in range(size)])


def after(value, *others):
    return lax.optimization_barrier((value, *others))[0]


def order_kernel(place_ref, mine_ref, theirs_ref, out_ref):
    out_ref[0, place_ref[0]] = mine_ref[0]
    out_ref[0, 1 - place_ref[0]] = theirs_ref[0]


def stage(*values):
    return lax.optimization_barrier(values)


def in_order(mine, theirs, bit):
    count, some, width = mine.shape
    one = pl.BlockSpec((1, some, width), lambda i, place: (i, 0, 0))
    both = pl.pallas_call(
        order_kernel,
        grid_spec=pltpu.PrefetchScalarGridSpec(
            num_scalar_prefetch=1,
            grid=(count,),
            in_specs=[one, one],
            out_specs=pl.BlockSpec((1, 2, some, width), lambda i, place: (i, 0, 0, 0)),
        ),
        out_shape=jax.ShapeDtypeStruct((count, 2, some, width), mine.dtype),
        cost_estimate=SMALL,
        name="side_by_side",
    )(bit.astype(jnp.int32).reshape(1), mine, theirs)
    return both.reshape(2 * count, some, width)


def place_kernel(place_ref, *refs):
    for m, block_ref in enumerate(refs[:-1]):
        refs[-1][place_ref[0] ^ m] = block_ref[...]


def placed_blocks(blocks, place):
    count = len(blocks)
    return pl.pallas_call(
        place_kernel,
        grid_spec=pltpu.PrefetchScalarGridSpec(
            num_scalar_prefetch=1,
            grid=(1,),
            in_specs=[pl.BlockSpec(blocks[0].shape, lambda i, place: (0, 0))] * count,
            out_specs=pl.BlockSpec((count,) + blocks[0].shape, lambda i, place: (0, 0, 0)),
        ),
        out_shape=jax.ShapeDtypeStruct((count,) + blocks[0].shape, blocks[0].dtype),
        compiler_params=pltpu.CompilerParams(vmem_limit_bytes=56 * MIB),
        cost_estimate=SMALL,
        name="placed_blocks",
    )(place.reshape(1), *blocks)


def pick(hidden, named_ref, out_refs):
    count_rows = hidden.shape[0]
    tokens = out_refs[0].shape[1]
    topk = count_rows // tokens
    token = lax.broadcasted_iota(jnp.int32, (tokens, count_rows), 0)
    row = lax.broadcasted_iota(jnp.int32, (tokens, count_rows), 1)
    here = (row >= token * topk) & (row < token * topk + topk)
    m = 0
    for out_ref in out_refs:
        for i in range(out_ref.shape[0]):
            chosen = jnp.where(here & (named_ref[...] == m), 1.0, 0.0).astype(jnp.bfloat16)
            out_ref[i] = jnp.dot(chosen, hidden, preferred_element_type=jnp.float32).astype(
                jnp.bfloat16
            )
            m += 1


def hidden_kernel(gate_ref, up_ref, named_ref, first_ref, second_ref, *out_refs):
    gate = gate_ref[...].astype(jnp.float32)
    up = up_ref[...].astype(jnp.float32)
    hidden = (gate * jax.nn.sigmoid(gate) * up).astype(jnp.bfloat16)
    pick(hidden, named_ref, out_refs)
    early = pl.program_id(0) < pl.num_programs(0) // 2

    @pl.when(early)
    def _():
        first_ref[...] = hidden

    @pl.when(jnp.logical_not(early))
    def _():
        second_ref[...] = hidden


def pick_kernel(first_ref, second_ref, named_ref, *out_refs):
    early = pl.program_id(0) < pl.num_programs(0) // 2

    @pl.when(early)
    def _():
        pick(first_ref[...], named_ref, out_refs)

    @pl.when(jnp.logical_not(early))
    def _():
        pick(second_ref[...], named_ref, out_refs)


def picked_rows(arrays, named, group_tok, experts, fresh):
    cols = arrays[0].shape[1]
    topk = named.shape[1] // group_tok
    some = 128 if group_tok % 256 == 0 else group_tok // 2
    steps = group_tok // some
    sizes = [1] + [1 << b for b in range(experts.bit_length() - 1)]
    out_shape = [jax.ShapeDtypeStruct((n, group_tok, cols), jnp.bfloat16) for n in sizes]
    out_specs = [pl.BlockSpec((n, some, cols), lambda i: (0, i, 0)) for n in sizes]
    rows = (some * topk, cols)
    halves = [
        pl.BlockSpec(rows, lambda i: (jnp.minimum(i, steps // 2 - 1), 0)),
        pl.BlockSpec(rows, lambda i: (jnp.maximum(i - steps // 2, 0), 0)),
    ]
    in_specs = halves
    if fresh:
        in_specs = [pl.BlockSpec(rows, lambda i: (i, 0))] * 2
        half = jax.ShapeDtypeStruct((group_tok * topk // 2, cols), jnp.bfloat16)
        out_shape, out_specs = [half, half] + out_shape, halves + out_specs
    return pl.pallas_call(
        hidden_kernel if fresh else pick_kernel,
        grid=(steps,),
        in_specs=in_specs + [pl.BlockSpec((1, some * topk), lambda i: (0, i))],
        out_specs=out_specs,
        out_shape=out_shape,
        compiler_params=pltpu.CompilerParams(vmem_limit_bytes=56 * MIB),
        cost_estimate=SMALL,
        name="hidden_rows",
    )(*arrays, named)


def spread(picked, got, experts):
    half = experts // 2
    held = {0: {(1 << i) >> 1: rows for i, rows in enumerate(picked)}}
    bit = half
    while bit:
        for group in list(held):
            rows = got if bit == half else swapped(held[group][bit], "expert", bit)
            held[group ^ bit] = {0: rows[:1]}
            for i in range(bit.bit_length() - 1):
                held[group ^ bit][1 << i] = rows[1 << i : 2 << i]
        bit //= 2
    return [held[m][0][0] for m in range(experts)]


def term_kernel(count, place_ref, *refs):
    tokens, hidden, outs = refs[:count], refs[count : 2 * count], refs[2 * count :]
    total = None
    for token_ref, hidden_ref in zip(tokens, hidden):
        one = lax.dot_general(
            token_ref[...],
            hidden_ref[...],
            (((0,), (0,)), ((), ())),
            preferred_element_type=jnp.float32,
        )
        total = one if total is None else total + one
    total = total.astype(jnp.bfloat16)
    for m, out_ref in enumerate(outs):

        @pl.when(pl.program_id(0) == m)
        def _():
            out_ref[...] = total


def terms(tokens, hidden, tall, steps, block_of, place):
    group_tok, width = tokens[0].shape
    cols = hidden[0].shape[1]
    count = len(tokens)
    return pl.pallas_call(
        functools.partial(term_kernel, count),
        grid_spec=pltpu.PrefetchScalarGridSpec(
            num_scalar_prefetch=1,
            grid=(steps,),
            in_specs=[
                pl.BlockSpec((group_tok, tall), lambda m, place: (0, block_of(place[0], m)))
            ]
            * count
            + [pl.BlockSpec((group_tok, cols), lambda m, place: (0, 0))] * count,
            out_specs=[pl.BlockSpec((tall, cols), lambda m, place: (0, 0))] * steps,
        ),
        out_shape=[jax.ShapeDtypeStruct((tall, cols), jnp.bfloat16)] * steps,
        compiler_params=pltpu.CompilerParams(vmem_limit_bytes=56 * MIB),
        cost_estimate=SMALL,
        name="group_terms",
    )(place.reshape(1), *tokens, *hidden)


def deriv_kernel(tokens_ref, weight_ref, out_ref):
    out_ref[...] = jnp.dot(
        tokens_ref[...], weight_ref[...], preferred_element_type=jnp.float32
    )


def deriv_of(tokens, weight):
    group_tok, width = tokens.shape
    cols = weight.shape[1]
    wide = 256 if cols % 256 == 0 else cols
    return pl.pallas_call(
        deriv_kernel,
        grid=(cols // wide,),
        in_specs=[
            pl.BlockSpec((group_tok, width), lambda i: (0, 0)),
            pl.BlockSpec((width, wide), lambda i: (0, i)),
        ],
        out_specs=pl.BlockSpec((group_tok, wide), lambda i: (0, i)),
        out_shape=jax.ShapeDtypeStruct((group_tok, cols), jnp.float32),
        compiler_params=pltpu.CompilerParams(vmem_limit_bytes=56 * MIB),
        cost_estimate=SMALL,
        name="hidden_deriv",
    )(tokens, weight)


def update_kernel(count, place_ref, weight_ref, momentum_ref, *refs):
    grad_refs = refs[:count]
    new_weight_ref, new_momentum_ref = refs[-2:]
    for m, grad_ref in enumerate(grad_refs):

        @pl.when(pl.program_id(0) == m)
        def _():
            grad = grad_ref[...].astype(jnp.float32)
            moment = momentum_ref[0].astype(jnp.float32)
            weight = weight_ref[0].astype(jnp.float32)
            mix = beta_first * moment + (1.0 - beta_first) * grad
            new_weight_ref[0] = weight * (1.0 - step_rate * decay_rate) - step_rate * jnp.tanh(
                mix / sign_width
            )
            new_momentum_ref[0] = (beta_second * moment + (1.0 - beta_second) * grad).astype(
                jnp.bfloat16
            )


def update(part, place, grads, weight, momentum, done):
    count, rows, some = weight.shape
    parts = grads[0].shape[1] // some
    wide = pl.BlockSpec((1, rows, some), lambda m, place: (0, 0, (place[0] ^ m) * parts + part))
    size = weight.size
    return pl.pallas_call(
        functools.partial(update_kernel, count),
        grid_spec=pltpu.PrefetchScalarGridSpec(
            num_scalar_prefetch=1,
            grid=(count,),
            in_specs=[pl.BlockSpec((1, rows, some), lambda m, place: (place[0] ^ m, 0, 0)), wide]
            + [pl.BlockSpec((rows, some), lambda m, place: (0, part))] * count
            + [pl.BlockSpec(memory_space=pl.ANY)] * len(done),
            out_specs=[wide, wide],
        ),
        out_shape=[
            jax.ShapeDtypeStruct(momentum.shape, jnp.float32),
            jax.ShapeDtypeStruct(momentum.shape, jnp.bfloat16),
        ],
        input_output_aliases={3 + count + i: i for i in range(len(done))},
        compiler_params=pltpu.CompilerParams(vmem_limit_bytes=56 * MIB),
        cost_estimate=SMALL,
        name="lion_step",
    )(place.reshape(1), weight, momentum, *grads, *done)


def body(out_grad, gate_saved, up_saved, routing, down_weight, momentum):
    experts = lax.axis_size("expert")
    shards = lax.axis_size("dp")
    group_tok, topk, cols = gate_saved.shape
    width = out_grad.shape[1]
    rows = momentum.shape[1]
    mine = lax.axis_index("expert")
    place = lax.axis_index("dp")
    span = shards // 2
    each = range(experts)

    half = experts // 2
    others = sorted(range(2, experts, 2), key=lambda m: (bin(m).count("1"), -m))

    blocks = [swapped(out_grad, "dp", m) for m in range(0, shards, 2)]
    named = (routing ^ mine).reshape(1, group_tok * topk)
    first, second, *own_picked = picked_rows(
        [gate_saved.reshape(-1, cols), up_saved.reshape(-1, cols)], named, group_tok, experts, True
    )
    blocks, first, second, own_picked = stage(blocks, first, second, own_picked)

    held = {0: placed_blocks(blocks, place // 2)}
    held[0], first = stage(held[0], first)
    for m in others:
        held[m] = swapped(held[m & (m - 1)], "expert", m & -m)
    beside = swapped(held[0], "dp", 1)
    other_first = swapped(first, "dp", span)
    held, beside, other_first, second, own_picked = stage(
        held, beside, other_first, second, own_picked
    )

    last = (place & 1) != 0
    tokens = {0: in_order(held[0], beside, last).reshape(group_tok, width)}
    tokens[1] = swapped(tokens[0], "expert", 1)
    besides = {m: swapped(held[m], "dp", 1) for m in others}
    other_second = swapped(second, "dp", span)
    own_got = swapped(own_picked[-1], "expert", half)
    tokens, besides, other_second, own_got, own_picked = stage(
        tokens, besides, other_second, own_got, own_picked
    )

    for m in others:
        tokens[m] = in_order(held[m], besides[m], last).reshape(group_tok, width)
        tokens[m + 1] = swapped(tokens[m], "expert", 1)
    tokens = [tokens[m] for m in each]
    own_rows = spread(own_picked, own_got, experts)
    other_picked = picked_rows([other_first, other_second], named, group_tok, experts, False)
    other_got = swapped(other_picked[-1], "expert", half)

    def shard_terms(hidden_rows):
        if rows % 128 == 0:
            return terms(tokens, hidden_rows, rows, span, lambda place, m: place ^ m, place)
        tall = width // 8
        total = terms(
            tokens, hidden_rows, tall, 4, lambda place, m: place // span * 4 + m, place
        )
        total = jnp.concatenate(total, axis=0)
        return [
            lax.dynamic_slice_in_dim(total, (place % span ^ m) * rows, rows, axis=0)
            for m in range(span)
        ]

    own_terms = shard_terms(own_rows)
    weight, own_terms = stage(down_weight[0], own_terms)
    derivs = [deriv_of(tokens[m], weight) for m in each]

    other_got, other_picked, derivs = stage(other_got, other_picked, derivs)
    other_rows = spread(other_picked, other_got, experts)
    other_terms = shard_terms(other_rows)

    parts = 2 if cols % 256 == 0 else 1
    pieces = jnp.split(down_weight.reshape(shards, rows, cols), parts, axis=2)
    weights = []
    for part, piece in enumerate(pieces):
        begun = [other_second] if part == 0 else [weights[-1], other_terms]
        weights.append(
            lax.all_to_all(after(piece, *begun), "dp", split_axis=0, concat_axis=0, tiled=True)
        )

    other_terms = after(other_terms, weights[0])
    grads = {}
    for m in range(span):
        grads[m] = swapped(own_terms[m], "dp", m)
        grads[m ^ span] = swapped(other_terms[m], "dp", m)

    gate_saved, up_saved, _ = stage(gate_saved, up_saved, derivs)
    gate = gate_saved.astype(jnp.float32)
    up = up_saved.astype(jnp.float32)
    sigma = jax.nn.sigmoid(gate)
    deriv = jnp.zeros(gate.shape, jnp.float32)
    for m in each:
        chosen = (routing == (mine ^ m))[:, :, None]
        deriv = jnp.where(chosen, swapped(derivs[m], "expert", m)[:, None, :], deriv)
    d_up = (deriv * gate * sigma).astype(jnp.bfloat16)
    d_gate = (deriv * up * sigma * (1.0 + gate * (1.0 - sigma))).astype(jnp.bfloat16)

    done = ()
    for part in range(parts):
        done = update(part, place, [grads[m] for m in range(shards)], weights[part], momentum, done)
    new_weight, new_momentum = done
    return (d_gate, d_up, new_weight, new_momentum)


def solution(mesh):
    placed = (
        P(("expert", "dp"), None),
        P("expert", None, "dp"),
        P("expert", None, "dp"),
        P("expert", None),
        P("expert", None, "dp"),
        P("expert", "dp", None),
    )
    return jax.shard_map(
        body,
        mesh=mesh,
        in_specs=placed,
        out_specs=(
            P("expert", None, "dp"),
            P("expert", None, "dp"),
            P("expert", "dp", None),
            P("expert", "dp", None),
        ),
        check_vma=False,
    )
```

```python
import functools

import jax
import jax.numpy as jnp
from jax import lax
from jax.experimental import pallas as pl
from jax.experimental.pallas import tpu as pltpu
from jax.sharding import PartitionSpec as P

beta_first = 0.9
beta_second = 0.99
step_rate = 0.01
decay_rate = 1.0
sign_width = 10.0
MIB = 1024 * 1024
SMALL = pl.CostEstimate(flops=1024, bytes_accessed=1024, transcendentals=0)


def swapped(array, axis, mask):
    if mask == 0:
        return array
    size = lax.axis_size(axis)
    return lax.ppermute(array, axis, [(i, i ^ mask) for i in range(size)])


def after(value, *others):
    return lax.optimization_barrier((value, *others))[0]


def order_kernel(place_ref, mine_ref, theirs_ref, out_ref):
    out_ref[0, place_ref[0]] = mine_ref[0]
    out_ref[0, 1 - place_ref[0]] = theirs_ref[0]


def stage(*values):
    return lax.optimization_barrier(values)


def in_order(mine, theirs, bit):
    count, some, width = mine.shape
    one = pl.BlockSpec((1, some, width), lambda i, place: (i, 0, 0))
    both = pl.pallas_call(
        order_kernel,
        grid_spec=pltpu.PrefetchScalarGridSpec(
            num_scalar_prefetch=1,
            grid=(count,),
            in_specs=[one, one],
            out_specs=pl.BlockSpec((1, 2, some, width), lambda i, place: (i, 0, 0, 0)),
        ),
        out_shape=jax.ShapeDtypeStruct((count, 2, some, width), mine.dtype),
        cost_estimate=SMALL,
        name="side_by_side",
    )(bit.astype(jnp.int32).reshape(1), mine, theirs)
    return both.reshape(2 * count, some, width)


def place_kernel(place_ref, *refs):
    for m, block_ref in enumerate(refs[:-1]):
        refs[-1][place_ref[0] ^ m] = block_ref[...]


def placed_blocks(blocks, place):
    count = len(blocks)
    return pl.pallas_call(
        place_kernel,
        grid_spec=pltpu.PrefetchScalarGridSpec(
            num_scalar_prefetch=1,
            grid=(1,),
            in_specs=[pl.BlockSpec(blocks[0].shape, lambda i, place: (0, 0))] * count,
            out_specs=pl.BlockSpec((count,) + blocks[0].shape, lambda i, place: (0, 0, 0)),
        ),
        out_shape=jax.ShapeDtypeStruct((count,) + blocks[0].shape, blocks[0].dtype),
        compiler_params=pltpu.CompilerParams(vmem_limit_bytes=56 * MIB),
        cost_estimate=SMALL,
        name="placed_blocks",
    )(place.reshape(1), *blocks)


def pick(hidden, named_ref, out_refs):
    count_rows = hidden.shape[0]
    tokens = out_refs[0].shape[1]
    topk = count_rows // tokens
    token = lax.broadcasted_iota(jnp.int32, (tokens, count_rows), 0)
    row = lax.broadcasted_iota(jnp.int32, (tokens, count_rows), 1)
    here = (row >= token * topk) & (row < token * topk + topk)
    named = named_ref[pl.ds(pl.program_id(0), 1), :]
    m = 0
    for out_ref in out_refs:
        for i in range(out_ref.shape[0]):
            chosen = jnp.where(here & (named == m), 1.0, 0.0).astype(jnp.bfloat16)
            out_ref[i] = jnp.dot(chosen, hidden, preferred_element_type=jnp.float32).astype(
                jnp.bfloat16
            )
            m += 1


EIGHTHS = (3, 4, 1)


def of_part(step, body):
    begin = 0
    for part, count in enumerate(EIGHTHS):
        inside = (step >= begin) & (step < begin + count)
        pl.when(inside)(functools.partial(body, part))
        begin += count


def hidden_kernel(gate_ref, up_ref, named_ref, *refs):
    part_refs, out_refs = refs[: len(EIGHTHS)], refs[len(EIGHTHS) :]
    gate = gate_ref[...].astype(jnp.float32)
    up = up_ref[...].astype(jnp.float32)
    hidden = (gate * jax.nn.sigmoid(gate) * up).astype(jnp.bfloat16)
    pick(hidden, named_ref, out_refs)

    def write(part):
        part_refs[part][...] = hidden

    of_part(pl.program_id(0), write)


def pick_kernel(*refs):
    part_refs, named_ref = refs[: len(EIGHTHS)], refs[len(EIGHTHS)]

    def read(part):
        pick(part_refs[part][...], named_ref, refs[len(EIGHTHS) + 1 :])

    of_part(pl.program_id(0), read)


def picked_rows(arrays, named, group_tok, experts, fresh):
    cols = arrays[0].shape[1]
    topk = named.shape[1] // group_tok
    steps = sum(EIGHTHS)
    some = group_tok // steps
    sizes = [1] + [1 << b for b in range(experts.bit_length() - 1)]
    out_shape = [jax.ShapeDtypeStruct((n, group_tok, cols), jnp.bfloat16) for n in sizes]
    out_specs = [pl.BlockSpec((n, some, cols), lambda i: (0, i, 0)) for n in sizes]
    rows = (some * topk, cols)
    in_parts = [
        pl.BlockSpec(
            rows,
            lambda i, begin=sum(EIGHTHS[:p]), count=count: (jnp.clip(i - begin, 0, count - 1), 0),
        )
        for p, count in enumerate(EIGHTHS)
    ]
    in_specs = in_parts
    if fresh:
        in_specs = [pl.BlockSpec(rows, lambda i: (i, 0))] * 2
        out_shape = [
            jax.ShapeDtypeStruct((n * some * topk, cols), jnp.bfloat16) for n in EIGHTHS
        ] + out_shape
        out_specs = in_parts + out_specs
    return pl.pallas_call(
        hidden_kernel if fresh else pick_kernel,
        grid=(steps,),
        in_specs=in_specs + [pl.BlockSpec((steps, some * topk), lambda i: (0, 0))],
        out_specs=out_specs,
        out_shape=out_shape,
        compiler_params=pltpu.CompilerParams(vmem_limit_bytes=56 * MIB),
        cost_estimate=SMALL,
        name="hidden_rows",
    )(*arrays, named.reshape(steps, some * topk))


def spread(picked, got, experts):
    half = experts // 2
    held = {0: {(1 << i) >> 1: rows for i, rows in enumerate(picked)}}
    bit = half
    while bit:
        for group in list(held):
            rows = got if bit == half else swapped(held[group][bit], "expert", bit)
            held[group ^ bit] = {0: rows[:1]}
            for i in range(bit.bit_length() - 1):
                held[group ^ bit][1 << i] = rows[1 << i : 2 << i]
        bit //= 2
    return [held[m][0][0] for m in range(experts)]


def term_kernel(count, place_ref, *refs):
    tokens, hidden, outs = refs[:count], refs[count : 2 * count], refs[2 * count :]
    total = None
    for token_ref, hidden_ref in zip(tokens, hidden):
        one = lax.dot_general(
            token_ref[...],
            hidden_ref[...],
            (((0,), (0,)), ((), ())),
            preferred_element_type=jnp.float32,
        )
        total = one if total is None else total + one
    total = total.astype(jnp.bfloat16)
    for m, out_ref in enumerate(outs):

        @pl.when(pl.program_id(0) == m)
        def _():
            out_ref[...] = total


def terms(tokens, hidden, tall, steps, block_of, place):
    group_tok, width = tokens[0].shape
    cols = hidden[0].shape[1]
    count = len(tokens)
    return pl.pallas_call(
        functools.partial(term_kernel, count),
        grid_spec=pltpu.PrefetchScalarGridSpec(
            num_scalar_prefetch=1,
            grid=(steps,),
            in_specs=[
                pl.BlockSpec((group_tok, tall), lambda m, place: (0, block_of(place[0], m)))
            ]
            * count
            + [pl.BlockSpec((group_tok, cols), lambda m, place: (0, 0))] * count,
            out_specs=[pl.BlockSpec((tall, cols), lambda m, place: (0, 0))] * steps,
        ),
        out_shape=[jax.ShapeDtypeStruct((tall, cols), jnp.bfloat16)] * steps,
        compiler_params=pltpu.CompilerParams(vmem_limit_bytes=56 * MIB),
        cost_estimate=SMALL,
        name="group_terms",
    )(place.reshape(1), *tokens, *hidden)


def deriv_kernel(tokens_ref, weight_ref, out_ref):
    out_ref[...] = jnp.dot(
        tokens_ref[...], weight_ref[...], preferred_element_type=jnp.float32
    )


def deriv_of(tokens, weight):
    group_tok, width = tokens.shape
    cols = weight.shape[1]
    wide = 256 if cols % 256 == 0 else cols
    return pl.pallas_call(
        deriv_kernel,
        grid=(cols // wide,),
        in_specs=[
            pl.BlockSpec((group_tok, width), lambda i: (0, 0)),
            pl.BlockSpec((width, wide), lambda i: (0, i)),
        ],
        out_specs=pl.BlockSpec((group_tok, wide), lambda i: (0, i)),
        out_shape=jax.ShapeDtypeStruct((group_tok, cols), jnp.float32),
        compiler_params=pltpu.CompilerParams(vmem_limit_bytes=56 * MIB),
        cost_estimate=pl.CostEstimate(
            flops=2 * group_tok * width * cols,
            bytes_accessed=2 * (group_tok + cols) * width + 4 * group_tok * cols,
            transcendentals=0,
        ),
        name="hidden_deriv",
    )(tokens, weight)


def update_kernel(count, place_ref, weight_ref, momentum_ref, *refs):
    grad_refs = refs[:count]
    new_weight_ref, new_momentum_ref = refs[-2:]
    for m, grad_ref in enumerate(grad_refs):

        @pl.when(pl.program_id(0) == m)
        def _():
            grad = grad_ref[...].astype(jnp.float32)
            moment = momentum_ref[0].astype(jnp.float32)
            weight = weight_ref[0].astype(jnp.float32)
            mix = beta_first * moment + (1.0 - beta_first) * grad
            new_weight_ref[0] = weight * (1.0 - step_rate * decay_rate) - step_rate * jnp.tanh(
                mix / sign_width
            )
            new_momentum_ref[0] = (beta_second * moment + (1.0 - beta_second) * grad).astype(
                jnp.bfloat16
            )


def update(part, place, grads, weight, momentum, done):
    _, rows, some = weight.shape
    count = len(grads)
    parts = grads[0].shape[1] // some
    wide = pl.BlockSpec((1, rows, some), lambda m, place: (0, 0, (place[0] ^ m) * parts + part))
    return pl.pallas_call(
        functools.partial(update_kernel, count),
        grid_spec=pltpu.PrefetchScalarGridSpec(
            num_scalar_prefetch=1,
            grid=(count,),
            in_specs=[pl.BlockSpec((1, rows, some), lambda m, place: (place[0] ^ m, 0, 0)), wide]
            + [pl.BlockSpec((rows, some), lambda m, place: (0, part))] * count
            + [pl.BlockSpec(memory_space=pl.ANY)] * len(done),
            out_specs=[wide, wide],
        ),
        out_shape=[
            jax.ShapeDtypeStruct(momentum.shape, jnp.float32),
            jax.ShapeDtypeStruct(momentum.shape, jnp.bfloat16),
        ],
        input_output_aliases={3 + count + i: i for i in range(len(done))},
        compiler_params=pltpu.CompilerParams(vmem_limit_bytes=56 * MIB),
        cost_estimate=SMALL,
        name="lion_step",
    )(place.reshape(1), weight, momentum, *grads, *done)


def body(out_grad, gate_saved, up_saved, routing, down_weight, momentum):
    experts = lax.axis_size("expert")
    shards = lax.axis_size("dp")
    group_tok, topk, cols = gate_saved.shape
    width = out_grad.shape[1]
    rows = momentum.shape[1]
    mine = lax.axis_index("expert")
    place = lax.axis_index("dp")
    span = shards // 2
    each = range(experts)

    half = experts // 2
    others = sorted(range(2, experts, 2), key=lambda m: (bin(m).count("1"), -m))

    blocks = [swapped(out_grad, "dp", m) for m in range(0, shards, 2)]
    named = (routing ^ mine).reshape(1, group_tok * topk)
    hidden = picked_rows(
        [gate_saved.reshape(-1, cols), up_saved.reshape(-1, cols)], named, group_tok, experts, True
    )
    own_parts, own_picked = hidden[: len(EIGHTHS)], hidden[len(EIGHTHS) :]
    blocks, own_parts, own_picked = stage(blocks, own_parts, own_picked)

    held = {0: placed_blocks(blocks, place // 2)}
    held[0], own_parts = stage(held[0], own_parts)
    for m in others:
        held[m] = swapped(held[m & (m - 1)], "expert", m & -m)
    beside = {0: swapped(held[0], "dp", 1)}
    other_parts = [swapped(own_parts[0], "dp", span)]
    held, beside, other_parts, own_parts, own_picked = stage(
        held, beside, other_parts, own_parts, own_picked
    )

    last = (place & 1) != 0
    for m in others:
        beside[m] = swapped(held[m], "dp", 1)
    other_parts.append(swapped(own_parts[1], "dp", span))
    own_got = swapped(own_picked[-1], "expert", half)
    tokens = {0: in_order(held[0], beside[0], last).reshape(group_tok, width)}
    tokens[1] = swapped(tokens[0], "expert", 1)
    tokens, beside, own_got, own_picked, own_parts, other_parts = stage(
        tokens, beside, own_got, own_picked, own_parts, other_parts
    )

    for m in others:
        tokens[m] = in_order(held[m], beside[m], last).reshape(group_tok, width)
        tokens[m + 1] = swapped(tokens[m], "expert", 1)
    tokens = [tokens[m] for m in each]
    other_parts.append(swapped(own_parts[2], "dp", span))
    own_rows = spread(own_picked, own_got, experts)
    tokens, own_rows, other_parts = stage(tokens, own_rows, other_parts)

    other_picked = picked_rows(other_parts, named, group_tok, experts, False)
    other_got = swapped(other_picked[-1], "expert", half)

    def shard_terms(hidden_rows):
        if rows % 128 == 0:
            return terms(tokens, hidden_rows, rows, span, lambda place, m: place ^ m, place)
        tall = width // 8
        total = terms(
            tokens, hidden_rows, tall, 4, lambda place, m: place // span * 4 + m, place
        )
        total = jnp.concatenate(total, axis=0)
        return [
            lax.dynamic_slice_in_dim(total, (place % span ^ m) * rows, rows, axis=0)
            for m in range(span)
        ]

    own_terms = shard_terms(own_rows)
    weight, own_terms = stage(down_weight[0], own_terms)
    derivs = [deriv_of(tokens[m], weight) for m in each]

    other_got, other_picked, derivs = stage(other_got, other_picked, derivs)
    own_grads = [swapped(own_terms[m], "dp", m) for m in range(span)]
    other_rows = spread(other_picked, other_got, experts)
    other_rows, own_grads = stage(other_rows, own_grads)
    other_terms = shard_terms(other_rows)

    parts = 2 if cols % 256 == 0 else 1
    pieces = jnp.split(down_weight.reshape(shards, rows, cols), parts, axis=2)
    weights = []
    for part, piece in enumerate(pieces):
        begun = [other_parts] if part == 0 else [weights[-1], other_terms]
        weights.append(
            lax.all_to_all(after(piece, *begun), "dp", split_axis=0, concat_axis=0, tiled=True)
        )

    other_terms = after(other_terms, weights[0])
    other_grads = [swapped(other_terms[m], "dp", m) for m in range(span)]

    gate_saved, up_saved, _ = stage(gate_saved, up_saved, derivs)
    gate = gate_saved.astype(jnp.float32)
    up = up_saved.astype(jnp.float32)
    sigma = jax.nn.sigmoid(gate)
    deriv = jnp.zeros(gate.shape, jnp.float32)
    for m in each:
        chosen = (routing == (mine ^ m))[:, :, None]
        deriv = jnp.where(chosen, swapped(derivs[m], "expert", m)[:, None, :], deriv)
    d_up = (deriv * gate * sigma).astype(jnp.bfloat16)
    d_gate = (deriv * up * sigma * (1.0 + gate * (1.0 - sigma))).astype(jnp.bfloat16)

    done = ()
    for part, grads, off in [
        (part, grads, off)
        for part in range(parts)
        for grads, off in ((own_grads, 0), (other_grads, span))
    ]:
        done = update(part, place ^ off, grads, weights[part], momentum, done)
    new_weight, new_momentum = done
    return (d_gate, d_up, new_weight, new_momentum)


def solution(mesh):
    placed = (
        P(("expert", "dp"), None),
        P("expert", None, "dp"),
        P("expert", None, "dp"),
        P("expert", None),
        P("expert", None, "dp"),
        P("expert", "dp", None),
    )
    return jax.shard_map(
        body,
        mesh=mesh,
        in_specs=placed,
        out_specs=(
            P("expert", None, "dp"),
            P("expert", None, "dp"),
            P("expert", "dp", None),
            P("expert", "dp", None),
        ),
        check_vma=False,
    )
```

```python
import functools

import jax
import jax.numpy as jnp
from jax import lax
from jax.experimental import pallas as pl
from jax.experimental.pallas import tpu as pltpu
from jax.sharding import PartitionSpec as P

beta_first = 0.9
beta_second = 0.99
step_rate = 0.01
decay_rate = 1.0
sign_width = 10.0
MIB = 1024 * 1024
SMALL = pl.CostEstimate(flops=1024, bytes_accessed=1024, transcendentals=0)


def swapped(array, axis, mask):
    if mask == 0:
        return array
    size = lax.axis_size(axis)
    return lax.ppermute(array, axis, [(i, i ^ mask) for i in range(size)])


def after(value, *others):
    return lax.optimization_barrier((value, *others))[0]


def order_kernel(place_ref, mine_ref, theirs_ref, out_ref):
    out_ref[0, place_ref[0]] = mine_ref[0]
    out_ref[0, 1 - place_ref[0]] = theirs_ref[0]


def stage(*values):
    return lax.optimization_barrier(values)


def in_order(mine, theirs, bit):
    count, some, width = mine.shape
    one = pl.BlockSpec((1, some, width), lambda i, place: (i, 0, 0))
    both = pl.pallas_call(
        order_kernel,
        grid_spec=pltpu.PrefetchScalarGridSpec(
            num_scalar_prefetch=1,
            grid=(count,),
            in_specs=[one, one],
            out_specs=pl.BlockSpec((1, 2, some, width), lambda i, place: (i, 0, 0, 0)),
        ),
        out_shape=jax.ShapeDtypeStruct((count, 2, some, width), mine.dtype),
        cost_estimate=SMALL,
        name="side_by_side",
    )(bit.astype(jnp.int32).reshape(1), mine, theirs)
    return both.reshape(2 * count, some, width)


def place_kernel(place_ref, *refs):
    for m, block_ref in enumerate(refs[:-1]):
        refs[-1][place_ref[0] ^ m] = block_ref[...]


def placed_blocks(blocks, place):
    count = len(blocks)
    return pl.pallas_call(
        place_kernel,
        grid_spec=pltpu.PrefetchScalarGridSpec(
            num_scalar_prefetch=1,
            grid=(1,),
            in_specs=[pl.BlockSpec(blocks[0].shape, lambda i, place: (0, 0))] * count,
            out_specs=pl.BlockSpec((count,) + blocks[0].shape, lambda i, place: (0, 0, 0)),
        ),
        out_shape=jax.ShapeDtypeStruct((count,) + blocks[0].shape, blocks[0].dtype),
        compiler_params=pltpu.CompilerParams(vmem_limit_bytes=56 * MIB),
        cost_estimate=SMALL,
        name="placed_blocks",
    )(place.reshape(1), *blocks)


def pick(hidden, named_ref, out_refs):
    count_rows = hidden.shape[0]
    tokens = out_refs[0].shape[1]
    topk = count_rows // tokens
    token = lax.broadcasted_iota(jnp.int32, (tokens, count_rows), 0)
    row = lax.broadcasted_iota(jnp.int32, (tokens, count_rows), 1)
    here = (row >= token * topk) & (row < token * topk + topk)
    named = named_ref[pl.ds(pl.program_id(0), 1), :]
    m = 0
    for out_ref in out_refs:
        for i in range(out_ref.shape[0]):
            chosen = jnp.where(here & (named == m), 1.0, 0.0).astype(jnp.bfloat16)
            out_ref[i] = jnp.dot(chosen, hidden, preferred_element_type=jnp.float32).astype(
                jnp.bfloat16
            )
            m += 1


def hidden_kernel(gate_ref, up_ref, named_ref, *out_refs):
    gate = gate_ref[...].astype(jnp.float32)
    up = up_ref[...].astype(jnp.float32)
    pick((gate * jax.nn.sigmoid(gate) * up).astype(jnp.bfloat16), named_ref, out_refs)


def picked_rows(gate, up, named, group_tok, experts):
    cols = gate.shape[1]
    topk = named.shape[1] // group_tok
    steps = 4
    some = group_tok // steps
    sizes = [1] + [1 << b for b in range(experts.bit_length() - 1)]
    rows = pl.BlockSpec((some * topk, cols), lambda i: (i, 0))
    return pl.pallas_call(
        hidden_kernel,
        grid=(steps,),
        in_specs=[rows, rows, pl.BlockSpec((steps, some * topk), lambda i: (0, 0))],
        out_specs=[pl.BlockSpec((n, some, cols), lambda i: (0, i, 0)) for n in sizes],
        out_shape=[jax.ShapeDtypeStruct((n, group_tok, cols), jnp.bfloat16) for n in sizes],
        compiler_params=pltpu.CompilerParams(vmem_limit_bytes=56 * MIB),
        cost_estimate=SMALL,
        name="hidden_rows",
    )(gate, up, named.reshape(steps, some * topk))


def spread(picked, got, experts):
    half = experts // 2
    held = {0: {(1 << i) >> 1: rows for i, rows in enumerate(picked)}}
    bit = half
    while bit:
        for group in list(held):
            rows = got if bit == half else swapped(held[group][bit], "expert", bit)
            held[group ^ bit] = {0: rows[:1]}
            for i in range(bit.bit_length() - 1):
                held[group ^ bit][1 << i] = rows[1 << i : 2 << i]
        bit //= 2
    return [held[m][0][0] for m in range(experts)]


def term_kernel(count, *refs):
    tokens, hidden, out_ref = refs[:count], refs[count : 2 * count], refs[-1]
    total = None
    for token_ref, hidden_ref in zip(tokens, hidden):
        one = lax.dot_general(
            token_ref[...],
            hidden_ref[...],
            (((0,), (0,)), ((), ())),
            preferred_element_type=jnp.float32,
        )
        total = one if total is None else total + one
    out_ref[...] = total.astype(jnp.bfloat16)


def terms(part, parts, tokens, hidden):
    group_tok, width = tokens[0].shape
    cols = hidden[0].shape[1] // parts
    tall = width // 8
    count = len(tokens)
    return pl.pallas_call(
        functools.partial(term_kernel, count),
        grid=(width // tall,),
        in_specs=[pl.BlockSpec((group_tok, tall), lambda i: (0, i))] * count
        + [pl.BlockSpec((group_tok, cols), lambda i: (0, part))] * count,
        out_specs=pl.BlockSpec((tall, cols), lambda i: (i, 0)),
        out_shape=jax.ShapeDtypeStruct((width, cols), jnp.bfloat16),
        compiler_params=pltpu.CompilerParams(vmem_limit_bytes=56 * MIB),
        cost_estimate=SMALL,
        name="group_terms",
    )(*tokens, *hidden)


def deriv_kernel(tokens_ref, weight_ref, out_ref):
    out_ref[...] = jnp.dot(
        tokens_ref[...], weight_ref[...], preferred_element_type=jnp.float32
    )


def deriv_of(tokens, weight):
    group_tok, width = tokens.shape
    cols = weight.shape[1]
    wide = 256 if cols % 256 == 0 else cols
    return pl.pallas_call(
        deriv_kernel,
        grid=(cols // wide,),
        in_specs=[
            pl.BlockSpec((group_tok, width), lambda i: (0, 0)),
            pl.BlockSpec((width, wide), lambda i: (0, i)),
        ],
        out_specs=pl.BlockSpec((group_tok, wide), lambda i: (0, i)),
        out_shape=jax.ShapeDtypeStruct((group_tok, cols), jnp.float32),
        compiler_params=pltpu.CompilerParams(vmem_limit_bytes=56 * MIB),
        cost_estimate=pl.CostEstimate(
            flops=2 * group_tok * width * cols,
            bytes_accessed=2 * (group_tok + cols) * width + 4 * group_tok * cols,
            transcendentals=0,
        ),
        name="hidden_deriv",
    )(tokens, weight)


def update_kernel(grad_ref, weight_ref, momentum_ref, *refs):
    new_weight_ref, new_momentum_ref = refs[-2:]
    grad = grad_ref[0].astype(jnp.float32)
    moment = momentum_ref[0].astype(jnp.float32)
    weight = weight_ref[0].astype(jnp.float32)
    mix = beta_first * moment + (1.0 - beta_first) * grad
    new_weight_ref[0] = weight * (1.0 - step_rate * decay_rate) - step_rate * jnp.tanh(
        mix / sign_width
    )
    new_momentum_ref[0] = (beta_second * moment + (1.0 - beta_second) * grad).astype(
        jnp.bfloat16
    )


def update(part, parts, grad, weight, momentum, done):
    count, rows, some = weight.shape
    own = pl.BlockSpec((1, rows, some), lambda m: (m, 0, 0))
    wide = pl.BlockSpec((1, rows, some), lambda m: (0, 0, m * parts + part))
    return pl.pallas_call(
        update_kernel,
        grid=(count,),
        in_specs=[own, own, wide] + [pl.BlockSpec(memory_space=pl.ANY)] * len(done),
        out_specs=[wide, wide],
        out_shape=[
            jax.ShapeDtypeStruct(momentum.shape, jnp.float32),
            jax.ShapeDtypeStruct(momentum.shape, jnp.bfloat16),
        ],
        input_output_aliases={3 + i: i for i in range(len(done))},
        compiler_params=pltpu.CompilerParams(vmem_limit_bytes=56 * MIB),
        cost_estimate=SMALL,
        name="lion_step",
    )(grad, weight, momentum, *done)


def body(out_grad, gate_saved, up_saved, routing, down_weight, momentum):
    experts = lax.axis_size("expert")
    shards = lax.axis_size("dp")
    group_tok, topk, cols = gate_saved.shape
    width = out_grad.shape[1]
    rows = momentum.shape[1]
    mine = lax.axis_index("expert")
    place = lax.axis_index("dp")
    each = range(experts)

    half = experts // 2
    others = sorted(range(2, experts, 2), key=lambda m: (bin(m).count("1"), -m))

    parts = 2 if cols % 256 == 0 else 1

    def to_owners(array, *begun):
        array = after(array.reshape(shards, rows, cols // parts), *begun)
        return lax.all_to_all(array, "dp", split_axis=0, concat_axis=0, tiled=True)

    blocks = [swapped(out_grad, "dp", m) for m in range(0, shards, 2)]
    named = (routing ^ mine).reshape(1, group_tok * topk)
    picked = picked_rows(
        gate_saved.reshape(-1, cols), up_saved.reshape(-1, cols), named, group_tok, experts
    )
    pieces = jnp.split(down_weight[0], parts, axis=1)
    weights = [to_owners(pieces[0], picked)]
    blocks, picked = stage(blocks, picked)

    held = {0: placed_blocks(blocks, place // 2)}
    for m in others:
        held[m] = swapped(held[m & (m - 1)], "expert", m & -m)
    beside = {0: swapped(held[0], "dp", 1)}
    held, beside, picked, weights = stage(held, beside, picked, weights)

    for piece in pieces[1:]:
        weights.append(to_owners(piece, weights))
    last = (place & 1) != 0
    for m in others:
        beside[m] = swapped(held[m], "dp", 1)
    got = swapped(picked[-1], "expert", half)
    tokens = {}
    for m in [0] + others:
        tokens[m] = in_order(held[m], beside[m], last).reshape(group_tok, width)
        tokens[m + 1] = swapped(tokens[m], "expert", 1)
    tokens = [tokens[m] for m in each]
    hidden = spread(picked, got, experts)
    tokens, hidden = stage(tokens, hidden)

    term = terms(0, parts, tokens, hidden)
    weight, term = stage(down_weight[0], term)
    derivs = [deriv_of(tokens[m], weight) for m in each]
    backs = [swapped(derivs[m], "expert", m) for m in each]
    grads = [to_owners(term, weights)]
    for part in range(1, parts):
        term = terms(part, parts, tokens, after(hidden, derivs))
        grads.append(to_owners(term, grads, backs[half]))

    gate_saved, up_saved, _ = stage(gate_saved, up_saved, derivs)
    gate = gate_saved.astype(jnp.float32)
    up = up_saved.astype(jnp.float32)
    sigma = jax.nn.sigmoid(gate)
    deriv = jnp.zeros(gate.shape, jnp.float32)
    for m in each:
        chosen = (routing == (mine ^ m))[:, :, None]
        deriv = jnp.where(chosen, backs[m][:, None, :], deriv)
    d_up = (deriv * gate * sigma).astype(jnp.bfloat16)
    d_gate = (deriv * up * sigma * (1.0 + gate * (1.0 - sigma))).astype(jnp.bfloat16)

    done = ()
    for part in range(parts):
        done = update(part, parts, grads[part], weights[part], momentum, done)
    new_weight, new_momentum = done
    return (d_gate, d_up, new_weight, new_momentum)


def solution(mesh):
    placed = (
        P(("expert", "dp"), None),
        P("expert", None, "dp"),
        P("expert", None, "dp"),
        P("expert", None),
        P("expert", None, "dp"),
        P("expert", "dp", None),
    )
    return jax.shard_map(
        body,
        mesh=mesh,
        in_specs=placed,
        out_specs=(
            P("expert", None, "dp"),
            P("expert", None, "dp"),
            P("expert", "dp", None),
            P("expert", "dp", None),
        ),
        check_vma=False,
    )
```

```python
import functools

import jax
import jax.numpy as jnp
from jax import lax
from jax.experimental import pallas as pl
from jax.experimental.pallas import tpu as pltpu
from jax.sharding import PartitionSpec as P

beta_first = 0.9
beta_second = 0.99
step_rate = 0.01
decay_rate = 1.0
sign_width = 10.0
MIB = 1024 * 1024
SMALL = pl.CostEstimate(flops=1024, bytes_accessed=1024, transcendentals=0)


def swapped(array, axis, mask):
    if mask == 0:
        return array
    size = lax.axis_size(axis)
    return lax.ppermute(array, axis, [(i, i ^ mask) for i in range(size)])


def after(value, *others):
    return lax.optimization_barrier((value, *others))[0]


def order_kernel(place_ref, mine_ref, theirs_ref, out_ref):
    out_ref[0, place_ref[0]] = mine_ref[0]
    out_ref[0, 1 - place_ref[0]] = theirs_ref[0]


def stage(*values):
    return lax.optimization_barrier(values)


def in_order(mine, theirs, bit):
    count, some, width = mine.shape
    one = pl.BlockSpec((1, some, width), lambda i, place: (i, 0, 0))
    both = pl.pallas_call(
        order_kernel,
        grid_spec=pltpu.PrefetchScalarGridSpec(
            num_scalar_prefetch=1,
            grid=(count,),
            in_specs=[one, one],
            out_specs=pl.BlockSpec((1, 2, some, width), lambda i, place: (i, 0, 0, 0)),
        ),
        out_shape=jax.ShapeDtypeStruct((count, 2, some, width), mine.dtype),
        cost_estimate=SMALL,
        name="side_by_side",
    )(bit.astype(jnp.int32).reshape(1), mine, theirs)
    return both.reshape(2 * count, some, width)


def place_kernel(place_ref, *refs):
    for m, block_ref in enumerate(refs[:-1]):
        refs[-1][place_ref[0] ^ m] = block_ref[...]


def placed_blocks(blocks, place):
    count = len(blocks)
    return pl.pallas_call(
        place_kernel,
        grid_spec=pltpu.PrefetchScalarGridSpec(
            num_scalar_prefetch=1,
            grid=(1,),
            in_specs=[pl.BlockSpec(blocks[0].shape, lambda i, place: (0, 0))] * count,
            out_specs=pl.BlockSpec((count,) + blocks[0].shape, lambda i, place: (0, 0, 0)),
        ),
        out_shape=jax.ShapeDtypeStruct((count,) + blocks[0].shape, blocks[0].dtype),
        compiler_params=pltpu.CompilerParams(vmem_limit_bytes=56 * MIB),
        cost_estimate=SMALL,
        name="placed_blocks",
    )(place.reshape(1), *blocks)


def pick(hidden, named_ref, out_refs):
    count_rows = hidden.shape[0]
    tokens = out_refs[0].shape[1]
    topk = count_rows // tokens
    token = lax.broadcasted_iota(jnp.int32, (tokens, count_rows), 0)
    row = lax.broadcasted_iota(jnp.int32, (tokens, count_rows), 1)
    here = (row >= token * topk) & (row < token * topk + topk)
    named = named_ref[pl.ds(pl.program_id(0), 1), :]
    m = 0
    for out_ref in out_refs:
        for i in range(out_ref.shape[0]):
            chosen = jnp.where(here & (named == m), 1.0, 0.0).astype(jnp.bfloat16)
            out_ref[i] = jnp.dot(chosen, hidden, preferred_element_type=jnp.float32).astype(
                jnp.bfloat16
            )
            m += 1


def hidden_kernel(gate_ref, up_ref, named_ref, *out_refs):
    gate = gate_ref[...].astype(jnp.float32)
    up = up_ref[...].astype(jnp.float32)
    pick((gate * jax.nn.sigmoid(gate) * up).astype(jnp.bfloat16), named_ref, out_refs)


def picked_rows(gate, up, named, group_tok, experts):
    cols = gate.shape[1]
    topk = named.shape[1] // group_tok
    steps = 4
    some = group_tok // steps
    sizes = [1] + [1 << b for b in range(experts.bit_length() - 1)]
    rows = pl.BlockSpec((some * topk, cols), lambda i: (i, 0))
    return pl.pallas_call(
        hidden_kernel,
        grid=(steps,),
        in_specs=[rows, rows, pl.BlockSpec((steps, some * topk), lambda i: (0, 0))],
        out_specs=[pl.BlockSpec((n, some, cols), lambda i: (0, i, 0)) for n in sizes],
        out_shape=[jax.ShapeDtypeStruct((n, group_tok, cols), jnp.bfloat16) for n in sizes],
        compiler_params=pltpu.CompilerParams(vmem_limit_bytes=56 * MIB),
        cost_estimate=SMALL,
        name="hidden_rows",
    )(gate, up, named.reshape(steps, some * topk))


def spread(picked, got, experts):
    half = experts // 2
    held = {0: {(1 << i) >> 1: rows for i, rows in enumerate(picked)}}
    bit = half
    while bit:
        for group in list(held):
            rows = got if bit == half else swapped(held[group][bit], "expert", bit)
            held[group ^ bit] = {0: rows[:1]}
            for i in range(bit.bit_length() - 1):
                held[group ^ bit][1 << i] = rows[1 << i : 2 << i]
        bit //= 2
    return [held[m][0][0] for m in range(experts)]


def term_kernel(count, *refs):
    tokens, hidden, out_ref = refs[:count], refs[count : 2 * count], refs[-1]
    total = None
    for token_ref, hidden_ref in zip(tokens, hidden):
        one = lax.dot_general(
            token_ref[...],
            hidden_ref[...],
            (((0,), (0,)), ((), ())),
            preferred_element_type=jnp.float32,
        )
        total = one if total is None else total + one
    out_ref[...] = total.astype(jnp.bfloat16)


def terms(part, parts, tokens, hidden):
    group_tok, width = tokens[0].shape
    cols = hidden[0].shape[1] // parts
    tall = width // 8
    count = len(tokens)
    return pl.pallas_call(
        functools.partial(term_kernel, count),
        grid=(width // tall,),
        in_specs=[pl.BlockSpec((group_tok, tall), lambda i: (0, i))] * count
        + [pl.BlockSpec((group_tok, cols), lambda i: (0, part))] * count,
        out_specs=pl.BlockSpec((tall, cols), lambda i: (i, 0)),
        out_shape=jax.ShapeDtypeStruct((width, cols), jnp.bfloat16),
        compiler_params=pltpu.CompilerParams(vmem_limit_bytes=56 * MIB),
        cost_estimate=SMALL,
        name="group_terms",
    )(*tokens, *hidden)


def deriv_kernel(tokens_ref, weight_ref, out_ref):
    out_ref[...] = jnp.dot(
        tokens_ref[...], weight_ref[...], preferred_element_type=jnp.float32
    )


def deriv_of(tokens, weight):
    group_tok, width = tokens.shape
    cols = weight.shape[1]
    wide = 256 if cols % 256 == 0 else cols
    return pl.pallas_call(
        deriv_kernel,
        grid=(cols // wide,),
        in_specs=[
            pl.BlockSpec((group_tok, width), lambda i: (0, 0)),
            pl.BlockSpec((width, wide), lambda i: (0, i)),
        ],
        out_specs=pl.BlockSpec((group_tok, wide), lambda i: (0, i)),
        out_shape=jax.ShapeDtypeStruct((group_tok, cols), jnp.float32),
        compiler_params=pltpu.CompilerParams(vmem_limit_bytes=56 * MIB),
        cost_estimate=pl.CostEstimate(
            flops=2 * group_tok * width * cols,
            bytes_accessed=2 * (group_tok + cols) * width + 4 * group_tok * cols,
            transcendentals=0,
        ),
        name="hidden_deriv",
    )(tokens, weight)


def update_kernel(count, place_ref, grad_ref, momentum_ref, *refs):
    weight_refs = refs[:count]
    new_weight_ref, new_momentum_ref = refs[-2:]
    for m, weight_ref in enumerate(weight_refs):

        @pl.when(pl.program_id(0) == m)
        def _():
            grad = grad_ref[0].astype(jnp.float32)
            moment = momentum_ref[0].astype(jnp.float32)
            weight = weight_ref[...].astype(jnp.float32)
            mix = beta_first * moment + (1.0 - beta_first) * grad
            new_weight_ref[0] = weight * (1.0 - step_rate * decay_rate) - step_rate * jnp.tanh(
                mix / sign_width
            )
            new_momentum_ref[0] = (beta_second * moment + (1.0 - beta_second) * grad).astype(
                jnp.bfloat16
            )


def update(part, parts, place, grad, weights, momentum, done):
    count, rows, some = grad.shape
    wide = pl.BlockSpec((1, rows, some), lambda m, place: (0, 0, (place[0] ^ m) * parts + part))
    return pl.pallas_call(
        functools.partial(update_kernel, count),
        grid_spec=pltpu.PrefetchScalarGridSpec(
            num_scalar_prefetch=1,
            grid=(count,),
            in_specs=[pl.BlockSpec((1, rows, some), lambda m, place: (place[0] ^ m, 0, 0)), wide]
            + [pl.BlockSpec((rows, some), lambda m, place: (0, part))] * count
            + [pl.BlockSpec(memory_space=pl.ANY)] * len(done),
            out_specs=[wide, wide],
        ),
        out_shape=[
            jax.ShapeDtypeStruct(momentum.shape, jnp.float32),
            jax.ShapeDtypeStruct(momentum.shape, jnp.bfloat16),
        ],
        input_output_aliases={3 + count + i: i for i in range(len(done))},
        compiler_params=pltpu.CompilerParams(vmem_limit_bytes=56 * MIB),
        cost_estimate=SMALL,
        name="lion_step",
    )(place.reshape(1), grad, momentum, *weights, *done)


def body(out_grad, gate_saved, up_saved, routing, down_weight, momentum):
    experts = lax.axis_size("expert")
    shards = lax.axis_size("dp")
    group_tok, topk, cols = gate_saved.shape
    width = out_grad.shape[1]
    rows = momentum.shape[1]
    mine = lax.axis_index("expert")
    place = lax.axis_index("dp")
    each = range(experts)

    half = experts // 2
    others = sorted(range(2, experts, 2), key=lambda m: (bin(m).count("1"), -m))

    parts = 2 if cols % 256 == 0 else 1

    def to_owners(array, *begun):
        array = after(array.reshape(shards, rows, cols // parts), *begun)
        return lax.all_to_all(array, "dp", split_axis=0, concat_axis=0, tiled=True)

    weight = down_weight[0]
    tuned = shards == 8

    def block_for(m, begin=0, count=rows):
        return lax.dynamic_slice_in_dim(weight, (place ^ m) * rows + begin, count, axis=0)

    blocks = [swapped(out_grad, "dp", m) for m in range(0, shards, 2)]
    named = (routing ^ mine).reshape(1, group_tok * topk)
    picked = picked_rows(
        gate_saved.reshape(-1, cols), up_saved.reshape(-1, cols), named, group_tok, experts
    )
    if tuned:
        cut = rows // 2
        mixed = jnp.concatenate([block_for(4), block_for(5, 0, cut)], axis=0)
        mixed, rest, six, seven = stage(mixed, block_for(5, cut, rows - cut), block_for(6), block_for(7))
        mixed = swapped(after(mixed, blocks[1]), "dp", 4)
    blocks, picked = stage(blocks, picked)

    held = {0: placed_blocks(blocks, place // 2)}
    for m in others:
        held[m] = swapped(held[m & (m - 1)], "expert", m & -m)
    beside = {0: swapped(held[0], "dp", 1)}
    held, beside, picked = stage(held, beside, picked)
    if tuned:
        mixed, rest, six, held, beside, picked = stage(mixed, rest, six, held, beside, picked)

    last = (place & 1) != 0
    for m in others:
        beside[m] = swapped(held[m], "dp", 1)
    got = swapped(picked[-1], "expert", half)
    tokens = {0: in_order(held[0], beside[0], last).reshape(group_tok, width)}
    tokens[1] = swapped(tokens[0], "expert", 1)
    tokens, beside, got, picked = stage(tokens, beside, got, picked)
    if tuned:
        rest = swapped(rest, "dp", 4)
        six = swapped(six, "dp", 6)
        rest, six, seven, tokens, beside, got, picked = stage(
            rest, six, seven, tokens, beside, got, picked
        )

    for m in others:
        tokens[m] = in_order(held[m], beside[m], last).reshape(group_tok, width)
        tokens[m + 1] = swapped(tokens[m], "expert", 1)
    tokens = [tokens[m] for m in each]
    hidden = spread(picked, got, experts)
    if tuned:
        one, five, weight = stage(
            block_for(1), jnp.concatenate([mixed[rows:], rest], axis=0), weight
        )
        one = swapped(after(one, rest), "dp", 1)
        seven = swapped(seven, "dp", 7)
        tokens, hidden, one, five = stage(tokens, hidden, one, five)
        five = swapped(five, "dp", 1)
        first_weights, last_weights = [seven, five], []
        weights = [block_for(0), one, None, None, mixed[:rows], five, six, seven]
        for m in (2, 3):
            weights[m] = swapped(after(block_for(m), hidden), "dp", m)
            last_weights.append(weights[m])
    else:
        tokens, hidden = stage(tokens, hidden)
        every = lax.all_to_all(
            weight.reshape(shards, rows, cols), "dp", split_axis=0, concat_axis=0, tiled=True
        )
        first_weights, last_weights = [every], []
        weights = [
            lax.dynamic_index_in_dim(every, place ^ m, axis=0, keepdims=False)
            for m in range(shards)
        ]

    term = terms(0, parts, tokens, hidden)
    weight, term = stage(weight, term)
    derivs = [deriv_of(tokens[m], weight) for m in each]
    backs = [swapped(derivs[m], "expert", m) for m in each]
    grads = [to_owners(term, first_weights)]
    for part in range(1, parts):
        term = terms(part, parts, tokens, after(hidden, derivs))
        grads.append(to_owners(term, grads, last_weights, backs[half]))

    gate_saved, up_saved, _ = stage(gate_saved, up_saved, derivs)
    gate = gate_saved.astype(jnp.float32)
    up = up_saved.astype(jnp.float32)
    sigma = jax.nn.sigmoid(gate)
    deriv = jnp.zeros(gate.shape, jnp.float32)
    for m in each:
        chosen = (routing == (mine ^ m))[:, :, None]
        deriv = jnp.where(chosen, backs[m][:, None, :], deriv)
    d_up = (deriv * gate * sigma).astype(jnp.bfloat16)
    d_gate = (deriv * up * sigma * (1.0 + gate * (1.0 - sigma))).astype(jnp.bfloat16)

    done = ()
    for part in range(parts):
        done = update(part, parts, place, grads[part], weights, momentum, done)
    new_weight, new_momentum = done
    return (d_gate, d_up, new_weight, new_momentum)


def solution(mesh):
    placed = (
        P(("expert", "dp"), None),
        P("expert", None, "dp"),
        P("expert", None, "dp"),
        P("expert", None),
        P("expert", None, "dp"),
        P("expert", "dp", None),
    )
    return jax.shard_map(
        body,
        mesh=mesh,
        in_specs=placed,
        out_specs=(
            P("expert", None, "dp"),
            P("expert", None, "dp"),
            P("expert", "dp", None),
            P("expert", "dp", None),
        ),
        check_vma=False,
    )
```

```python
import functools

import jax
import jax.numpy as jnp
from jax import lax
from jax.experimental import pallas as pl
from jax.experimental.pallas import tpu as pltpu
from jax.sharding import PartitionSpec as P

beta_first = 0.9
beta_second = 0.99
step_rate = 0.01
decay_rate = 1.0
sign_width = 10.0
MIB = 1024 * 1024
SMALL = pl.CostEstimate(flops=1024, bytes_accessed=1024, transcendentals=0)


def swapped(array, axis, mask):
    if mask == 0:
        return array
    size = lax.axis_size(axis)
    return lax.ppermute(array, axis, [(i, i ^ mask) for i in range(size)])


def after(value, *others):
    return lax.optimization_barrier((value, *others))[0]


def order_kernel(place_ref, mine_ref, theirs_ref, out_ref):
    out_ref[0, place_ref[0]] = mine_ref[0]
    out_ref[0, 1 - place_ref[0]] = theirs_ref[0]


def stage(*values):
    return lax.optimization_barrier(values)


def in_order(mine, theirs, bit):
    count, some, width = mine.shape
    one = pl.BlockSpec((1, some, width), lambda i, place: (i, 0, 0))
    both = pl.pallas_call(
        order_kernel,
        grid_spec=pltpu.PrefetchScalarGridSpec(
            num_scalar_prefetch=1,
            grid=(count,),
            in_specs=[one, one],
            out_specs=pl.BlockSpec((1, 2, some, width), lambda i, place: (i, 0, 0, 0)),
        ),
        out_shape=jax.ShapeDtypeStruct((count, 2, some, width), mine.dtype),
        cost_estimate=SMALL,
        name="side_by_side",
    )(bit.astype(jnp.int32).reshape(1), mine, theirs)
    return both.reshape(2 * count, some, width)


def place_kernel(place_ref, *refs):
    for m, block_ref in enumerate(refs[:-1]):
        refs[-1][place_ref[0] ^ m] = block_ref[...]


def placed_blocks(blocks, place):
    count = len(blocks)
    return pl.pallas_call(
        place_kernel,
        grid_spec=pltpu.PrefetchScalarGridSpec(
            num_scalar_prefetch=1,
            grid=(1,),
            in_specs=[pl.BlockSpec(blocks[0].shape, lambda i, place: (0, 0))] * count,
            out_specs=pl.BlockSpec((count,) + blocks[0].shape, lambda i, place: (0, 0, 0)),
        ),
        out_shape=jax.ShapeDtypeStruct((count,) + blocks[0].shape, blocks[0].dtype),
        compiler_params=pltpu.CompilerParams(vmem_limit_bytes=56 * MIB),
        cost_estimate=SMALL,
        name="placed_blocks",
    )(place.reshape(1), *blocks)


def pick(hidden, named_ref, out_refs):
    count_rows = hidden.shape[0]
    tokens = out_refs[0].shape[1]
    topk = count_rows // tokens
    token = lax.broadcasted_iota(jnp.int32, (tokens, count_rows), 0)
    row = lax.broadcasted_iota(jnp.int32, (tokens, count_rows), 1)
    here = (row >= token * topk) & (row < token * topk + topk)
    named = named_ref[pl.ds(pl.program_id(0), 1), :]
    m = 0
    for out_ref in out_refs:
        for i in range(out_ref.shape[0]):
            chosen = jnp.where(here & (named == m), 1.0, 0.0).astype(jnp.bfloat16)
            out_ref[i] = jnp.dot(chosen, hidden, preferred_element_type=jnp.float32).astype(
                jnp.bfloat16
            )
            m += 1


def hidden_kernel(gate_ref, up_ref, named_ref, *out_refs):
    gate = gate_ref[...].astype(jnp.float32)
    up = up_ref[...].astype(jnp.float32)
    pick((gate * jax.nn.sigmoid(gate) * up).astype(jnp.bfloat16), named_ref, out_refs)


def picked_rows(gate, up, named, group_tok, experts):
    cols = gate.shape[1]
    topk = named.shape[1] // group_tok
    steps = 4
    some = group_tok // steps
    sizes = [1] + [1 << b for b in range(experts.bit_length() - 1)]
    rows = pl.BlockSpec((some * topk, cols), lambda i: (i, 0))
    return pl.pallas_call(
        hidden_kernel,
        grid=(steps,),
        in_specs=[rows, rows, pl.BlockSpec((steps, some * topk), lambda i: (0, 0))],
        out_specs=[pl.BlockSpec((n, some, cols), lambda i: (0, i, 0)) for n in sizes],
        out_shape=[jax.ShapeDtypeStruct((n, group_tok, cols), jnp.bfloat16) for n in sizes],
        compiler_params=pltpu.CompilerParams(vmem_limit_bytes=56 * MIB),
        cost_estimate=SMALL,
        name="hidden_rows",
    )(gate, up, named.reshape(steps, some * topk))


def spread(picked, got, experts):
    half = experts // 2
    held = {0: {(1 << i) >> 1: rows for i, rows in enumerate(picked)}}
    bit = half
    while bit:
        for group in list(held):
            rows = got if bit == half else swapped(held[group][bit], "expert", bit)
            held[group ^ bit] = {0: rows[:1]}
            for i in range(bit.bit_length() - 1):
                held[group ^ bit][1 << i] = rows[1 << i : 2 << i]
        bit //= 2
    return [held[m][0][0] for m in range(experts)]


def term_kernel(count, *refs):
    tokens, hidden, out_ref = refs[:count], refs[count : 2 * count], refs[-1]
    total = None
    for token_ref, hidden_ref in zip(tokens, hidden):
        one = lax.dot_general(
            token_ref[...],
            hidden_ref[...],
            (((0,), (0,)), ((), ())),
            preferred_element_type=jnp.float32,
        )
        total = one if total is None else total + one
    out_ref[...] = total.astype(jnp.bfloat16)


def terms(part, parts, tokens, hidden):
    group_tok, width = tokens[0].shape
    cols = hidden[0].shape[1] // parts
    tall = width // 8
    count = len(tokens)
    return pl.pallas_call(
        functools.partial(term_kernel, count),
        grid=(width // tall,),
        in_specs=[pl.BlockSpec((group_tok, tall), lambda i: (0, i))] * count
        + [pl.BlockSpec((group_tok, cols), lambda i: (0, part))] * count,
        out_specs=pl.BlockSpec((tall, cols), lambda i: (i, 0)),
        out_shape=jax.ShapeDtypeStruct((width, cols), jnp.bfloat16),
        compiler_params=pltpu.CompilerParams(vmem_limit_bytes=56 * MIB),
        cost_estimate=SMALL,
        name="group_terms",
    )(*tokens, *hidden)


def deriv_kernel(tokens_ref, weight_ref, out_ref):
    out_ref[...] = jnp.dot(
        tokens_ref[...], weight_ref[...], preferred_element_type=jnp.float32
    )


def deriv_of(tokens, weight):
    group_tok, width = tokens.shape
    cols = weight.shape[1]
    wide = 256 if cols % 256 == 0 else cols
    return pl.pallas_call(
        deriv_kernel,
        grid=(cols // wide,),
        in_specs=[
            pl.BlockSpec((group_tok, width), lambda i: (0, 0)),
            pl.BlockSpec((width, wide), lambda i: (0, i)),
        ],
        out_specs=pl.BlockSpec((group_tok, wide), lambda i: (0, i)),
        out_shape=jax.ShapeDtypeStruct((group_tok, cols), jnp.float32),
        compiler_params=pltpu.CompilerParams(vmem_limit_bytes=56 * MIB),
        cost_estimate=pl.CostEstimate(
            flops=2 * group_tok * width * cols,
            bytes_accessed=2 * (group_tok + cols) * width + 4 * group_tok * cols,
            transcendentals=0,
        ),
        name="hidden_deriv",
    )(tokens, weight)


def update_kernel(count, place_ref, grad_ref, momentum_ref, *refs):
    weight_refs = refs[:count]
    new_weight_ref, new_momentum_ref = refs[-2:]
    for m, weight_ref in enumerate(weight_refs):

        @pl.when(pl.program_id(0) == m)
        def _():
            grad = grad_ref[0].astype(jnp.float32)
            moment = momentum_ref[0].astype(jnp.float32)
            weight = weight_ref[...].astype(jnp.float32)
            mix = beta_first * moment + (1.0 - beta_first) * grad
            new_weight_ref[0] = weight * (1.0 - step_rate * decay_rate) - step_rate * jnp.tanh(
                mix / sign_width
            )
            new_momentum_ref[0] = (beta_second * moment + (1.0 - beta_second) * grad).astype(
                jnp.bfloat16
            )


def update(part, parts, place, grad, weights, momentum, done):
    count, rows, some = grad.shape
    wide = pl.BlockSpec((1, rows, some), lambda m, place: (0, 0, (place[0] ^ m) * parts + part))
    return pl.pallas_call(
        functools.partial(update_kernel, count),
        grid_spec=pltpu.PrefetchScalarGridSpec(
            num_scalar_prefetch=1,
            grid=(count,),
            in_specs=[pl.BlockSpec((1, rows, some), lambda m, place: (place[0] ^ m, 0, 0)), wide]
            + [pl.BlockSpec((rows, some), lambda m, place: (0, part))] * count
            + [pl.BlockSpec(memory_space=pl.ANY)] * len(done),
            out_specs=[wide, wide],
        ),
        out_shape=[
            jax.ShapeDtypeStruct(momentum.shape, jnp.float32),
            jax.ShapeDtypeStruct(momentum.shape, jnp.bfloat16),
        ],
        input_output_aliases={3 + count + i: i for i in range(len(done))},
        compiler_params=pltpu.CompilerParams(vmem_limit_bytes=56 * MIB),
        cost_estimate=SMALL,
        name="lion_step",
    )(place.reshape(1), grad, momentum, *weights, *done)


def body(out_grad, gate_saved, up_saved, routing, down_weight, momentum):
    experts = lax.axis_size("expert")
    shards = lax.axis_size("dp")
    group_tok, topk, cols = gate_saved.shape
    width = out_grad.shape[1]
    rows = momentum.shape[1]
    mine = lax.axis_index("expert")
    place = lax.axis_index("dp")
    each = range(experts)

    half = experts // 2
    others = sorted(range(2, experts, 2), key=lambda m: (bin(m).count("1"), -m))

    parts = 2 if cols % 256 == 0 else 1

    def to_owners(array, *begun):
        array = after(array.reshape(shards, rows, cols // parts), *begun)
        return lax.all_to_all(array, "dp", split_axis=0, concat_axis=0, tiled=True)

    weight = down_weight[0]
    tuned = shards == 8

    def sent(m, *begun):
        return swapped(after(cuts[m], *begun), "dp", m)

    blocks = [swapped(out_grad, "dp", m) for m in range(0, shards, 2)]
    named = (routing ^ mine).reshape(1, group_tok * topk)
    picked = picked_rows(
        gate_saved.reshape(-1, cols), up_saved.reshape(-1, cols), named, group_tok, experts
    )
    cuts = [
        lax.dynamic_slice_in_dim(weight, (place ^ m) * rows, rows, axis=0)
        for m in range(shards if tuned else 1)
    ]
    blocks, picked, cuts = stage(blocks, picked, cuts)

    held = placed_blocks(blocks, place // 2)
    beside = swapped(held, "dp", 1)
    got = swapped(picked[-1], "expert", half)
    weights = {0: cuts[0]}
    if tuned:
        weights[4] = sent(4)
    held, beside, got, picked, weights, cuts = stage(held, beside, got, picked, weights, cuts)

    tokens = {0: in_order(held, beside, (place & 1) != 0).reshape(group_tok, width)}
    for m in others:
        tokens[m] = swapped(tokens[m & (m - 1)], "expert", m & -m)
    tokens[1] = swapped(tokens[0], "expert", 1)
    hidden = spread(picked, got, experts)
    if tuned:
        for m in (6, 5, 1):
            weights[m] = sent(m)
    tokens, hidden, weights, cuts = stage(tokens, hidden, weights, cuts)

    for m in others:
        tokens[m + 1] = swapped(tokens[m], "expert", 1)
    tokens = [tokens[m] for m in each]
    if tuned:
        for m in (7, 2, 3):
            weights[m] = sent(m)
        first_weights, last_weights = weights[7], (weights[2], weights[3])
    else:
        every = lax.all_to_all(
            weight.reshape(shards, rows, cols), "dp", split_axis=0, concat_axis=0, tiled=True
        )
        first_weights, last_weights = every, ()
        for m in range(1, shards):
            weights[m] = lax.dynamic_index_in_dim(every, place ^ m, axis=0, keepdims=False)

    term = terms(0, parts, tokens, hidden)
    weight, term = stage(weight, term)
    derivs = [deriv_of(tokens[m], weight) for m in each]
    backs = [swapped(derivs[m], "expert", m) for m in each]
    grads = [to_owners(term, first_weights)]
    for part in range(1, parts):
        term = terms(part, parts, tokens, after(hidden, derivs))
        grads.append(to_owners(term, grads, last_weights))

    gate_saved, up_saved, _ = stage(gate_saved, up_saved, derivs)
    gate = gate_saved.astype(jnp.float32)
    up = up_saved.astype(jnp.float32)
    sigma = jax.nn.sigmoid(gate)
    deriv = jnp.zeros(gate.shape, jnp.float32)
    for m in each:
        chosen = (routing == (mine ^ m))[:, :, None]
        deriv = jnp.where(chosen, backs[m][:, None, :], deriv)
    d_up = (deriv * gate * sigma).astype(jnp.bfloat16)
    d_gate = (deriv * up * sigma * (1.0 + gate * (1.0 - sigma))).astype(jnp.bfloat16)

    done = ()
    for part in range(parts):
        done = update(
            part, parts, place, grads[part], [weights[m] for m in range(shards)], momentum, done
        )
    new_weight, new_momentum = done
    return (d_gate, d_up, new_weight, new_momentum)


def solution(mesh):
    placed = (
        P(("expert", "dp"), None),
        P("expert", None, "dp"),
        P("expert", None, "dp"),
        P("expert", None),
        P("expert", None, "dp"),
        P("expert", "dp", None),
    )
    return jax.shard_map(
        body,
        mesh=mesh,
        in_specs=placed,
        out_specs=(
            P("expert", None, "dp"),
            P("expert", None, "dp"),
            P("expert", "dp", None),
            P("expert", "dp", None),
        ),
        check_vma=False,
    )
```

```python
import functools

import jax
import jax.numpy as jnp
from jax import lax
from jax.experimental import pallas as pl
from jax.experimental.pallas import tpu as pltpu
from jax.sharding import PartitionSpec as P

beta_first = 0.9
beta_second = 0.99
step_rate = 0.01
decay_rate = 1.0
sign_width = 10.0
MIB = 1024 * 1024
SMALL = pl.CostEstimate(flops=1024, bytes_accessed=1024, transcendentals=0)


def swapped(array, axis, mask):
    if mask == 0:
        return array
    size = lax.axis_size(axis)
    return lax.ppermute(array, axis, [(i, i ^ mask) for i in range(size)])


def after(value, *others):
    return lax.optimization_barrier((value, *others))[0]


def order_kernel(place_ref, mine_ref, theirs_ref, out_ref):
    out_ref[0, place_ref[0]] = mine_ref[0]
    out_ref[0, 1 - place_ref[0]] = theirs_ref[0]


def stage(*values):
    return lax.optimization_barrier(values)


def in_order(mine, theirs, bit):
    count, some, width = mine.shape
    one = pl.BlockSpec((1, some, width), lambda i, place: (i, 0, 0))
    both = pl.pallas_call(
        order_kernel,
        grid_spec=pltpu.PrefetchScalarGridSpec(
            num_scalar_prefetch=1,
            grid=(count,),
            in_specs=[one, one],
            out_specs=pl.BlockSpec((1, 2, some, width), lambda i, place: (i, 0, 0, 0)),
        ),
        out_shape=jax.ShapeDtypeStruct((count, 2, some, width), mine.dtype),
        cost_estimate=SMALL,
        name="side_by_side",
    )(bit.astype(jnp.int32).reshape(1), mine, theirs)
    return both.reshape(2 * count, some, width)


def place_kernel(place_ref, *refs):
    for m, block_ref in enumerate(refs[:-1]):
        refs[-1][place_ref[0] ^ m] = block_ref[...]


def placed_blocks(blocks, place):
    count = len(blocks)
    return pl.pallas_call(
        place_kernel,
        grid_spec=pltpu.PrefetchScalarGridSpec(
            num_scalar_prefetch=1,
            grid=(1,),
            in_specs=[pl.BlockSpec(blocks[0].shape, lambda i, place: (0, 0))] * count,
            out_specs=pl.BlockSpec((count,) + blocks[0].shape, lambda i, place: (0, 0, 0)),
        ),
        out_shape=jax.ShapeDtypeStruct((count,) + blocks[0].shape, blocks[0].dtype),
        compiler_params=pltpu.CompilerParams(vmem_limit_bytes=56 * MIB),
        cost_estimate=SMALL,
        name="placed_blocks",
    )(place.reshape(1), *blocks)


def pick(hidden, named_ref, out_refs):
    count_rows = hidden.shape[0]
    tokens = out_refs[0].shape[1]
    topk = count_rows // tokens
    token = lax.broadcasted_iota(jnp.int32, (tokens, count_rows), 0)
    row = lax.broadcasted_iota(jnp.int32, (tokens, count_rows), 1)
    here = (row >= token * topk) & (row < token * topk + topk)
    named = named_ref[pl.ds(pl.program_id(0), 1), :]
    m = 0
    for out_ref in out_refs:
        for i in range(out_ref.shape[0]):
            chosen = jnp.where(here & (named == m), 1.0, 0.0).astype(jnp.bfloat16)
            out_ref[i] = jnp.dot(chosen, hidden, preferred_element_type=jnp.float32).astype(
                jnp.bfloat16
            )
            m += 1


def hidden_kernel(gate_ref, up_ref, named_ref, *out_refs):
    gate = gate_ref[...].astype(jnp.float32)
    up = up_ref[...].astype(jnp.float32)
    pick((gate * jax.nn.sigmoid(gate) * up).astype(jnp.bfloat16), named_ref, out_refs)


def picked_rows(gate, up, named, group_tok, experts):
    cols = gate.shape[1]
    topk = named.shape[1] // group_tok
    steps = 4
    some = group_tok // steps
    sizes = [1] + [1 << b for b in range(experts.bit_length() - 1)]
    rows = pl.BlockSpec((some * topk, cols), lambda i: (i, 0))
    return pl.pallas_call(
        hidden_kernel,
        grid=(steps,),
        in_specs=[rows, rows, pl.BlockSpec((steps, some * topk), lambda i: (0, 0))],
        out_specs=[pl.BlockSpec((n, some, cols), lambda i: (0, i, 0)) for n in sizes],
        out_shape=[jax.ShapeDtypeStruct((n, group_tok, cols), jnp.bfloat16) for n in sizes],
        compiler_params=pltpu.CompilerParams(vmem_limit_bytes=56 * MIB),
        cost_estimate=SMALL,
        name="hidden_rows",
    )(gate, up, named.reshape(steps, some * topk))


def spread(picked, got, experts):
    half = experts // 2
    held = {0: {(1 << i) >> 1: rows for i, rows in enumerate(picked)}}
    bit = half
    while bit:
        for group in list(held):
            rows = got if bit == half else swapped(held[group][bit], "expert", bit)
            held[group ^ bit] = {0: rows[:1]}
            for i in range(bit.bit_length() - 1):
                held[group ^ bit][1 << i] = rows[1 << i : 2 << i]
        bit //= 2
    return [held[m][0][0] for m in range(experts)]


def term_kernel(count, owners_ref, *refs):
    tokens, hidden, outs = refs[:count], refs[count : 2 * count], refs[2 * count :]
    total = None
    for token_ref, hidden_ref in zip(tokens, hidden):
        one = lax.dot_general(
            token_ref[...],
            hidden_ref[...],
            (((0,), (0,)), ((), ())),
            preferred_element_type=jnp.float32,
        )
        total = one if total is None else total + one
    total = total.astype(jnp.bfloat16)
    for i, out_ref in enumerate(outs):

        @pl.when(pl.program_id(0) == i)
        def _():
            out_ref[...] = total


def terms(tokens, hidden, tall, owners):
    group_tok, width = tokens[0].shape
    cols = hidden[0].shape[1]
    count, steps = len(tokens), len(owners)
    return pl.pallas_call(
        functools.partial(term_kernel, count),
        grid_spec=pltpu.PrefetchScalarGridSpec(
            num_scalar_prefetch=1,
            grid=(steps,),
            in_specs=[pl.BlockSpec((group_tok, tall), lambda i, owners: (0, owners[i]))] * count
            + [pl.BlockSpec((group_tok, cols), lambda i, owners: (0, 0))] * count,
            out_specs=[pl.BlockSpec((tall, cols), lambda i, owners: (0, 0))] * steps,
        ),
        out_shape=[jax.ShapeDtypeStruct((tall, cols), jnp.bfloat16)] * steps,
        compiler_params=pltpu.CompilerParams(vmem_limit_bytes=56 * MIB),
        cost_estimate=SMALL,
        name="group_terms",
    )(jnp.stack(owners), *tokens, *hidden)


def deriv_kernel(tokens_ref, weight_ref, out_ref):
    out_ref[...] = jnp.dot(
        tokens_ref[...], weight_ref[...], preferred_element_type=jnp.float32
    )


def deriv_of(tokens, weight):
    group_tok, width = tokens.shape
    cols = weight.shape[1]
    wide = 256 if cols % 256 == 0 else cols
    return pl.pallas_call(
        deriv_kernel,
        grid=(cols // wide,),
        in_specs=[
            pl.BlockSpec((group_tok, width), lambda i: (0, 0)),
            pl.BlockSpec((width, wide), lambda i: (0, i)),
        ],
        out_specs=pl.BlockSpec((group_tok, wide), lambda i: (0, i)),
        out_shape=jax.ShapeDtypeStruct((group_tok, cols), jnp.float32),
        compiler_params=pltpu.CompilerParams(vmem_limit_bytes=56 * MIB),
        cost_estimate=pl.CostEstimate(
            flops=2 * group_tok * width * cols,
            bytes_accessed=2 * (group_tok + cols) * width + 4 * group_tok * cols,
            transcendentals=0,
        ),
        name="hidden_deriv",
    )(tokens, weight)


def update_kernel(count, sources_ref, momentum_ref, *refs):
    new_weight_ref, new_momentum_ref = refs[-2:]
    for i in range(count):

        @pl.when(pl.program_id(0) == i)
        def _():
            grad = refs[i][...].astype(jnp.float32)
            moment = momentum_ref[0].astype(jnp.float32)
            weight = refs[count + i][...].astype(jnp.float32)
            mix = beta_first * moment + (1.0 - beta_first) * grad
            new_weight_ref[0] = weight * (1.0 - step_rate * decay_rate) - step_rate * jnp.tanh(
                mix / sign_width
            )
            new_momentum_ref[0] = (beta_second * moment + (1.0 - beta_second) * grad).astype(
                jnp.bfloat16
            )


def update(sources, grads, weights, momentum, done):
    count = len(grads)
    rows, cols = grads[0].shape
    wide = pl.BlockSpec((1, rows, cols), lambda i, sources: (0, 0, sources[i]))
    return pl.pallas_call(
        functools.partial(update_kernel, count),
        grid_spec=pltpu.PrefetchScalarGridSpec(
            num_scalar_prefetch=1,
            grid=(count,),
            in_specs=[wide]
            + [pl.BlockSpec((rows, cols), lambda i, sources: (0, 0))] * (2 * count)
            + [pl.BlockSpec(memory_space=pl.ANY)] * len(done),
            out_specs=[wide, wide],
        ),
        out_shape=[
            jax.ShapeDtypeStruct(momentum.shape, jnp.float32),
            jax.ShapeDtypeStruct(momentum.shape, jnp.bfloat16),
        ],
        input_output_aliases={2 + 2 * count + i: i for i in range(len(done))},
        compiler_params=pltpu.CompilerParams(vmem_limit_bytes=56 * MIB),
        cost_estimate=SMALL,
        name="lion_step",
    )(jnp.stack(sources), momentum, *grads, *weights, *done)


def body(out_grad, gate_saved, up_saved, routing, down_weight, momentum):
    experts = lax.axis_size("expert")
    shards = lax.axis_size("dp")
    group_tok, topk, cols = gate_saved.shape
    width = out_grad.shape[1]
    rows = momentum.shape[1]
    mine = lax.axis_index("expert")
    place = lax.axis_index("dp")
    each = range(experts)

    half = experts // 2
    others = sorted(range(2, experts, 2), key=lambda m: (bin(m).count("1"), -m))

    weight = down_weight[0]
    tuned = shards == 8

    def sent(m, *begun):
        return swapped(after(cuts[m], *begun), "dp", m)

    blocks = [swapped(out_grad, "dp", m) for m in range(0, shards, 2)]
    named = (routing ^ mine).reshape(1, group_tok * topk)
    picked = picked_rows(
        gate_saved.reshape(-1, cols), up_saved.reshape(-1, cols), named, group_tok, experts
    )
    cuts = [
        lax.dynamic_slice_in_dim(weight, (place ^ m) * rows, rows, axis=0)
        for m in range(shards if tuned else 1)
    ]
    blocks, picked, cuts = stage(blocks, picked, cuts)

    held = {0: placed_blocks(blocks, place // 2)}
    for m in others:
        held[m] = swapped(held[m & (m - 1)], "expert", m & -m)
    beside = {0: swapped(held[0], "dp", 1)}
    weights = {0: cuts[0]}
    if tuned:
        for m in (4, 6):
            weights[m] = sent(m)
    held, beside, picked, weights, cuts = stage(held, beside, picked, weights, cuts)

    last = (place & 1) != 0
    for m in others:
        beside[m] = swapped(held[m], "dp", 1)
    got = swapped(picked[-1], "expert", half)
    tokens = {0: in_order(held[0], beside[0], last).reshape(group_tok, width)}
    tokens[1] = swapped(tokens[0], "expert", 1)
    if tuned:
        weights[2] = sent(2)
    tokens, beside, got, picked, weights, cuts = stage(
        tokens, beside, got, picked, weights, cuts
    )

    for m in others:
        tokens[m] = in_order(held[m], beside[m], last).reshape(group_tok, width)
        tokens[m + 1] = swapped(tokens[m], "expert", 1)
    tokens = [tokens[m] for m in each]
    hidden = spread(picked, got, experts)
    if tuned:
        for m in (5, 1):
            weights[m] = sent(m)
    tokens, hidden, cuts = stage(tokens, hidden, cuts)

    if tuned:
        early, late = (4, 6, 5, 7), (2, 3, 1, 0)
        grads = {}
        some = terms(tokens, hidden, rows, [place ^ m for m in early])
        for m in (7, 3):
            weights[m] = sent(m, *hidden)
        for m, term in zip(early, some):
            grads[m] = swapped(term, "dp", m)
        others_hidden = after(hidden, some, weights[5], weights[1])
        some = terms(tokens, others_hidden, rows, [place ^ m for m in late])
        for m, term in zip(late, some):
            grads[m] = swapped(term, "dp", m)
        batches = (early, late)
    else:
        tall = width // 8
        some = terms(tokens, hidden, tall, [jnp.int32(i) for i in range(8)])
        arrived = [
            lax.all_to_all(
                array.reshape(shards, rows, cols), "dp", split_axis=0, concat_axis=0, tiled=True
            )
            for array in (weight, jnp.concatenate(some, axis=0))
        ]
        weights, grads = [
            [
                lax.dynamic_index_in_dim(array, place ^ m, axis=0, keepdims=False)
                for m in range(shards)
            ]
            for array in arrived
        ]
        batches = (range(shards),)
    weight, _ = stage(weight, some)
    derivs = [deriv_of(tokens[m], weight) for m in each]
    backs = [swapped(derivs[m], "expert", m) for m in each]
    gate_saved, up_saved, _ = stage(gate_saved, up_saved, derivs)
    gate = gate_saved.astype(jnp.float32)
    up = up_saved.astype(jnp.float32)
    sigma = jax.nn.sigmoid(gate)
    deriv = jnp.zeros(gate.shape, jnp.float32)
    for m in each:
        chosen = (routing == (mine ^ m))[:, :, None]
        deriv = jnp.where(chosen, backs[m][:, None, :], deriv)
    d_up = (deriv * gate * sigma).astype(jnp.bfloat16)
    d_gate = (deriv * up * sigma * (1.0 + gate * (1.0 - sigma))).astype(jnp.bfloat16)

    done = ()
    for batch in batches:
        done = update(
            [place ^ m for m in batch],
            [grads[m] for m in batch],
            [weights[m] for m in batch],
            momentum,
            done,
        )
    new_weight, new_momentum = done
    return (d_gate, d_up, new_weight, new_momentum)


def solution(mesh):
    placed = (
        P(("expert", "dp"), None),
        P("expert", None, "dp"),
        P("expert", None, "dp"),
        P("expert", None),
        P("expert", None, "dp"),
        P("expert", "dp", None),
    )
    return jax.shard_map(
        body,
        mesh=mesh,
        in_specs=placed,
        out_specs=(
            P("expert", None, "dp"),
            P("expert", None, "dp"),
            P("expert", "dp", None),
            P("expert", "dp", None),
        ),
        check_vma=False,
    )
```

```python
import functools

import jax
import jax.numpy as jnp
from jax import lax
from jax.experimental import pallas as pl
from jax.experimental.pallas import tpu as pltpu
from jax.sharding import PartitionSpec as P

beta_first = 0.9
beta_second = 0.99
step_rate = 0.01
decay_rate = 1.0
sign_width = 10.0
MIB = 1024 * 1024
SMALL = pl.CostEstimate(flops=1024, bytes_accessed=1024, transcendentals=0)


def swapped(array, axis, mask):
    if mask == 0:
        return array
    size = lax.axis_size(axis)
    return lax.ppermute(array, axis, [(i, i ^ mask) for i in range(size)])


def after(value, *others):
    return lax.optimization_barrier((value, *others))[0]


def order_kernel(place_ref, mine_ref, theirs_ref, out_ref):
    out_ref[0, place_ref[0]] = mine_ref[0]
    out_ref[0, 1 - place_ref[0]] = theirs_ref[0]


def stage(*values):
    return lax.optimization_barrier(values)


def in_order(mine, theirs, bit):
    count, some, width = mine.shape
    one = pl.BlockSpec((1, some, width), lambda i, place: (i, 0, 0))
    both = pl.pallas_call(
        order_kernel,
        grid_spec=pltpu.PrefetchScalarGridSpec(
            num_scalar_prefetch=1,
            grid=(count,),
            in_specs=[one, one],
            out_specs=pl.BlockSpec((1, 2, some, width), lambda i, place: (i, 0, 0, 0)),
        ),
        out_shape=jax.ShapeDtypeStruct((count, 2, some, width), mine.dtype),
        cost_estimate=SMALL,
        name="side_by_side",
    )(bit.astype(jnp.int32).reshape(1), mine, theirs)
    return both.reshape(2 * count, some, width)


def place_kernel(place_ref, *refs):
    for m, block_ref in enumerate(refs[:-1]):
        refs[-1][place_ref[0] ^ m] = block_ref[...]


def placed_blocks(blocks, place):
    count = len(blocks)
    return pl.pallas_call(
        place_kernel,
        grid_spec=pltpu.PrefetchScalarGridSpec(
            num_scalar_prefetch=1,
            grid=(1,),
            in_specs=[pl.BlockSpec(blocks[0].shape, lambda i, place: (0, 0))] * count,
            out_specs=pl.BlockSpec((count,) + blocks[0].shape, lambda i, place: (0, 0, 0)),
        ),
        out_shape=jax.ShapeDtypeStruct((count,) + blocks[0].shape, blocks[0].dtype),
        compiler_params=pltpu.CompilerParams(vmem_limit_bytes=56 * MIB),
        cost_estimate=SMALL,
        name="placed_blocks",
    )(place.reshape(1), *blocks)


def pick(hidden, named, out_refs):
    count_rows = hidden.shape[0]
    tokens = out_refs[0].shape[1]
    topk = count_rows // tokens
    token = lax.broadcasted_iota(jnp.int32, (tokens, count_rows), 0)
    row = lax.broadcasted_iota(jnp.int32, (tokens, count_rows), 1)
    here = (row >= token * topk) & (row < token * topk + topk)
    m = 0
    for out_ref in out_refs:
        for i in range(out_ref.shape[0]):
            chosen = jnp.where(here & (named == m), 1.0, 0.0).astype(jnp.bfloat16)
            out_ref[i] = jnp.dot(chosen, hidden, preferred_element_type=jnp.float32).astype(
                jnp.bfloat16
            )
            m += 1


def hidden_kernel(place_ref, gate_ref, up_ref, named_ref, twice_ref, *out_refs):
    gate = gate_ref[...].astype(jnp.float32)
    up = up_ref[...].astype(jnp.float32)
    hidden = (gate * jax.nn.sigmoid(gate) * up).astype(jnp.bfloat16)
    twice_ref[0] = hidden
    twice_ref[1] = hidden
    pick(hidden, named_ref[pl.ds(pl.program_id(0), 1), :], out_refs)


def pick_kernel(place_ref, hidden_ref, named_ref, *out_refs):
    pick(hidden_ref[0], named_ref[pl.ds(pl.program_id(0), 1), :], out_refs)


def picked_rows(arrays, named, group_tok, experts, which):
    cols = arrays[0].shape[-1]
    topk = named.shape[1] // group_tok
    steps = 4
    some = group_tok // steps
    fresh = len(arrays) == 2
    sizes = [1] + [1 << b for b in range(experts.bit_length() - 1)]
    out_shape = [jax.ShapeDtypeStruct((n, group_tok, cols), jnp.bfloat16) for n in sizes]
    out_specs = [pl.BlockSpec((n, some, cols), lambda i, which: (0, i, 0)) for n in sizes]
    if fresh:
        in_specs = [pl.BlockSpec((some * topk, cols), lambda i, which: (i, 0))] * 2
        out_shape = [
            jax.ShapeDtypeStruct((2, group_tok * topk, cols), jnp.bfloat16)
        ] + out_shape
        out_specs = [pl.BlockSpec((2, some * topk, cols), lambda i, which: (0, i, 0))] + out_specs
    else:
        in_specs = [pl.BlockSpec((1, some * topk, cols), lambda i, which: (which[0], i, 0))]
    return pl.pallas_call(
        hidden_kernel if fresh else pick_kernel,
        grid_spec=pltpu.PrefetchScalarGridSpec(
            num_scalar_prefetch=1,
            grid=(steps,),
            in_specs=in_specs + [pl.BlockSpec((steps, some * topk), lambda i, which: (0, 0))],
            out_specs=out_specs,
        ),
        out_shape=out_shape,
        compiler_params=pltpu.CompilerParams(vmem_limit_bytes=56 * MIB),
        cost_estimate=SMALL,
        name="hidden_rows",
    )(which.reshape(1), *arrays, named.reshape(steps, some * topk))


def spread(picked, got, experts):
    half = experts // 2
    held = {0: {(1 << i) >> 1: rows for i, rows in enumerate(picked)}}
    bit = half
    while bit:
        for group in list(held):
            rows = got if bit == half else swapped(held[group][bit], "expert", bit)
            held[group ^ bit] = {0: rows[:1]}
            for i in range(bit.bit_length() - 1):
                held[group ^ bit][1 << i] = rows[1 << i : 2 << i]
        bit //= 2
    return [held[m][0][0] for m in range(experts)]


def term_kernel(count, place_ref, *refs):
    tokens, hidden, outs = refs[:count], refs[count : 2 * count], refs[2 * count :]
    total = None
    for token_ref, hidden_ref in zip(tokens, hidden):
        one = lax.dot_general(
            token_ref[...],
            hidden_ref[...],
            (((0,), (0,)), ((), ())),
            preferred_element_type=jnp.float32,
        )
        total = one if total is None else total + one
    total = total.astype(jnp.bfloat16)
    for m, out_ref in enumerate(outs):

        @pl.when(pl.program_id(0) == m)
        def _():
            out_ref[...] = total


def terms(tokens, hidden, tall, steps, block_of, place):
    group_tok, width = tokens[0].shape
    cols = hidden[0].shape[1]
    count = len(tokens)
    return pl.pallas_call(
        functools.partial(term_kernel, count),
        grid_spec=pltpu.PrefetchScalarGridSpec(
            num_scalar_prefetch=1,
            grid=(steps,),
            in_specs=[
                pl.BlockSpec((group_tok, tall), lambda m, place: (0, block_of(place[0], m)))
            ]
            * count
            + [pl.BlockSpec((group_tok, cols), lambda m, place: (0, 0))] * count,
            out_specs=[pl.BlockSpec((tall, cols), lambda m, place: (0, 0))] * steps,
        ),
        out_shape=[jax.ShapeDtypeStruct((tall, cols), jnp.bfloat16)] * steps,
        compiler_params=pltpu.CompilerParams(vmem_limit_bytes=56 * MIB),
        cost_estimate=SMALL,
        name="group_terms",
    )(place.reshape(1), *tokens, *hidden)


def deriv_kernel(tokens_ref, weight_ref, out_ref):
    out_ref[...] = jnp.dot(
        tokens_ref[...], weight_ref[...], preferred_element_type=jnp.float32
    )


def deriv_of(tokens, weight):
    group_tok, width = tokens.shape
    cols = weight.shape[1]
    wide = 256 if cols % 256 == 0 else cols
    return pl.pallas_call(
        deriv_kernel,
        grid=(cols // wide,),
        in_specs=[
            pl.BlockSpec((group_tok, width), lambda i: (0, 0)),
            pl.BlockSpec((width, wide), lambda i: (0, i)),
        ],
        out_specs=pl.BlockSpec((group_tok, wide), lambda i: (0, i)),
        out_shape=jax.ShapeDtypeStruct((group_tok, cols), jnp.float32),
        compiler_params=pltpu.CompilerParams(vmem_limit_bytes=56 * MIB),
        cost_estimate=SMALL,
        name="hidden_deriv",
    )(tokens, weight)


def update_kernel(count, place_ref, weight_ref, momentum_ref, *refs):
    grad_refs = refs[:count]
    new_weight_ref, new_momentum_ref = refs[-2:]
    for m, grad_ref in enumerate(grad_refs):

        @pl.when(pl.program_id(0) == m)
        def _():
            grad = grad_ref[...].astype(jnp.float32)
            moment = momentum_ref[0].astype(jnp.float32)
            weight = weight_ref[0].astype(jnp.float32)
            mix = beta_first * moment + (1.0 - beta_first) * grad
            new_weight_ref[0] = weight * (1.0 - step_rate * decay_rate) - step_rate * jnp.tanh(
                mix / sign_width
            )
            new_momentum_ref[0] = (beta_second * moment + (1.0 - beta_second) * grad).astype(
                jnp.bfloat16
            )


def update(part, place, grads, weight, momentum, done):
    _, rows, some = weight.shape
    count = len(grads)
    parts = grads[0].shape[1] // some
    wide = pl.BlockSpec((1, rows, some), lambda m, place: (0, 0, (place[0] ^ m) * parts + part))
    return pl.pallas_call(
        functools.partial(update_kernel, count),
        grid_spec=pltpu.PrefetchScalarGridSpec(
            num_scalar_prefetch=1,
            grid=(count,),
            in_specs=[pl.BlockSpec((1, rows, some), lambda m, place: (place[0] ^ m, 0, 0)), wide]
            + [pl.BlockSpec((rows, some), lambda m, place: (0, part))] * count
            + [pl.BlockSpec(memory_space=pl.ANY)] * len(done),
            out_specs=[wide, wide],
        ),
        out_shape=[
            jax.ShapeDtypeStruct(momentum.shape, jnp.float32),
            jax.ShapeDtypeStruct(momentum.shape, jnp.bfloat16),
        ],
        input_output_aliases={3 + count + i: i for i in range(len(done))},
        compiler_params=pltpu.CompilerParams(vmem_limit_bytes=56 * MIB),
        cost_estimate=SMALL,
        name="lion_step",
    )(place.reshape(1), weight, momentum, *grads, *done)


def body(out_grad, gate_saved, up_saved, routing, down_weight, momentum):
    experts = lax.axis_size("expert")
    shards = lax.axis_size("dp")
    group_tok, topk, cols = gate_saved.shape
    width = out_grad.shape[1]
    rows = momentum.shape[1]
    mine = lax.axis_index("expert")
    place = lax.axis_index("dp")
    span = shards // 2
    each = range(experts)

    half = experts // 2
    others = sorted(range(2, experts, 2), key=lambda m: (bin(m).count("1"), -m))

    blocks = [swapped(out_grad, "dp", m) for m in range(0, shards, 2)]
    named = (routing ^ mine).reshape(1, group_tok * topk)
    upper = place // span
    twice, *own_picked = picked_rows(
        [gate_saved.reshape(-1, cols), up_saved.reshape(-1, cols)],
        named,
        group_tok,
        experts,
        upper,
    )
    blocks, twice, own_picked = stage(blocks, twice, own_picked)

    pairs = [[i, i + span] for i in range(span)]
    other_twice = lax.all_to_all(
        twice, "dp", split_axis=0, concat_axis=0, tiled=True, axis_index_groups=pairs
    )

    held = {0: placed_blocks(blocks, place // 2)}
    for m in others:
        held[m] = swapped(held[m & (m - 1)], "expert", m & -m)
    beside = {0: swapped(held[0], "dp", 1)}
    held, beside, own_picked = stage(held, beside, own_picked)

    last = (place & 1) != 0
    for m in others:
        beside[m] = swapped(held[m], "dp", 1)
    own_got = swapped(own_picked[-1], "expert", half)
    tokens = {}
    for m in [0] + others:
        tokens[m] = in_order(held[m], beside[m], last).reshape(group_tok, width)
        tokens[m + 1] = swapped(tokens[m], "expert", 1)
    tokens = [tokens[m] for m in each]
    own_rows = spread(own_picked, own_got, experts)
    tokens, own_rows, other_twice = stage(tokens, own_rows, other_twice)

    other_picked = picked_rows([other_twice], named, group_tok, experts, 1 - upper)
    other_got = swapped(other_picked[-1], "expert", half)

    def shard_terms(hidden_rows):
        if rows % 128 == 0:
            return terms(tokens, hidden_rows, rows, span, lambda place, m: place ^ m, place)
        tall = width // 8
        total = terms(
            tokens, hidden_rows, tall, 4, lambda place, m: place // span * 4 + m, place
        )
        total = jnp.concatenate(total, axis=0)
        return [
            lax.dynamic_slice_in_dim(total, (place % span ^ m) * rows, rows, axis=0)
            for m in range(span)
        ]

    own_terms = shard_terms(own_rows)
    weight, own_terms = stage(down_weight[0], own_terms)
    derivs = [deriv_of(tokens[m], weight) for m in each]

    other_got, other_picked, derivs = stage(other_got, other_picked, derivs)
    other_rows = spread(other_picked, other_got, experts)
    other_terms = shard_terms(other_rows)

    parts = 2 if cols % 256 == 0 else 1
    pieces = jnp.split(down_weight.reshape(shards, rows, cols), parts, axis=2)
    weights = []
    for part, piece in enumerate(pieces):
        begun = [other_twice] if part == 0 else [weights[-1], other_terms]
        weights.append(
            lax.all_to_all(after(piece, *begun), "dp", split_axis=0, concat_axis=0, tiled=True)
        )

    other_terms = after(other_terms, weights[0])
    own_grads = [swapped(own_terms[m], "dp", m) for m in range(span)]
    other_grads = [swapped(other_terms[m], "dp", m) for m in range(span)]

    gate_saved, up_saved, _ = stage(gate_saved, up_saved, derivs)
    gate = gate_saved.astype(jnp.float32)
    up = up_saved.astype(jnp.float32)
    sigma = jax.nn.sigmoid(gate)
    deriv = jnp.zeros(gate.shape, jnp.float32)
    for m in each:
        chosen = (routing == (mine ^ m))[:, :, None]
        deriv = jnp.where(chosen, swapped(derivs[m], "expert", m)[:, None, :], deriv)
    d_up = (deriv * gate * sigma).astype(jnp.bfloat16)
    d_gate = (deriv * up * sigma * (1.0 + gate * (1.0 - sigma))).astype(jnp.bfloat16)

    done = ()
    for part, grads, off in [
        (part, grads, off)
        for part in range(parts)
        for grads, off in ((own_grads, 0), (other_grads, span))
    ]:
        done = update(part, place ^ off, grads, weights[part], momentum, done)
    new_weight, new_momentum = done
    return (d_gate, d_up, new_weight, new_momentum)


def solution(mesh):
    placed = (
        P(("expert", "dp"), None),
        P("expert", None, "dp"),
        P("expert", None, "dp"),
        P("expert", None),
        P("expert", None, "dp"),
        P("expert", "dp", None),
    )
    return jax.shard_map(
        body,
        mesh=mesh,
        in_specs=placed,
        out_specs=(
            P("expert", None, "dp"),
            P("expert", None, "dp"),
            P("expert", "dp", None),
            P("expert", "dp", None),
        ),
        check_vma=False,
    )
```

```python
import functools

import jax
import jax.numpy as jnp
from jax import lax
from jax.experimental import pallas as pl
from jax.experimental.pallas import tpu as pltpu
from jax.sharding import PartitionSpec as P

beta_first = 0.9
beta_second = 0.99
step_rate = 0.01
decay_rate = 1.0
sign_width = 10.0
MIB = 1024 * 1024
TOP = 14.0
SMALL = pl.CostEstimate(flops=1024, bytes_accessed=1024, transcendentals=0)


def swapped(array, axis, mask):
    if mask == 0:
        return array
    size = lax.axis_size(axis)
    return lax.ppermute(array, axis, [(i, i ^ mask) for i in range(size)])


def after(value, *others):
    return lax.optimization_barrier((value, *others))[0]


def order_kernel(place_ref, mine_ref, theirs_ref, out_ref):
    out_ref[0, place_ref[0]] = mine_ref[0]
    out_ref[0, 1 - place_ref[0]] = theirs_ref[0]


def stage(*values):
    return lax.optimization_barrier(values)


def in_order(mine, theirs, bit):
    count, some, width = mine.shape
    one = pl.BlockSpec((1, some, width), lambda i, place: (i, 0, 0))
    both = pl.pallas_call(
        order_kernel,
        grid_spec=pltpu.PrefetchScalarGridSpec(
            num_scalar_prefetch=1,
            grid=(count,),
            in_specs=[one, one],
            out_specs=pl.BlockSpec((1, 2, some, width), lambda i, place: (i, 0, 0, 0)),
        ),
        out_shape=jax.ShapeDtypeStruct((count, 2, some, width), mine.dtype),
        cost_estimate=SMALL,
        name="side_by_side",
    )(bit.astype(jnp.int32).reshape(1), mine, theirs)
    return both.reshape(2 * count, some, width)


def place_kernel(place_ref, *refs):
    for m, block_ref in enumerate(refs[:-1]):
        refs[-1][place_ref[0] ^ m] = block_ref[...]


def placed_blocks(blocks, place):
    count = len(blocks)
    return pl.pallas_call(
        place_kernel,
        grid_spec=pltpu.PrefetchScalarGridSpec(
            num_scalar_prefetch=1,
            grid=(1,),
            in_specs=[pl.BlockSpec(blocks[0].shape, lambda i, place: (0, 0))] * count,
            out_specs=pl.BlockSpec((count,) + blocks[0].shape, lambda i, place: (0, 0, 0)),
        ),
        out_shape=jax.ShapeDtypeStruct((count,) + blocks[0].shape, blocks[0].dtype),
        compiler_params=pltpu.CompilerParams(vmem_limit_bytes=56 * MIB),
        cost_estimate=SMALL,
        name="placed_blocks",
    )(place.reshape(1), *blocks)


def pick(hidden, named, out_refs):
    count_rows = hidden.shape[0]
    tokens = out_refs[0].shape[1]
    topk = count_rows // tokens
    token = lax.broadcasted_iota(jnp.int32, (tokens, count_rows), 0)
    row = lax.broadcasted_iota(jnp.int32, (tokens, count_rows), 1)
    here = (row >= token * topk) & (row < token * topk + topk)
    m = 0
    for out_ref in out_refs:
        for i in range(out_ref.shape[0]):
            chosen = jnp.where(here & (named == m), 1.0, 0.0).astype(jnp.bfloat16)
            out_ref[i] = jnp.dot(chosen, hidden, preferred_element_type=jnp.float32).astype(
                jnp.bfloat16
            )
            m += 1


def hidden_kernel(place_ref, gate_ref, up_ref, named_ref, twice_ref, *out_refs):
    gate = gate_ref[...].astype(jnp.float32)
    up = up_ref[...].astype(jnp.float32)
    hidden = (gate * jax.nn.sigmoid(gate) * up).astype(jnp.bfloat16)
    twice_ref[0] = hidden
    twice_ref[1] = hidden
    pick(hidden, named_ref[pl.ds(pl.program_id(0), 1), :], out_refs)


def pick_kernel(place_ref, hidden_ref, named_ref, *out_refs):
    pick(hidden_ref[0], named_ref[pl.ds(pl.program_id(0), 1), :], out_refs)


def picked_rows(arrays, named, group_tok, experts, which):
    cols = arrays[0].shape[-1]
    topk = named.shape[1] // group_tok
    steps = 4
    some = group_tok // steps
    fresh = len(arrays) == 2
    sizes = [1] + [1 << b for b in range(experts.bit_length() - 1)]
    out_shape = [jax.ShapeDtypeStruct((n, group_tok, cols), jnp.bfloat16) for n in sizes]
    out_specs = [pl.BlockSpec((n, some, cols), lambda i, which: (0, i, 0)) for n in sizes]
    if fresh:
        in_specs = [pl.BlockSpec((some * topk, cols), lambda i, which: (i, 0))] * 2
        out_shape = [
            jax.ShapeDtypeStruct((2, group_tok * topk, cols), jnp.bfloat16)
        ] + out_shape
        out_specs = [pl.BlockSpec((2, some * topk, cols), lambda i, which: (0, i, 0))] + out_specs
    else:
        in_specs = [pl.BlockSpec((1, some * topk, cols), lambda i, which: (which[0], i, 0))]
    return pl.pallas_call(
        hidden_kernel if fresh else pick_kernel,
        grid_spec=pltpu.PrefetchScalarGridSpec(
            num_scalar_prefetch=1,
            grid=(steps,),
            in_specs=in_specs + [pl.BlockSpec((steps, some * topk), lambda i, which: (0, 0))],
            out_specs=out_specs,
        ),
        out_shape=out_shape,
        compiler_params=pltpu.CompilerParams(vmem_limit_bytes=56 * MIB),
        cost_estimate=SMALL,
        name="hidden_rows",
    )(which.reshape(1), *arrays, named.reshape(steps, some * topk))


def spread(picked, got, experts):
    half = experts // 2
    held = {0: {(1 << i) >> 1: rows for i, rows in enumerate(picked)}}
    bit = half
    while bit:
        for group in list(held):
            rows = got if bit == half else swapped(held[group][bit], "expert", bit)
            held[group ^ bit] = {0: rows[:1]}
            for i in range(bit.bit_length() - 1):
                held[group ^ bit][1 << i] = rows[1 << i : 2 << i]
        bit //= 2
    return [held[m][0][0] for m in range(experts)]


def term_kernel(count, place_ref, *refs):
    tokens, hidden, outs = refs[:count], refs[count : 2 * count], refs[2 * count :]
    total = None
    for token_ref, hidden_ref in zip(tokens, hidden):
        one = lax.dot_general(
            token_ref[...],
            hidden_ref[...],
            (((0,), (0,)), ((), ())),
            preferred_element_type=jnp.float32,
        )
        total = one if total is None else total + one
    total = total.astype(jnp.bfloat16)
    for m, out_ref in enumerate(outs):

        @pl.when(pl.program_id(0) == m)
        def _():
            out_ref[...] = total


def terms(tokens, hidden, tall, steps, block_of, place):
    group_tok, width = tokens[0].shape
    cols = hidden[0].shape[1]
    count = len(tokens)
    return pl.pallas_call(
        functools.partial(term_kernel, count),
        grid_spec=pltpu.PrefetchScalarGridSpec(
            num_scalar_prefetch=1,
            grid=(steps,),
            in_specs=[
                pl.BlockSpec((group_tok, tall), lambda m, place: (0, block_of(place[0], m)))
            ]
            * count
            + [pl.BlockSpec((group_tok, cols), lambda m, place: (0, 0))] * count,
            out_specs=[pl.BlockSpec((tall, cols), lambda m, place: (0, 0))] * steps,
        ),
        out_shape=[jax.ShapeDtypeStruct((tall, cols), jnp.bfloat16)] * steps,
        compiler_params=pltpu.CompilerParams(vmem_limit_bytes=56 * MIB),
        cost_estimate=SMALL,
        name="group_terms",
    )(place.reshape(1), *tokens, *hidden)


def deriv_kernel(tokens_ref, weight_ref, out_ref):
    out_ref[...] = jnp.dot(
        tokens_ref[...], weight_ref[...], preferred_element_type=jnp.float32
    )


def packed_kernel(tokens_ref, weight_ref, out_ref):
    deriv = jnp.dot(tokens_ref[...], weight_ref[...], preferred_element_type=jnp.float32)
    group_tok = deriv.shape[0]
    largest = jnp.max(jnp.abs(deriv), axis=0, keepdims=True)
    power = jnp.ceil(jnp.log2(jnp.maximum(largest, 2.0**-100)))
    out_ref[:group_tok, :] = deriv * jnp.exp2(TOP - power)
    rest = out_ref.shape[0] - group_tok
    out_ref[group_tok:, :] = jnp.broadcast_to(power, (rest, deriv.shape[1]))


def unpacked(packed, group_tok):
    power = packed[group_tok : group_tok + 1].astype(jnp.float32)
    return packed[:group_tok].astype(jnp.float32) * jnp.exp2(power - TOP)


def deriv_of(tokens, weight, packed):
    group_tok, width = tokens.shape
    cols = weight.shape[1]
    wide = 256 if cols % 256 == 0 else cols
    tall = group_tok + 16 if packed else group_tok
    return pl.pallas_call(
        packed_kernel if packed else deriv_kernel,
        grid=(cols // wide,),
        in_specs=[
            pl.BlockSpec((group_tok, width), lambda i: (0, 0)),
            pl.BlockSpec((width, wide), lambda i: (0, i)),
        ],
        out_specs=pl.BlockSpec((tall, wide), lambda i: (0, i)),
        out_shape=jax.ShapeDtypeStruct((tall, cols), jnp.float32),
        compiler_params=pltpu.CompilerParams(vmem_limit_bytes=56 * MIB),
        cost_estimate=SMALL,
        name="hidden_deriv",
    )(tokens, weight)


def update_kernel(count, place_ref, weight_ref, momentum_ref, *refs):
    grad_refs = refs[:count]
    new_weight_ref, new_momentum_ref = refs[-2:]
    for m, grad_ref in enumerate(grad_refs):

        @pl.when(pl.program_id(0) == m)
        def _():
            grad = grad_ref[...].astype(jnp.float32)
            moment = momentum_ref[0].astype(jnp.float32)
            weight = weight_ref[0].astype(jnp.float32)
            mix = beta_first * moment + (1.0 - beta_first) * grad
            new_weight_ref[0] = weight * (1.0 - step_rate * decay_rate) - step_rate * jnp.tanh(
                mix / sign_width
            )
            new_momentum_ref[0] = (beta_second * moment + (1.0 - beta_second) * grad).astype(
                jnp.bfloat16
            )


def update(part, place, grads, weight, momentum, done):
    _, rows, some = weight.shape
    count = len(grads)
    parts = grads[0].shape[1] // some
    wide = pl.BlockSpec((1, rows, some), lambda m, place: (0, 0, (place[0] ^ m) * parts + part))
    return pl.pallas_call(
        functools.partial(update_kernel, count),
        grid_spec=pltpu.PrefetchScalarGridSpec(
            num_scalar_prefetch=1,
            grid=(count,),
            in_specs=[pl.BlockSpec((1, rows, some), lambda m, place: (place[0] ^ m, 0, 0)), wide]
            + [pl.BlockSpec((rows, some), lambda m, place: (0, part))] * count
            + [pl.BlockSpec(memory_space=pl.ANY)] * len(done),
            out_specs=[wide, wide],
        ),
        out_shape=[
            jax.ShapeDtypeStruct(momentum.shape, jnp.float32),
            jax.ShapeDtypeStruct(momentum.shape, jnp.bfloat16),
        ],
        input_output_aliases={3 + count + i: i for i in range(len(done))},
        compiler_params=pltpu.CompilerParams(vmem_limit_bytes=56 * MIB),
        cost_estimate=SMALL,
        name="lion_step",
    )(place.reshape(1), weight, momentum, *grads, *done)


def body(out_grad, gate_saved, up_saved, routing, down_weight, momentum):
    experts = lax.axis_size("expert")
    shards = lax.axis_size("dp")
    group_tok, topk, cols = gate_saved.shape
    width = out_grad.shape[1]
    rows = momentum.shape[1]
    mine = lax.axis_index("expert")
    place = lax.axis_index("dp")
    span = shards // 2
    each = range(experts)

    half = experts // 2
    others = sorted(range(2, experts, 2), key=lambda m: (bin(m).count("1"), -m))

    blocks = [swapped(out_grad, "dp", m) for m in range(0, shards, 2)]
    named = (routing ^ mine).reshape(1, group_tok * topk)
    upper = place // span
    twice, *own_picked = picked_rows(
        [gate_saved.reshape(-1, cols), up_saved.reshape(-1, cols)],
        named,
        group_tok,
        experts,
        upper,
    )
    blocks, twice, own_picked = stage(blocks, twice, own_picked)

    pairs = [[i, i + span] for i in range(span)]
    other_twice = lax.all_to_all(
        twice, "dp", split_axis=0, concat_axis=0, tiled=True, axis_index_groups=pairs
    )

    held = {0: placed_blocks(blocks, place // 2)}
    for m in others:
        held[m] = swapped(held[m & (m - 1)], "expert", m & -m)
    beside = {0: swapped(held[0], "dp", 1)}
    held, beside, own_picked = stage(held, beside, own_picked)

    last = (place & 1) != 0
    for m in others:
        beside[m] = swapped(held[m], "dp", 1)
    own_got = swapped(own_picked[-1], "expert", half)
    tokens = {}
    for m in [0] + others:
        theirs = after(beside[m], other_twice) if m else beside[m]
        tokens[m] = in_order(held[m], theirs, last).reshape(group_tok, width)
        tokens[m + 1] = swapped(tokens[m], "expert", 1)
    tokens = [tokens[m] for m in each]
    own_rows = spread(own_picked, own_got, experts)
    tokens, own_rows, other_twice = stage(tokens, own_rows, other_twice)

    other_picked = picked_rows([other_twice], named, group_tok, experts, 1 - upper)
    other_got = swapped(other_picked[-1], "expert", half)

    def shard_terms(hidden_rows):
        if rows % 128 == 0:
            return terms(tokens, hidden_rows, rows, span, lambda place, m: place ^ m, place)
        tall = width // 8
        total = terms(
            tokens, hidden_rows, tall, 4, lambda place, m: place // span * 4 + m, place
        )
        total = jnp.concatenate(total, axis=0)
        return [
            lax.dynamic_slice_in_dim(total, (place % span ^ m) * rows, rows, axis=0)
            for m in range(span)
        ]

    own_terms = shard_terms(own_rows)
    weight, own_terms = stage(down_weight[0], own_terms)
    derivs = [deriv_of(tokens[m], weight, m > 0) for m in each]
    derivs = derivs[:1] + [deriv.astype(jnp.float16) for deriv in derivs[1:]]

    other_got, other_picked, derivs = stage(other_got, other_picked, derivs)
    other_rows = spread(other_picked, other_got, experts)
    other_terms = shard_terms(other_rows)

    parts = 2 if cols % 256 == 0 else 1
    pieces = jnp.split(down_weight.reshape(shards, rows, cols), parts, axis=2)
    weights = []
    for part, piece in enumerate(pieces):
        begun = [other_twice] if part == 0 else [weights[-1], other_terms]
        weights.append(
            lax.all_to_all(after(piece, *begun), "dp", split_axis=0, concat_axis=0, tiled=True)
        )

    other_terms = after(other_terms, weights[0])
    own_grads = [swapped(own_terms[m], "dp", m) for m in range(span)]
    other_grads = [swapped(other_terms[m], "dp", m) for m in range(span)]

    gate_saved, up_saved, _ = stage(gate_saved, up_saved, derivs)
    gate = gate_saved.astype(jnp.float32)
    up = up_saved.astype(jnp.float32)
    sigma = jax.nn.sigmoid(gate)
    deriv = jnp.zeros(gate.shape, jnp.float32)
    for m in each:
        chosen = (routing == (mine ^ m))[:, :, None]
        back = unpacked(swapped(derivs[m], "expert", m), group_tok) if m else derivs[m]
        deriv = jnp.where(chosen, back[:, None, :], deriv)
    d_up = (deriv * gate * sigma).astype(jnp.bfloat16)
    d_gate = (deriv * up * sigma * (1.0 + gate * (1.0 - sigma))).astype(jnp.bfloat16)

    done = ()
    for part, grads, off in [
        (part, grads, off)
        for part in range(parts)
        for grads, off in ((own_grads, 0), (other_grads, span))
    ]:
        done = update(part, place ^ off, grads, weights[part], momentum, done)
    new_weight, new_momentum = done
    return (d_gate, d_up, new_weight, new_momentum)


def solution(mesh):
    placed = (
        P(("expert", "dp"), None),
        P("expert", None, "dp"),
        P("expert", None, "dp"),
        P("expert", None),
        P("expert", None, "dp"),
        P("expert", "dp", None),
    )
    return jax.shard_map(
        body,
        mesh=mesh,
        in_specs=placed,
        out_specs=(
            P("expert", None, "dp"),
            P("expert", None, "dp"),
            P("expert", "dp", None),
            P("expert", "dp", None),
        ),
        check_vma=False,
    )
```

```python
import functools

import jax
import jax.numpy as jnp
from jax import lax
from jax.experimental import pallas as pl
from jax.experimental.pallas import tpu as pltpu
from jax.sharding import PartitionSpec as P

beta_first = 0.9
beta_second = 0.99
step_rate = 0.01
decay_rate = 1.0
sign_width = 10.0
MIB = 1024 * 1024
TOP = 14.0
SMALL = pl.CostEstimate(flops=1024, bytes_accessed=1024, transcendentals=0)


def swapped(array, axis, mask):
    if mask == 0:
        return array
    size = lax.axis_size(axis)
    return lax.ppermute(array, axis, [(i, i ^ mask) for i in range(size)])


def after(value, *others):
    return lax.optimization_barrier((value, *others))[0]


def order_kernel(place_ref, mine_ref, theirs_ref, out_ref):
    out_ref[0, place_ref[0]] = mine_ref[0]
    out_ref[0, 1 - place_ref[0]] = theirs_ref[0]


def stage(*values):
    return lax.optimization_barrier(values)


def in_order(mine, theirs, bit):
    count, some, width = mine.shape
    one = pl.BlockSpec((1, some, width), lambda i, place: (i, 0, 0))
    both = pl.pallas_call(
        order_kernel,
        grid_spec=pltpu.PrefetchScalarGridSpec(
            num_scalar_prefetch=1,
            grid=(count,),
            in_specs=[one, one],
            out_specs=pl.BlockSpec((1, 2, some, width), lambda i, place: (i, 0, 0, 0)),
        ),
        out_shape=jax.ShapeDtypeStruct((count, 2, some, width), mine.dtype),
        cost_estimate=SMALL,
        name="side_by_side",
    )(bit.astype(jnp.int32).reshape(1), mine, theirs)
    return both.reshape(2 * count, some, width)


def place_kernel(place_ref, *refs):
    for m, block_ref in enumerate(refs[:-1]):
        refs[-1][place_ref[0] ^ m] = block_ref[...]


def placed_blocks(blocks, place):
    count = len(blocks)
    return pl.pallas_call(
        place_kernel,
        grid_spec=pltpu.PrefetchScalarGridSpec(
            num_scalar_prefetch=1,
            grid=(1,),
            in_specs=[pl.BlockSpec(blocks[0].shape, lambda i, place: (0, 0))] * count,
            out_specs=pl.BlockSpec((count,) + blocks[0].shape, lambda i, place: (0, 0, 0)),
        ),
        out_shape=jax.ShapeDtypeStruct((count,) + blocks[0].shape, blocks[0].dtype),
        compiler_params=pltpu.CompilerParams(vmem_limit_bytes=56 * MIB),
        cost_estimate=SMALL,
        name="placed_blocks",
    )(place.reshape(1), *blocks)


def pick(hidden, named, out_refs):
    count_rows = hidden.shape[0]
    tokens = out_refs[0].shape[1]
    topk = count_rows // tokens
    token = lax.broadcasted_iota(jnp.int32, (tokens, count_rows), 0)
    row = lax.broadcasted_iota(jnp.int32, (tokens, count_rows), 1)
    here = (row >= token * topk) & (row < token * topk + topk)
    m = 0
    for out_ref in out_refs:
        for i in range(out_ref.shape[0]):
            chosen = jnp.where(here & (named == m), 1.0, 0.0).astype(jnp.bfloat16)
            out_ref[i] = jnp.dot(chosen, hidden, preferred_element_type=jnp.float32).astype(
                jnp.bfloat16
            )
            m += 1


def hidden_kernel(place_ref, gate_ref, up_ref, named_ref, twice_ref, *out_refs):
    gate = gate_ref[...].astype(jnp.float32)
    up = up_ref[...].astype(jnp.float32)
    hidden = (gate * jax.nn.sigmoid(gate) * up).astype(jnp.bfloat16)
    twice_ref[0] = hidden
    twice_ref[1] = hidden
    pick(hidden, named_ref[pl.ds(pl.program_id(0), 1), :], out_refs)


def pick_kernel(place_ref, hidden_ref, named_ref, *out_refs):
    pick(hidden_ref[0], named_ref[pl.ds(pl.program_id(0), 1), :], out_refs)


def picked_rows(arrays, named, group_tok, experts, which):
    cols = arrays[0].shape[-1]
    topk = named.shape[1] // group_tok
    steps = 4
    some = group_tok // steps
    fresh = len(arrays) == 2
    sizes = [1] + [1 << b for b in range(experts.bit_length() - 1)]
    out_shape = [jax.ShapeDtypeStruct((n, group_tok, cols), jnp.bfloat16) for n in sizes]
    out_specs = [pl.BlockSpec((n, some, cols), lambda i, which: (0, i, 0)) for n in sizes]
    if fresh:
        in_specs = [pl.BlockSpec((some * topk, cols), lambda i, which: (i, 0))] * 2
        out_shape = [
            jax.ShapeDtypeStruct((2, group_tok * topk, cols), jnp.bfloat16)
        ] + out_shape
        out_specs = [pl.BlockSpec((2, some * topk, cols), lambda i, which: (0, i, 0))] + out_specs
    else:
        in_specs = [pl.BlockSpec((1, some * topk, cols), lambda i, which: (which[0], i, 0))]
    return pl.pallas_call(
        hidden_kernel if fresh else pick_kernel,
        grid_spec=pltpu.PrefetchScalarGridSpec(
            num_scalar_prefetch=1,
            grid=(steps,),
            in_specs=in_specs + [pl.BlockSpec((steps, some * topk), lambda i, which: (0, 0))],
            out_specs=out_specs,
        ),
        out_shape=out_shape,
        compiler_params=pltpu.CompilerParams(vmem_limit_bytes=56 * MIB),
        cost_estimate=SMALL,
        name="hidden_rows",
    )(which.reshape(1), *arrays, named.reshape(steps, some * topk))


def spread(picked, got, experts):
    half = experts // 2
    held = {0: {(1 << i) >> 1: rows for i, rows in enumerate(picked)}}
    bit = half
    while bit:
        for group in list(held):
            rows = got if bit == half else swapped(held[group][bit], "expert", bit)
            held[group ^ bit] = {0: rows[:1]}
            for i in range(bit.bit_length() - 1):
                held[group ^ bit][1 << i] = rows[1 << i : 2 << i]
        bit //= 2
    return [held[m][0][0] for m in range(experts)]


def term_kernel(count, steps, place_ref, *refs):
    tokens, hidden, before = refs[:count], refs[count : 2 * count], refs[2 * count : -steps]
    total = None
    for token_ref, hidden_ref in zip(tokens, hidden):
        one = lax.dot_general(
            token_ref[...],
            hidden_ref[...],
            (((0,), (0,)), ((), ())),
            preferred_element_type=jnp.float32,
        )
        total = one if total is None else total + one
    total = total.astype(jnp.bfloat16)
    for m, out_ref in enumerate(refs[-steps:]):

        @pl.when(pl.program_id(0) == m)
        def _():
            if before:
                out_ref[0] = before[m][0]
            out_ref[out_ref.shape[0] - 1] = total


def terms(tokens, hidden, tall, steps, block_of, place, before=()):
    group_tok, width = tokens[0].shape
    cols = hidden[0].shape[1]
    count = len(tokens)
    deep = 2 if before else 1
    return pl.pallas_call(
        functools.partial(term_kernel, count, steps),
        grid_spec=pltpu.PrefetchScalarGridSpec(
            num_scalar_prefetch=1,
            grid=(steps,),
            in_specs=[
                pl.BlockSpec((group_tok, tall), lambda m, place: (0, block_of(place[0], m)))
            ]
            * count
            + [pl.BlockSpec((group_tok, cols), lambda m, place: (0, 0))] * count
            + [pl.BlockSpec((1, tall, cols), lambda m, place: (0, 0, 0))] * len(before),
            out_specs=[pl.BlockSpec((deep, tall, cols), lambda m, place: (0, 0, 0))] * steps,
        ),
        out_shape=[jax.ShapeDtypeStruct((deep, tall, cols), jnp.bfloat16)] * steps,
        compiler_params=pltpu.CompilerParams(vmem_limit_bytes=56 * MIB),
        cost_estimate=SMALL,
        name="group_terms",
    )(place.reshape(1), *tokens, *hidden, *before)


def deriv_kernel(tokens_ref, weight_ref, out_ref):
    out_ref[...] = jnp.dot(
        tokens_ref[...], weight_ref[...], preferred_element_type=jnp.float32
    )


def packed_kernel(tokens_ref, weight_ref, out_ref):
    deriv = jnp.dot(tokens_ref[...], weight_ref[...], preferred_element_type=jnp.float32)
    group_tok = deriv.shape[0]
    largest = jnp.max(jnp.abs(deriv), axis=0, keepdims=True)
    power = jnp.ceil(jnp.log2(jnp.maximum(largest, 2.0**-100)))
    out_ref[:group_tok, :] = deriv * jnp.exp2(TOP - power)
    rest = out_ref.shape[0] - group_tok
    out_ref[group_tok:, :] = jnp.broadcast_to(power, (rest, deriv.shape[1]))


def unpacked(packed, group_tok):
    power = packed[group_tok : group_tok + 1].astype(jnp.float32)
    return packed[:group_tok].astype(jnp.float32) * jnp.exp2(power - TOP)


def deriv_of(tokens, weight, packed):
    group_tok, width = tokens.shape
    cols = weight.shape[1]
    wide = 256 if cols % 256 == 0 else cols
    tall = group_tok + 16 if packed else group_tok
    return pl.pallas_call(
        packed_kernel if packed else deriv_kernel,
        grid=(cols // wide,),
        in_specs=[
            pl.BlockSpec((group_tok, width), lambda i: (0, 0)),
            pl.BlockSpec((width, wide), lambda i: (0, i)),
        ],
        out_specs=pl.BlockSpec((tall, wide), lambda i: (0, i)),
        out_shape=jax.ShapeDtypeStruct((tall, cols), jnp.float32),
        compiler_params=pltpu.CompilerParams(vmem_limit_bytes=56 * MIB),
        cost_estimate=SMALL,
        name="hidden_deriv",
    )(tokens, weight)


def update_kernel(count, place_ref, weight_ref, momentum_ref, *refs):
    grad_refs = refs[:count]
    new_weight_ref, new_momentum_ref = refs[-2:]
    for m, grad_ref in enumerate(grad_refs):

        @pl.when(pl.program_id(1) == m)
        def _():
            grad = grad_ref[0].astype(jnp.float32)
            moment = momentum_ref[0].astype(jnp.float32)
            weight = weight_ref[0].astype(jnp.float32)
            mix = beta_first * moment + (1.0 - beta_first) * grad
            new_weight_ref[0] = weight * (1.0 - step_rate * decay_rate) - step_rate * jnp.tanh(
                mix / sign_width
            )
            new_momentum_ref[0] = (beta_second * moment + (1.0 - beta_second) * grad).astype(
                jnp.bfloat16
            )


def update(part, place, grads, weight, momentum, done):
    sources, rows, some = weight.shape
    count = len(grads)
    parts = grads[0].shape[2] // some

    def source(far, m, place):
        return place[0] ^ m ^ (far * count)

    wide = pl.BlockSpec(
        (1, rows, some), lambda far, m, place: (0, 0, source(far, m, place) * parts + part)
    )
    return pl.pallas_call(
        functools.partial(update_kernel, count),
        grid_spec=pltpu.PrefetchScalarGridSpec(
            num_scalar_prefetch=1,
            grid=(2, count),
            in_specs=[
                pl.BlockSpec((1, rows, some), lambda far, m, place: (source(far, m, place), 0, 0)),
                wide,
            ]
            + [pl.BlockSpec((1, rows, some), lambda far, m, place: (far, 0, part))] * count
            + [pl.BlockSpec(memory_space=pl.ANY)] * len(done),
            out_specs=[wide, wide],
        ),
        out_shape=[
            jax.ShapeDtypeStruct(momentum.shape, jnp.float32),
            jax.ShapeDtypeStruct(momentum.shape, jnp.bfloat16),
        ],
        input_output_aliases={3 + count + i: i for i in range(len(done))},
        compiler_params=pltpu.CompilerParams(vmem_limit_bytes=56 * MIB),
        cost_estimate=SMALL,
        name="lion_step",
    )(place.reshape(1), weight, momentum, *grads, *done)


def body(out_grad, gate_saved, up_saved, routing, down_weight, momentum):
    experts = lax.axis_size("expert")
    shards = lax.axis_size("dp")
    group_tok, topk, cols = gate_saved.shape
    width = out_grad.shape[1]
    rows = momentum.shape[1]
    mine = lax.axis_index("expert")
    place = lax.axis_index("dp")
    span = shards // 2
    each = range(experts)

    half = experts // 2
    others = sorted(range(2, experts, 2), key=lambda m: (bin(m).count("1"), -m))

    blocks = [swapped(out_grad, "dp", m) for m in range(0, shards, 2)]
    named = (routing ^ mine).reshape(1, group_tok * topk)
    upper = place // span
    twice, *own_picked = picked_rows(
        [gate_saved.reshape(-1, cols), up_saved.reshape(-1, cols)],
        named,
        group_tok,
        experts,
        upper,
    )
    blocks, twice, own_picked = stage(blocks, twice, own_picked)

    pairs = [[i, i + span] for i in range(span)]
    other_twice = lax.all_to_all(
        twice, "dp", split_axis=0, concat_axis=0, tiled=True, axis_index_groups=pairs
    )

    held = {0: placed_blocks(blocks, place // 2)}
    for m in others:
        held[m] = swapped(held[m & (m - 1)], "expert", m & -m)
    beside = {0: swapped(held[0], "dp", 1)}
    held, beside, own_picked = stage(held, beside, own_picked)

    last = (place & 1) != 0
    for m in others:
        beside[m] = swapped(held[m], "dp", 1)
    own_got = swapped(own_picked[-1], "expert", half)
    tokens = {}
    for m in [0] + others:
        theirs = after(beside[m], other_twice) if m else beside[m]
        tokens[m] = in_order(held[m], theirs, last).reshape(group_tok, width)
        tokens[m + 1] = swapped(tokens[m], "expert", 1)
    tokens = [tokens[m] for m in each]
    own_rows = spread(own_picked, own_got, experts)
    tokens, own_rows = stage(tokens, own_rows)

    other_picked = picked_rows([other_twice], named, group_tok, experts, 1 - upper)
    other_got = swapped(other_picked[-1], "expert", half)

    def shard_terms(hidden_rows, before):
        if rows % 128 == 0:
            return terms(tokens, hidden_rows, rows, span, lambda place, m: place ^ m, place, before)
        tall = width // 8
        total = terms(
            tokens, hidden_rows, tall, 4, lambda place, m: place // span * 4 + m, place
        )
        total = jnp.concatenate(total, axis=1)
        blocks = [
            lax.dynamic_slice_in_dim(total, (place % span ^ m) * rows, rows, axis=1)
            for m in range(span)
        ]
        return [jnp.concatenate(pair, axis=0) for pair in zip(before, blocks)] if before else blocks

    own_terms = shard_terms(own_rows, ())
    weight, own_terms = stage(down_weight[0], own_terms)
    derivs = [deriv_of(tokens[m], weight, m > 0) for m in each]
    derivs = derivs[:1] + [deriv.astype(jnp.float16) for deriv in derivs[1:]]

    other_got, other_picked, derivs = stage(other_got, other_picked, derivs)
    other_rows = spread(other_picked, other_got, experts)
    both_terms = shard_terms(other_rows, own_terms)

    parts = 2 if cols % 256 == 0 else 1
    pieces = jnp.split(down_weight.reshape(shards, rows, cols), parts, axis=2)
    weights = []
    for part, piece in enumerate(pieces):
        begun = [other_twice] if part == 0 else [weights[-1], both_terms]
        weights.append(
            lax.all_to_all(after(piece, *begun), "dp", split_axis=0, concat_axis=0, tiled=True)
        )

    grads = [swapped(both_terms[m], "dp", m) for m in range(span)]

    gate_saved, up_saved, _ = stage(gate_saved, up_saved, derivs)
    gate = gate_saved.astype(jnp.float32)
    up = up_saved.astype(jnp.float32)
    sigma = jax.nn.sigmoid(gate)
    deriv = jnp.zeros(gate.shape, jnp.float32)
    for m in each:
        chosen = (routing == (mine ^ m))[:, :, None]
        back = unpacked(swapped(derivs[m], "expert", m), group_tok) if m else derivs[m]
        deriv = jnp.where(chosen, back[:, None, :], deriv)
    d_up = (deriv * gate * sigma).astype(jnp.bfloat16)
    d_gate = (deriv * up * sigma * (1.0 + gate * (1.0 - sigma))).astype(jnp.bfloat16)

    done = ()
    for part in range(parts):
        done = update(part, place, grads, weights[part], momentum, done)
    new_weight, new_momentum = done
    return (d_gate, d_up, new_weight, new_momentum)


def solution(mesh):
    placed = (
        P(("expert", "dp"), None),
        P("expert", None, "dp"),
        P("expert", None, "dp"),
        P("expert", None),
        P("expert", None, "dp"),
        P("expert", "dp", None),
    )
    return jax.shard_map(
        body,
        mesh=mesh,
        in_specs=placed,
        out_specs=(
            P("expert", None, "dp"),
            P("expert", None, "dp"),
            P("expert", "dp", None),
            P("expert", "dp", None),
        ),
        check_vma=False,
    )
```

```python
import functools

import jax
import jax.numpy as jnp
from jax import lax
from jax.experimental import pallas as pl
from jax.experimental.pallas import tpu as pltpu
from jax.sharding import PartitionSpec as P

beta_first = 0.9
beta_second = 0.99
step_rate = 0.01
decay_rate = 1.0
sign_width = 10.0
MIB = 1024 * 1024
TOP = 14.0
SMALL = pl.CostEstimate(flops=1024, bytes_accessed=1024, transcendentals=0)


def swapped(array, axis, mask):
    if mask == 0:
        return array
    size = lax.axis_size(axis)
    return lax.ppermute(array, axis, [(i, i ^ mask) for i in range(size)])


def after(value, *others):
    return lax.optimization_barrier((value, *others))[0]


def order_kernel(place_ref, mine_ref, theirs_ref, out_ref):
    out_ref[0, place_ref[0]] = mine_ref[0]
    out_ref[0, 1 - place_ref[0]] = theirs_ref[0]


def stage(*values):
    return lax.optimization_barrier(values)


def in_order(mine, theirs, bit):
    count, some, width = mine.shape
    one = pl.BlockSpec((1, some, width), lambda i, place: (i, 0, 0))
    both = pl.pallas_call(
        order_kernel,
        grid_spec=pltpu.PrefetchScalarGridSpec(
            num_scalar_prefetch=1,
            grid=(count,),
            in_specs=[one, one],
            out_specs=pl.BlockSpec((1, 2, some, width), lambda i, place: (i, 0, 0, 0)),
        ),
        out_shape=jax.ShapeDtypeStruct((count, 2, some, width), mine.dtype),
        cost_estimate=SMALL,
        name="side_by_side",
    )(bit.astype(jnp.int32).reshape(1), mine, theirs)
    return both.reshape(2 * count, some, width)


def place_kernel(place_ref, *refs):
    for m, block_ref in enumerate(refs[:-1]):
        refs[-1][place_ref[0] ^ m] = block_ref[...]


def placed_blocks(blocks, place):
    count = len(blocks)
    return pl.pallas_call(
        place_kernel,
        grid_spec=pltpu.PrefetchScalarGridSpec(
            num_scalar_prefetch=1,
            grid=(1,),
            in_specs=[pl.BlockSpec(blocks[0].shape, lambda i, place: (0, 0))] * count,
            out_specs=pl.BlockSpec((count,) + blocks[0].shape, lambda i, place: (0, 0, 0)),
        ),
        out_shape=jax.ShapeDtypeStruct((count,) + blocks[0].shape, blocks[0].dtype),
        compiler_params=pltpu.CompilerParams(vmem_limit_bytes=56 * MIB),
        cost_estimate=SMALL,
        name="placed_blocks",
    )(place.reshape(1), *blocks)


def pick(hidden, named, out_refs):
    count_rows = hidden.shape[0]
    tokens = out_refs[0].shape[1]
    topk = count_rows // tokens
    token = lax.broadcasted_iota(jnp.int32, (tokens, count_rows), 0)
    row = lax.broadcasted_iota(jnp.int32, (tokens, count_rows), 1)
    here = (row >= token * topk) & (row < token * topk + topk)
    m = 0
    for out_ref in out_refs:
        for i in range(out_ref.shape[0]):
            chosen = jnp.where(here & (named == m), 1.0, 0.0).astype(jnp.bfloat16)
            out_ref[i] = jnp.dot(chosen, hidden, preferred_element_type=jnp.float32).astype(
                jnp.bfloat16
            )
            m += 1


def hidden_kernel(place_ref, gate_ref, up_ref, named_ref, twice_ref, *out_refs):
    gate = gate_ref[...].astype(jnp.float32)
    up = up_ref[...].astype(jnp.float32)
    hidden = (gate * jax.nn.sigmoid(gate) * up).astype(jnp.bfloat16)
    twice_ref[0] = hidden
    twice_ref[1] = hidden
    pick(hidden, named_ref[pl.ds(pl.program_id(0), 1), :], out_refs)


def pick_kernel(place_ref, hidden_ref, named_ref, *out_refs):
    pick(hidden_ref[0], named_ref[pl.ds(pl.program_id(0), 1), :], out_refs)


def picked_rows(arrays, named, group_tok, experts, which):
    cols = arrays[0].shape[-1]
    topk = named.shape[1] // group_tok
    steps = 4
    some = group_tok // steps
    fresh = len(arrays) == 2
    sizes = [1] + [1 << b for b in range(experts.bit_length() - 1)]
    out_shape = [jax.ShapeDtypeStruct((n, group_tok, cols), jnp.bfloat16) for n in sizes]
    out_specs = [pl.BlockSpec((n, some, cols), lambda i, which: (0, i, 0)) for n in sizes]
    if fresh:
        in_specs = [pl.BlockSpec((some * topk, cols), lambda i, which: (i, 0))] * 2
        out_shape = [
            jax.ShapeDtypeStruct((2, group_tok * topk, cols), jnp.bfloat16)
        ] + out_shape
        out_specs = [pl.BlockSpec((2, some * topk, cols), lambda i, which: (0, i, 0))] + out_specs
    else:
        in_specs = [pl.BlockSpec((1, some * topk, cols), lambda i, which: (which[0], i, 0))]
    return pl.pallas_call(
        hidden_kernel if fresh else pick_kernel,
        grid_spec=pltpu.PrefetchScalarGridSpec(
            num_scalar_prefetch=1,
            grid=(steps,),
            in_specs=in_specs + [pl.BlockSpec((steps, some * topk), lambda i, which: (0, 0))],
            out_specs=out_specs,
        ),
        out_shape=out_shape,
        compiler_params=pltpu.CompilerParams(vmem_limit_bytes=56 * MIB),
        cost_estimate=SMALL,
        name="hidden_rows",
    )(which.reshape(1), *arrays, named.reshape(steps, some * topk))


def spread(picked, got, experts):
    half = experts // 2
    held = {0: {(1 << i) >> 1: rows for i, rows in enumerate(picked)}}
    bit = half
    while bit:
        for group in list(held):
            rows = got if bit == half else swapped(held[group][bit], "expert", bit)
            held[group ^ bit] = {0: rows[:1]}
            for i in range(bit.bit_length() - 1):
                held[group ^ bit][1 << i] = rows[1 << i : 2 << i]
        bit //= 2
    return [held[m][0][0] for m in range(experts)]


def term_kernel(count, steps, place_ref, *refs):
    tokens, hidden, before = refs[:count], refs[count : 2 * count], refs[2 * count : -steps]
    total = None
    for token_ref, hidden_ref in zip(tokens, hidden):
        one = lax.dot_general(
            token_ref[...],
            hidden_ref[...],
            (((0,), (0,)), ((), ())),
            preferred_element_type=jnp.float32,
        )
        total = one if total is None else total + one
    total = total.astype(jnp.bfloat16)
    for m, out_ref in enumerate(refs[-steps:]):

        @pl.when(pl.program_id(0) == m)
        def _():
            if before:
                out_ref[0] = before[m][0]
            out_ref[out_ref.shape[0] - 1] = total


def terms(tokens, hidden, tall, steps, block_of, place, before=()):
    group_tok, width = tokens[0].shape
    cols = hidden[0].shape[1]
    count = len(tokens)
    deep = 2 if before else 1
    return pl.pallas_call(
        functools.partial(term_kernel, count, steps),
        grid_spec=pltpu.PrefetchScalarGridSpec(
            num_scalar_prefetch=1,
            grid=(steps,),
            in_specs=[
                pl.BlockSpec((group_tok, tall), lambda m, place: (0, block_of(place[0], m)))
            ]
            * count
            + [pl.BlockSpec((group_tok, cols), lambda m, place: (0, 0))] * count
            + [pl.BlockSpec((1, tall, cols), lambda m, place: (0, 0, 0))] * len(before),
            out_specs=[pl.BlockSpec((deep, tall, cols), lambda m, place: (0, 0, 0))] * steps,
        ),
        out_shape=[jax.ShapeDtypeStruct((deep, tall, cols), jnp.bfloat16)] * steps,
        compiler_params=pltpu.CompilerParams(vmem_limit_bytes=56 * MIB),
        cost_estimate=SMALL,
        name="group_terms",
    )(place.reshape(1), *tokens, *hidden, *before)


def deriv_kernel(tokens_ref, weight_ref, out_ref):
    out_ref[...] = jnp.dot(
        tokens_ref[...], weight_ref[...], preferred_element_type=jnp.float32
    )


def packed_kernel(tokens_ref, weight_ref, out_ref):
    deriv = jnp.dot(tokens_ref[...], weight_ref[...], preferred_element_type=jnp.float32)
    group_tok = deriv.shape[0]
    largest = jnp.max(jnp.abs(deriv), axis=0, keepdims=True)
    power = jnp.ceil(jnp.log2(jnp.maximum(largest, 2.0**-100)))
    out_ref[:group_tok, :] = deriv * jnp.exp2(TOP - power)
    rest = out_ref.shape[0] - group_tok
    out_ref[group_tok:, :] = jnp.broadcast_to(power, (rest, deriv.shape[1]))


def unpacked(packed, group_tok):
    power = packed[group_tok : group_tok + 1].astype(jnp.float32)
    return packed[:group_tok].astype(jnp.float32) * jnp.exp2(power - TOP)


def deriv_of(tokens, weight, packed):
    group_tok, width = tokens.shape
    cols = weight.shape[1]
    wide = 256 if cols % 256 == 0 else cols
    tall = group_tok + 16 if packed else group_tok
    return pl.pallas_call(
        packed_kernel if packed else deriv_kernel,
        grid=(cols // wide,),
        in_specs=[
            pl.BlockSpec((group_tok, width), lambda i: (0, 0)),
            pl.BlockSpec((width, wide), lambda i: (0, i)),
        ],
        out_specs=pl.BlockSpec((tall, wide), lambda i: (0, i)),
        out_shape=jax.ShapeDtypeStruct((tall, cols), jnp.float32),
        compiler_params=pltpu.CompilerParams(vmem_limit_bytes=56 * MIB),
        cost_estimate=SMALL,
        name="hidden_deriv",
    )(tokens, weight)


def update_kernel(count, place_ref, weight_ref, momentum_ref, *refs):
    grad_refs = refs[:count]
    new_weight_ref, new_momentum_ref = refs[-2:]
    for m, grad_ref in enumerate(grad_refs):

        @pl.when(pl.program_id(1) == m)
        def _():
            grad = grad_ref[0].astype(jnp.float32)
            moment = momentum_ref[0].astype(jnp.float32)
            weight = weight_ref[0].astype(jnp.float32)
            mix = beta_first * moment + (1.0 - beta_first) * grad
            new_weight_ref[0] = weight * (1.0 - step_rate * decay_rate) - step_rate * jnp.tanh(
                mix / sign_width
            )
            new_momentum_ref[0] = (beta_second * moment + (1.0 - beta_second) * grad).astype(
                jnp.bfloat16
            )


def update(part, place, grads, weight, momentum, done):
    sources, rows, some = weight.shape
    count = len(grads)
    parts = grads[0].shape[2] // some

    def source(far, m, place):
        return place[0] ^ m ^ (far * count)

    wide = pl.BlockSpec(
        (1, rows, some), lambda far, m, place: (0, 0, source(far, m, place) * parts + part)
    )
    return pl.pallas_call(
        functools.partial(update_kernel, count),
        grid_spec=pltpu.PrefetchScalarGridSpec(
            num_scalar_prefetch=1,
            grid=(2, count),
            in_specs=[
                pl.BlockSpec((1, rows, some), lambda far, m, place: (source(far, m, place), 0, 0)),
                wide,
            ]
            + [pl.BlockSpec((1, rows, some), lambda far, m, place: (far, 0, part))] * count
            + [pl.BlockSpec(memory_space=pl.ANY)] * len(done),
            out_specs=[wide, wide],
        ),
        out_shape=[
            jax.ShapeDtypeStruct(momentum.shape, jnp.float32),
            jax.ShapeDtypeStruct(momentum.shape, jnp.bfloat16),
        ],
        input_output_aliases={3 + count + i: i for i in range(len(done))},
        compiler_params=pltpu.CompilerParams(vmem_limit_bytes=56 * MIB),
        cost_estimate=SMALL,
        name="lion_step",
    )(place.reshape(1), weight, momentum, *grads, *done)


def body(out_grad, gate_saved, up_saved, routing, down_weight, momentum):
    experts = lax.axis_size("expert")
    shards = lax.axis_size("dp")
    group_tok, topk, cols = gate_saved.shape
    width = out_grad.shape[1]
    rows = momentum.shape[1]
    mine = lax.axis_index("expert")
    place = lax.axis_index("dp")
    span = shards // 2
    each = range(experts)

    half = experts // 2
    others = sorted(range(2, experts, 2), key=lambda m: (bin(m).count("1"), -m))

    blocks = [swapped(out_grad, "dp", m) for m in range(0, shards, 2)]
    named = (routing ^ mine).reshape(1, group_tok * topk)
    upper = place // span
    twice, *own_picked = picked_rows(
        [gate_saved.reshape(-1, cols), up_saved.reshape(-1, cols)],
        named,
        group_tok,
        experts,
        upper,
    )
    blocks, twice, own_picked = stage(blocks, twice, own_picked)

    pairs = [[i, i + span] for i in range(span)]
    other_twice = lax.all_to_all(
        twice, "dp", split_axis=0, concat_axis=0, tiled=True, axis_index_groups=pairs
    )

    held = {0: placed_blocks(blocks, place // 2)}
    for m in others:
        held[m] = swapped(held[m & (m - 1)], "expert", m & -m)
    beside = {0: swapped(held[0], "dp", 1)}
    held, beside, own_picked = stage(held, beside, own_picked)

    last = (place & 1) != 0
    for m in others:
        beside[m] = swapped(held[m], "dp", 1)
    own_got = swapped(own_picked[-1], "expert", half)
    tokens = {}
    for m in [0] + others:
        theirs = after(beside[m], other_twice) if m else beside[m]
        tokens[m] = in_order(held[m], theirs, last).reshape(group_tok, width)
        tokens[m + 1] = swapped(tokens[m], "expert", 1)
    tokens = [tokens[m] for m in each]
    own_rows = spread(own_picked, own_got, experts)
    tokens, own_rows = stage(tokens, own_rows)

    other_picked = picked_rows([other_twice], named, group_tok, experts, 1 - upper)
    other_got = swapped(other_picked[-1], "expert", half)

    def shard_terms(hidden_rows, before):
        if rows % 128 == 0:
            return terms(tokens, hidden_rows, rows, span, lambda place, m: place ^ m, place, before)
        tall = width // 8
        total = terms(
            tokens, hidden_rows, tall, 4, lambda place, m: place // span * 4 + m, place
        )
        total = jnp.concatenate(total, axis=1)
        blocks = [
            lax.dynamic_slice_in_dim(total, (place % span ^ m) * rows, rows, axis=1)
            for m in range(span)
        ]
        return [jnp.concatenate(pair, axis=0) for pair in zip(before, blocks)] if before else blocks

    own_terms = shard_terms(own_rows, ())
    weight, own_terms = stage(down_weight[0], own_terms)
    derivs = [deriv_of(tokens[m], weight, m > 0) for m in each]
    derivs = derivs[:1] + [deriv.astype(jnp.float16) for deriv in derivs[1:]]

    other_got, other_picked, derivs = stage(other_got, other_picked, derivs)
    other_rows = spread(other_picked, other_got, experts)
    both_terms = shard_terms(other_rows, own_terms)

    parts = 2 if cols % 256 == 0 else 1
    pieces = jnp.split(down_weight.reshape(shards, rows, cols), parts, axis=2)
    weights = []
    for part, piece in enumerate(pieces):
        begun = [other_twice] if part == 0 else [weights[-1], both_terms]
        weights.append(
            lax.all_to_all(after(piece, *begun), "dp", split_axis=0, concat_axis=0, tiled=True)
        )

    grads = [swapped(both_terms[m], "dp", m) for m in range(span)]

    backs = [swapped(derivs[m], "expert", m) for m in each]
    gate_saved, up_saved, backs, _ = stage(gate_saved, up_saved, backs, weights[-1])
    gate = gate_saved.astype(jnp.float32)
    up = up_saved.astype(jnp.float32)
    sigma = jax.nn.sigmoid(gate)
    deriv = jnp.zeros(gate.shape, jnp.float32)
    for m in each:
        chosen = (routing == (mine ^ m))[:, :, None]
        back = unpacked(backs[m], group_tok) if m else backs[m]
        deriv = jnp.where(chosen, back[:, None, :], deriv)
    d_up = (deriv * gate * sigma).astype(jnp.bfloat16)
    d_gate = (deriv * up * sigma * (1.0 + gate * (1.0 - sigma))).astype(jnp.bfloat16)

    done = ()
    for part in range(parts):
        done = update(part, place, grads, weights[part], momentum, done)
    new_weight, new_momentum = done
    return (d_gate, d_up, new_weight, new_momentum)


def solution(mesh):
    placed = (
        P(("expert", "dp"), None),
        P("expert", None, "dp"),
        P("expert", None, "dp"),
        P("expert", None),
        P("expert", None, "dp"),
        P("expert", "dp", None),
    )
    return jax.shard_map(
        body,
        mesh=mesh,
        in_specs=placed,
        out_specs=(
            P("expert", None, "dp"),
            P("expert", None, "dp"),
            P("expert", "dp", None),
            P("expert", "dp", None),
        ),
        check_vma=False,
    )
```

```python
import functools

import jax
import jax.numpy as jnp
from jax import lax
from jax.experimental import pallas as pl
from jax.experimental.pallas import tpu as pltpu
from jax.sharding import PartitionSpec as P

beta_first = 0.9
beta_second = 0.99
step_rate = 0.01
decay_rate = 1.0
sign_width = 10.0
MIB = 1024 * 1024
TOP = 14.0
SMALL = pl.CostEstimate(flops=1024, bytes_accessed=1024, transcendentals=0)


def swapped(array, axis, mask):
    if mask == 0:
        return array
    size = lax.axis_size(axis)
    return lax.ppermute(array, axis, [(i, i ^ mask) for i in range(size)])


def after(value, *others):
    return lax.optimization_barrier((value, *others))[0]


def order_kernel(place_ref, mine_ref, theirs_ref, out_ref):
    out_ref[0, place_ref[0]] = mine_ref[0]
    out_ref[0, 1 - place_ref[0]] = theirs_ref[0]


def stage(*values):
    return lax.optimization_barrier(values)


def in_order(mine, theirs, bit):
    count, some, width = mine.shape
    one = pl.BlockSpec((1, some, width), lambda i, place: (i, 0, 0))
    both = pl.pallas_call(
        order_kernel,
        grid_spec=pltpu.PrefetchScalarGridSpec(
            num_scalar_prefetch=1,
            grid=(count,),
            in_specs=[one, one],
            out_specs=pl.BlockSpec((1, 2, some, width), lambda i, place: (i, 0, 0, 0)),
        ),
        out_shape=jax.ShapeDtypeStruct((count, 2, some, width), mine.dtype),
        cost_estimate=SMALL,
        name="side_by_side",
    )(bit.astype(jnp.int32).reshape(1), mine, theirs)
    return both.reshape(2 * count, some, width)


def place_kernel(place_ref, *refs):
    for m, block_ref in enumerate(refs[:-1]):
        refs[-1][place_ref[0] ^ m] = block_ref[...]


def placed_blocks(blocks, place):
    count = len(blocks)
    return pl.pallas_call(
        place_kernel,
        grid_spec=pltpu.PrefetchScalarGridSpec(
            num_scalar_prefetch=1,
            grid=(1,),
            in_specs=[pl.BlockSpec(blocks[0].shape, lambda i, place: (0, 0))] * count,
            out_specs=pl.BlockSpec((count,) + blocks[0].shape, lambda i, place: (0, 0, 0)),
        ),
        out_shape=jax.ShapeDtypeStruct((count,) + blocks[0].shape, blocks[0].dtype),
        compiler_params=pltpu.CompilerParams(vmem_limit_bytes=56 * MIB),
        cost_estimate=SMALL,
        name="placed_blocks",
    )(place.reshape(1), *blocks)


def pick(hidden, named, out_refs):
    count_rows = hidden.shape[0]
    tokens = out_refs[0].shape[1]
    topk = count_rows // tokens
    token = lax.broadcasted_iota(jnp.int32, (tokens, count_rows), 0)
    row = lax.broadcasted_iota(jnp.int32, (tokens, count_rows), 1)
    here = (row >= token * topk) & (row < token * topk + topk)
    m = 0
    for out_ref in out_refs:
        for i in range(out_ref.shape[0]):
            chosen = jnp.where(here & (named == m), 1.0, 0.0).astype(jnp.bfloat16)
            out_ref[i] = jnp.dot(chosen, hidden, preferred_element_type=jnp.float32).astype(
                jnp.bfloat16
            )
            m += 1


def hidden_kernel(place_ref, gate_ref, up_ref, named_ref, twice_ref, *out_refs):
    gate = gate_ref[...].astype(jnp.float32)
    up = up_ref[...].astype(jnp.float32)
    hidden = (gate * jax.nn.sigmoid(gate) * up).astype(jnp.bfloat16)
    twice_ref[0] = hidden
    twice_ref[1] = hidden
    pick(hidden, named_ref[pl.ds(pl.program_id(0), 1), :], out_refs)


def pick_kernel(place_ref, hidden_ref, named_ref, *out_refs):
    pick(hidden_ref[0], named_ref[pl.ds(pl.program_id(0), 1), :], out_refs)


def picked_rows(arrays, named, group_tok, experts, which):
    cols = arrays[0].shape[-1]
    topk = named.shape[1] // group_tok
    steps = 4
    some = group_tok // steps
    fresh = len(arrays) == 2
    sizes = [1] + [1 << b for b in range(experts.bit_length() - 1)]
    out_shape = [jax.ShapeDtypeStruct((n, group_tok, cols), jnp.bfloat16) for n in sizes]
    out_specs = [pl.BlockSpec((n, some, cols), lambda i, which: (0, i, 0)) for n in sizes]
    if fresh:
        in_specs = [pl.BlockSpec((some * topk, cols), lambda i, which: (i, 0))] * 2
        out_shape = [
            jax.ShapeDtypeStruct((2, group_tok * topk, cols), jnp.bfloat16)
        ] + out_shape
        out_specs = [pl.BlockSpec((2, some * topk, cols), lambda i, which: (0, i, 0))] + out_specs
    else:
        in_specs = [pl.BlockSpec((1, some * topk, cols), lambda i, which: (which[0], i, 0))]
    return pl.pallas_call(
        hidden_kernel if fresh else pick_kernel,
        grid_spec=pltpu.PrefetchScalarGridSpec(
            num_scalar_prefetch=1,
            grid=(steps,),
            in_specs=in_specs + [pl.BlockSpec((steps, some * topk), lambda i, which: (0, 0))],
            out_specs=out_specs,
        ),
        out_shape=out_shape,
        compiler_params=pltpu.CompilerParams(vmem_limit_bytes=56 * MIB),
        cost_estimate=SMALL,
        name="hidden_rows",
    )(which.reshape(1), *arrays, named.reshape(steps, some * topk))


def spread(picked, got, experts):
    half = experts // 2
    held = {0: {(1 << i) >> 1: rows for i, rows in enumerate(picked)}}
    bit = half
    while bit:
        for group in list(held):
            rows = got if bit == half else swapped(held[group][bit], "expert", bit)
            held[group ^ bit] = {0: rows[:1]}
            for i in range(bit.bit_length() - 1):
                held[group ^ bit][1 << i] = rows[1 << i : 2 << i]
        bit //= 2
    return [held[m][0][0] for m in range(experts)]


def term_kernel(count, steps, place_ref, *refs):
    tokens, hidden, before = refs[:count], refs[count : 2 * count], refs[2 * count : -steps]
    total = None
    for token_ref, hidden_ref in zip(tokens, hidden):
        one = lax.dot_general(
            token_ref[...],
            hidden_ref[...],
            (((0,), (0,)), ((), ())),
            preferred_element_type=jnp.float32,
        )
        total = one if total is None else total + one
    total = total.astype(jnp.bfloat16)
    for m, out_ref in enumerate(refs[-steps:]):

        @pl.when(pl.program_id(0) == m)
        def _():
            if before:
                out_ref[0] = before[m][0]
            out_ref[out_ref.shape[0] - 1] = total


def terms(tokens, hidden, tall, steps, block_of, place, before=()):
    group_tok, width = tokens[0].shape
    cols = hidden[0].shape[1]
    count = len(tokens)
    deep = 2 if before else 1
    return pl.pallas_call(
        functools.partial(term_kernel, count, steps),
        grid_spec=pltpu.PrefetchScalarGridSpec(
            num_scalar_prefetch=1,
            grid=(steps,),
            in_specs=[
                pl.BlockSpec((group_tok, tall), lambda m, place: (0, block_of(place[0], m)))
            ]
            * count
            + [pl.BlockSpec((group_tok, cols), lambda m, place: (0, 0))] * count
            + [pl.BlockSpec((1, tall, cols), lambda m, place: (0, 0, 0))] * len(before),
            out_specs=[pl.BlockSpec((deep, tall, cols), lambda m, place: (0, 0, 0))] * steps,
        ),
        out_shape=[jax.ShapeDtypeStruct((deep, tall, cols), jnp.bfloat16)] * steps,
        compiler_params=pltpu.CompilerParams(vmem_limit_bytes=56 * MIB),
        cost_estimate=SMALL,
        name="group_terms",
    )(place.reshape(1), *tokens, *hidden, *before)


def deriv_kernel(tokens_ref, weight_ref, out_ref):
    out_ref[...] = jnp.dot(
        tokens_ref[...], weight_ref[...], preferred_element_type=jnp.float32
    )


def packed_kernel(tokens_ref, weight_ref, out_ref):
    deriv = jnp.dot(tokens_ref[...], weight_ref[...], preferred_element_type=jnp.float32)
    group_tok = deriv.shape[0]
    largest = jnp.max(jnp.abs(deriv), axis=0, keepdims=True)
    power = jnp.ceil(jnp.log2(jnp.maximum(largest, 2.0**-100)))
    out_ref[:group_tok, :] = deriv * jnp.exp2(TOP - power)
    rest = out_ref.shape[0] - group_tok
    out_ref[group_tok:, :] = jnp.broadcast_to(power, (rest, deriv.shape[1]))


def unpacked(packed, group_tok):
    power = packed[group_tok : group_tok + 1].astype(jnp.float32)
    return packed[:group_tok].astype(jnp.float32) * jnp.exp2(power - TOP)


def deriv_of(tokens, weight, packed):
    group_tok, width = tokens.shape
    cols = weight.shape[1]
    wide = 256 if cols % 256 == 0 else cols
    tall = group_tok + 16 if packed else group_tok
    return pl.pallas_call(
        packed_kernel if packed else deriv_kernel,
        grid=(cols // wide,),
        in_specs=[
            pl.BlockSpec((group_tok, width), lambda i: (0, 0)),
            pl.BlockSpec((width, wide), lambda i: (0, i)),
        ],
        out_specs=pl.BlockSpec((tall, wide), lambda i: (0, i)),
        out_shape=jax.ShapeDtypeStruct((tall, cols), jnp.float32),
        compiler_params=pltpu.CompilerParams(vmem_limit_bytes=56 * MIB),
        cost_estimate=SMALL,
        name="hidden_deriv",
    )(tokens, weight)


def update_kernel(count, place_ref, weight_ref, momentum_ref, *refs):
    grad_refs = refs[:count]
    new_weight_ref, new_momentum_ref = refs[-2:]
    for m, grad_ref in enumerate(grad_refs):

        @pl.when(pl.program_id(1) == m)
        def _():
            grad = grad_ref[0].astype(jnp.float32)
            moment = momentum_ref[0].astype(jnp.float32)
            weight = weight_ref[0].astype(jnp.float32)
            mix = beta_first * moment + (1.0 - beta_first) * grad
            new_weight_ref[0] = weight * (1.0 - step_rate * decay_rate) - step_rate * jnp.tanh(
                mix / sign_width
            )
            new_momentum_ref[0] = (beta_second * moment + (1.0 - beta_second) * grad).astype(
                jnp.bfloat16
            )


def update(place, grads, weight, momentum):
    sources, rows, cols = weight.shape
    count = len(grads)

    def source(far, m, place):
        return place[0] ^ m ^ (far * count)

    wide = pl.BlockSpec((1, rows, cols), lambda far, m, place: (0, 0, source(far, m, place)))
    return pl.pallas_call(
        functools.partial(update_kernel, count),
        grid_spec=pltpu.PrefetchScalarGridSpec(
            num_scalar_prefetch=1,
            grid=(2, count),
            in_specs=[
                pl.BlockSpec((1, rows, cols), lambda far, m, place: (source(far, m, place), 0, 0)),
                wide,
            ]
            + [pl.BlockSpec((1, rows, cols), lambda far, m, place: (far, 0, 0))] * count,
            out_specs=[wide, wide],
        ),
        out_shape=[
            jax.ShapeDtypeStruct(momentum.shape, jnp.float32),
            jax.ShapeDtypeStruct(momentum.shape, jnp.bfloat16),
        ],
        compiler_params=pltpu.CompilerParams(vmem_limit_bytes=56 * MIB),
        cost_estimate=SMALL,
        name="lion_step",
    )(place.reshape(1), weight, momentum, *grads)


def body(out_grad, gate_saved, up_saved, routing, down_weight, momentum):
    experts = lax.axis_size("expert")
    shards = lax.axis_size("dp")
    group_tok, topk, cols = gate_saved.shape
    width = out_grad.shape[1]
    rows = momentum.shape[1]
    mine = lax.axis_index("expert")
    place = lax.axis_index("dp")
    span = shards // 2
    each = range(experts)

    half = experts // 2
    others = sorted(range(2, experts, 2), key=lambda m: (bin(m).count("1"), -m))

    blocks = [swapped(out_grad, "dp", m) for m in range(0, shards, 2)]
    named = (routing ^ mine).reshape(1, group_tok * topk)
    upper = place // span
    twice, *own_picked = picked_rows(
        [gate_saved.reshape(-1, cols), up_saved.reshape(-1, cols)],
        named,
        group_tok,
        experts,
        upper,
    )
    blocks, twice, own_picked = stage(blocks, twice, own_picked)

    pairs = [[i, i + span] for i in range(span)]
    other_twice = lax.all_to_all(
        twice, "dp", split_axis=0, concat_axis=0, tiled=True, axis_index_groups=pairs
    )

    held = {0: placed_blocks(blocks, place // 2)}
    for m in others:
        held[m] = swapped(held[m & (m - 1)], "expert", m & -m)
    beside = {0: swapped(held[0], "dp", 1)}
    held, beside, own_picked = stage(held, beside, own_picked)

    last = (place & 1) != 0
    for m in others:
        beside[m] = swapped(held[m], "dp", 1)
    own_got = swapped(own_picked[-1], "expert", half)
    tokens = {}
    for m in [0] + others:
        theirs = after(beside[m], other_twice) if m else beside[m]
        tokens[m] = in_order(held[m], theirs, last).reshape(group_tok, width)
        tokens[m + 1] = swapped(tokens[m], "expert", 1)
    tokens = [tokens[m] for m in each]
    own_rows = spread(own_picked, own_got, experts)
    tokens, own_rows = stage(tokens, own_rows)

    other_picked = picked_rows([other_twice], named, group_tok, experts, 1 - upper)
    other_got = swapped(other_picked[-1], "expert", half)

    def shard_terms(hidden_rows, before):
        if rows % 128 == 0:
            return terms(tokens, hidden_rows, rows, span, lambda place, m: place ^ m, place, before)
        tall = width // 8
        total = terms(
            tokens, hidden_rows, tall, 4, lambda place, m: place // span * 4 + m, place
        )
        total = jnp.concatenate(total, axis=1)
        blocks = [
            lax.dynamic_slice_in_dim(total, (place % span ^ m) * rows, rows, axis=1)
            for m in range(span)
        ]
        return [jnp.concatenate(pair, axis=0) for pair in zip(before, blocks)] if before else blocks

    own_terms = shard_terms(own_rows, ())
    weight, own_terms = stage(down_weight[0], own_terms)
    derivs = [deriv_of(tokens[m], weight, m > 0) for m in each]
    derivs = derivs[:1] + [deriv.astype(jnp.float16) for deriv in derivs[1:]]

    other_got, other_picked, derivs = stage(other_got, other_picked, derivs)
    other_rows = spread(other_picked, other_got, experts)
    both_terms = shard_terms(other_rows, own_terms)

    weights = lax.all_to_all(
        after(down_weight, other_twice).reshape(shards, rows, cols),
        "dp",
        split_axis=0,
        concat_axis=0,
        tiled=True,
    )

    grads = [swapped(both_terms[m], "dp", m) for m in range(span)]

    gate_saved, up_saved, _ = stage(gate_saved, up_saved, derivs)
    gate = gate_saved.astype(jnp.float32)
    up = up_saved.astype(jnp.float32)
    sigma = jax.nn.sigmoid(gate)
    deriv = jnp.zeros(gate.shape, jnp.float32)
    for m in each:
        chosen = (routing == (mine ^ m))[:, :, None]
        back = unpacked(swapped(derivs[m], "expert", m), group_tok) if m else derivs[m]
        deriv = jnp.where(chosen, back[:, None, :], deriv)
    d_up = (deriv * gate * sigma).astype(jnp.bfloat16)
    d_gate = (deriv * up * sigma * (1.0 + gate * (1.0 - sigma))).astype(jnp.bfloat16)

    new_weight, new_momentum = update(place, grads, weights, momentum)
    return (d_gate, d_up, new_weight, new_momentum)


def solution(mesh):
    placed = (
        P(("expert", "dp"), None),
        P("expert", None, "dp"),
        P("expert", None, "dp"),
        P("expert", None),
        P("expert", None, "dp"),
        P("expert", "dp", None),
    )
    return jax.shard_map(
        body,
        mesh=mesh,
        in_specs=placed,
        out_specs=(
            P("expert", None, "dp"),
            P("expert", None, "dp"),
            P("expert", "dp", None),
            P("expert", "dp", None),
        ),
        check_vma=False,
    )
```

```python
import functools

import jax
import jax.numpy as jnp
from jax import lax
from jax.experimental import pallas as pl
from jax.experimental.pallas import tpu as pltpu
from jax.sharding import PartitionSpec as P

beta_first = 0.9
beta_second = 0.99
step_rate = 0.01
decay_rate = 1.0
sign_width = 10.0
MIB = 1024 * 1024
TOP = 14.0
SMALL = pl.CostEstimate(flops=1024, bytes_accessed=1024, transcendentals=0)


def swapped(array, axis, mask):
    if mask == 0:
        return array
    size = lax.axis_size(axis)
    return lax.ppermute(array, axis, [(i, i ^ mask) for i in range(size)])


def after(value, *others):
    return lax.optimization_barrier((value, *others))[0]


def order_kernel(place_ref, mine_ref, theirs_ref, out_ref):
    out_ref[0, place_ref[0]] = mine_ref[0]
    out_ref[0, 1 - place_ref[0]] = theirs_ref[0]


def stage(*values):
    return lax.optimization_barrier(values)


def in_order(mine, theirs, bit):
    count, some, width = mine.shape
    one = pl.BlockSpec((1, some, width), lambda i, place: (i, 0, 0))
    both = pl.pallas_call(
        order_kernel,
        grid_spec=pltpu.PrefetchScalarGridSpec(
            num_scalar_prefetch=1,
            grid=(count,),
            in_specs=[one, one],
            out_specs=pl.BlockSpec((1, 2, some, width), lambda i, place: (i, 0, 0, 0)),
        ),
        out_shape=jax.ShapeDtypeStruct((count, 2, some, width), mine.dtype),
        cost_estimate=SMALL,
        name="side_by_side",
    )(bit.astype(jnp.int32).reshape(1), mine, theirs)
    return both.reshape(2 * count, some, width)


def place_kernel(place_ref, *refs):
    for m, block_ref in enumerate(refs[:-1]):
        refs[-1][place_ref[0] ^ m] = block_ref[...]


def placed_blocks(blocks, place):
    count = len(blocks)
    return pl.pallas_call(
        place_kernel,
        grid_spec=pltpu.PrefetchScalarGridSpec(
            num_scalar_prefetch=1,
            grid=(1,),
            in_specs=[pl.BlockSpec(blocks[0].shape, lambda i, place: (0, 0))] * count,
            out_specs=pl.BlockSpec((count,) + blocks[0].shape, lambda i, place: (0, 0, 0)),
        ),
        out_shape=jax.ShapeDtypeStruct((count,) + blocks[0].shape, blocks[0].dtype),
        compiler_params=pltpu.CompilerParams(vmem_limit_bytes=56 * MIB),
        cost_estimate=SMALL,
        name="placed_blocks",
    )(place.reshape(1), *blocks)


def pick(hidden, named, out_refs):
    count_rows = hidden.shape[0]
    tokens = out_refs[0].shape[1]
    topk = count_rows // tokens
    token = lax.broadcasted_iota(jnp.int32, (tokens, count_rows), 0)
    row = lax.broadcasted_iota(jnp.int32, (tokens, count_rows), 1)
    here = (row >= token * topk) & (row < token * topk + topk)
    m = 0
    for out_ref in out_refs:
        for i in range(out_ref.shape[0]):
            chosen = jnp.where(here & (named == m), 1.0, 0.0).astype(jnp.bfloat16)
            out_ref[i] = jnp.dot(chosen, hidden, preferred_element_type=jnp.float32).astype(
                jnp.bfloat16
            )
            m += 1


def hidden_kernel(place_ref, gate_ref, up_ref, named_ref, twice_ref, *out_refs):
    gate = gate_ref[...].astype(jnp.float32)
    up = up_ref[...].astype(jnp.float32)
    hidden = (gate * jax.nn.sigmoid(gate) * up).astype(jnp.bfloat16)
    twice_ref[0] = hidden
    twice_ref[1] = hidden
    pick(hidden, named_ref[pl.ds(pl.program_id(0), 1), :], out_refs)


def pick_kernel(place_ref, hidden_ref, named_ref, *out_refs):
    pick(hidden_ref[0], named_ref[pl.ds(pl.program_id(0), 1), :], out_refs)


def picked_rows(arrays, named, group_tok, experts, which):
    cols = arrays[0].shape[-1]
    topk = named.shape[1] // group_tok
    steps = 4
    some = group_tok // steps
    fresh = len(arrays) == 2
    sizes = [1] + [1 << b for b in range(experts.bit_length() - 1)]
    out_shape = [jax.ShapeDtypeStruct((n, group_tok, cols), jnp.bfloat16) for n in sizes]
    out_specs = [pl.BlockSpec((n, some, cols), lambda i, which: (0, i, 0)) for n in sizes]
    if fresh:
        in_specs = [pl.BlockSpec((some * topk, cols), lambda i, which: (i, 0))] * 2
        out_shape = [
            jax.ShapeDtypeStruct((2, group_tok * topk, cols), jnp.bfloat16)
        ] + out_shape
        out_specs = [pl.BlockSpec((2, some * topk, cols), lambda i, which: (0, i, 0))] + out_specs
    else:
        in_specs = [pl.BlockSpec((1, some * topk, cols), lambda i, which: (which[0], i, 0))]
    return pl.pallas_call(
        hidden_kernel if fresh else pick_kernel,
        grid_spec=pltpu.PrefetchScalarGridSpec(
            num_scalar_prefetch=1,
            grid=(steps,),
            in_specs=in_specs + [pl.BlockSpec((steps, some * topk), lambda i, which: (0, 0))],
            out_specs=out_specs,
        ),
        out_shape=out_shape,
        compiler_params=pltpu.CompilerParams(vmem_limit_bytes=56 * MIB),
        cost_estimate=SMALL,
        name="hidden_rows",
    )(which.reshape(1), *arrays, named.reshape(steps, some * topk))


def spread(picked, got, experts):
    half = experts // 2
    held = {0: {(1 << i) >> 1: rows for i, rows in enumerate(picked)}}
    bit = half
    while bit:
        for group in list(held):
            rows = got if bit == half else swapped(held[group][bit], "expert", bit)
            held[group ^ bit] = {0: rows[:1]}
            for i in range(bit.bit_length() - 1):
                held[group ^ bit][1 << i] = rows[1 << i : 2 << i]
        bit //= 2
    return [held[m][0][0] for m in range(experts)]


def term_kernel(count, steps, place_ref, *refs):
    tokens, hidden, before = refs[:count], refs[count : 2 * count], refs[2 * count : -steps]
    total = None
    for token_ref, hidden_ref in zip(tokens, hidden):
        one = lax.dot_general(
            token_ref[...],
            hidden_ref[...],
            (((0,), (0,)), ((), ())),
            preferred_element_type=jnp.float32,
        )
        total = one if total is None else total + one
    total = total.astype(jnp.bfloat16)
    for m, out_ref in enumerate(refs[-steps:]):

        @pl.when(pl.program_id(0) == m)
        def _():
            if before:
                out_ref[0] = before[m][0]
            out_ref[out_ref.shape[0] - 1] = total


def terms(tokens, hidden, tall, steps, block_of, place, before=()):
    group_tok, width = tokens[0].shape
    cols = hidden[0].shape[1]
    count = len(tokens)
    deep = 2 if before else 1
    return pl.pallas_call(
        functools.partial(term_kernel, count, steps),
        grid_spec=pltpu.PrefetchScalarGridSpec(
            num_scalar_prefetch=1,
            grid=(steps,),
            in_specs=[
                pl.BlockSpec((group_tok, tall), lambda m, place: (0, block_of(place[0], m)))
            ]
            * count
            + [pl.BlockSpec((group_tok, cols), lambda m, place: (0, 0))] * count
            + [pl.BlockSpec((1, tall, cols), lambda m, place: (0, 0, 0))] * len(before),
            out_specs=[pl.BlockSpec((deep, tall, cols), lambda m, place: (0, 0, 0))] * steps,
        ),
        out_shape=[jax.ShapeDtypeStruct((deep, tall, cols), jnp.bfloat16)] * steps,
        compiler_params=pltpu.CompilerParams(vmem_limit_bytes=56 * MIB),
        cost_estimate=SMALL,
        name="group_terms",
    )(place.reshape(1), *tokens, *hidden, *before)


def deriv_kernel(tokens_ref, weight_ref, out_ref):
    out_ref[...] = jnp.dot(
        tokens_ref[...], weight_ref[...], preferred_element_type=jnp.float32
    )


def packed_kernel(tokens_ref, weight_ref, out_ref):
    deriv = jnp.dot(tokens_ref[...], weight_ref[...], preferred_element_type=jnp.float32)
    group_tok = deriv.shape[0]
    largest = jnp.max(jnp.abs(deriv), axis=0, keepdims=True)
    power = jnp.ceil(jnp.log2(jnp.maximum(largest, 2.0**-100)))
    out_ref[:group_tok, :] = deriv * jnp.exp2(TOP - power)
    rest = out_ref.shape[0] - group_tok
    out_ref[group_tok:, :] = jnp.broadcast_to(power, (rest, deriv.shape[1]))


def unpacked(packed, group_tok):
    power = packed[group_tok : group_tok + 1].astype(jnp.float32)
    return packed[:group_tok].astype(jnp.float32) * jnp.exp2(power - TOP)


def deriv_of(tokens, weight, packed):
    group_tok, width = tokens.shape
    cols = weight.shape[1]
    wide = 256 if cols % 256 == 0 else cols
    tall = group_tok + 16 if packed else group_tok
    return pl.pallas_call(
        packed_kernel if packed else deriv_kernel,
        grid=(cols // wide,),
        in_specs=[
            pl.BlockSpec((group_tok, width), lambda i: (0, 0)),
            pl.BlockSpec((width, wide), lambda i: (0, i)),
        ],
        out_specs=pl.BlockSpec((tall, wide), lambda i: (0, i)),
        out_shape=jax.ShapeDtypeStruct((tall, cols), jnp.float32),
        compiler_params=pltpu.CompilerParams(vmem_limit_bytes=56 * MIB),
        cost_estimate=SMALL,
        name="hidden_deriv",
    )(tokens, weight)


def update_kernel(count, place_ref, weight_ref, momentum_ref, *refs):
    grad_refs = refs[:count]
    new_weight_ref, new_momentum_ref = refs[-2:]
    for m, grad_ref in enumerate(grad_refs):

        @pl.when(pl.program_id(1) == m)
        def _():
            grad = grad_ref[0].astype(jnp.float32)
            moment = momentum_ref[0].astype(jnp.float32)
            weight = weight_ref[0].astype(jnp.float32)
            mix = beta_first * moment + (1.0 - beta_first) * grad
            new_weight_ref[0] = weight * (1.0 - step_rate * decay_rate) - step_rate * jnp.tanh(
                mix / sign_width
            )
            new_momentum_ref[0] = (beta_second * moment + (1.0 - beta_second) * grad).astype(
                jnp.bfloat16
            )


def update(place, begin, span, grads, weight, momentum, done):
    _, rows, cols = weight.shape
    count = len(grads)

    def source(far, m, place):
        return place[0] ^ (begin + m) ^ (far * span)

    wide = pl.BlockSpec((1, rows, cols), lambda far, m, place: (0, 0, source(far, m, place)))
    return pl.pallas_call(
        functools.partial(update_kernel, count),
        grid_spec=pltpu.PrefetchScalarGridSpec(
            num_scalar_prefetch=1,
            grid=(2, count),
            in_specs=[
                pl.BlockSpec((1, rows, cols), lambda far, m, place: (source(far, m, place), 0, 0)),
                wide,
            ]
            + [pl.BlockSpec((1, rows, cols), lambda far, m, place: (far, 0, 0))] * count
            + [pl.BlockSpec(memory_space=pl.ANY)] * len(done),
            out_specs=[wide, wide],
        ),
        out_shape=[
            jax.ShapeDtypeStruct(momentum.shape, jnp.float32),
            jax.ShapeDtypeStruct(momentum.shape, jnp.bfloat16),
        ],
        input_output_aliases={3 + count + i: i for i in range(len(done))},
        compiler_params=pltpu.CompilerParams(vmem_limit_bytes=56 * MIB),
        cost_estimate=SMALL,
        name="lion_step",
    )(place.reshape(1), weight, momentum, *grads, *done)


def body(out_grad, gate_saved, up_saved, routing, down_weight, momentum):
    experts = lax.axis_size("expert")
    shards = lax.axis_size("dp")
    group_tok, topk, cols = gate_saved.shape
    width = out_grad.shape[1]
    rows = momentum.shape[1]
    mine = lax.axis_index("expert")
    place = lax.axis_index("dp")
    span = shards // 2
    each = range(experts)

    half = experts // 2
    others = sorted(range(2, experts, 2), key=lambda m: (bin(m).count("1"), -m))

    blocks = [swapped(out_grad, "dp", m) for m in range(0, shards, 2)]
    named = (routing ^ mine).reshape(1, group_tok * topk)
    upper = place // span
    twice, *own_picked = picked_rows(
        [gate_saved.reshape(-1, cols), up_saved.reshape(-1, cols)],
        named,
        group_tok,
        experts,
        upper,
    )
    blocks, twice, own_picked = stage(blocks, twice, own_picked)

    pairs = [[i, i + span] for i in range(span)]
    other_twice = lax.all_to_all(
        twice, "dp", split_axis=0, concat_axis=0, tiled=True, axis_index_groups=pairs
    )

    held = {0: placed_blocks(blocks, place // 2)}
    for m in others:
        held[m] = swapped(held[m & (m - 1)], "expert", m & -m)
    beside = {0: swapped(held[0], "dp", 1)}
    held, beside, own_picked = stage(held, beside, own_picked)

    last = (place & 1) != 0
    for m in others:
        beside[m] = swapped(held[m], "dp", 1)
    own_got = swapped(own_picked[-1], "expert", half)
    tokens = {}
    for m in [0] + others:
        theirs = after(beside[m], other_twice) if m else beside[m]
        tokens[m] = in_order(held[m], theirs, last).reshape(group_tok, width)
        tokens[m + 1] = swapped(tokens[m], "expert", 1)
    tokens = [tokens[m] for m in each]
    own_rows = spread(own_picked, own_got, experts)
    tokens, own_rows = stage(tokens, own_rows)

    other_picked = picked_rows([other_twice], named, group_tok, experts, 1 - upper)
    other_got = swapped(other_picked[-1], "expert", half)

    def shard_terms(hidden_rows, before):
        if rows % 128 == 0:
            return terms(tokens, hidden_rows, rows, span, lambda place, m: place ^ m, place, before)
        tall = width // 8
        total = terms(
            tokens, hidden_rows, tall, 4, lambda place, m: place // span * 4 + m, place
        )
        total = jnp.concatenate(total, axis=1)
        blocks = [
            lax.dynamic_slice_in_dim(total, (place % span ^ m) * rows, rows, axis=1)
            for m in range(span)
        ]
        return [jnp.concatenate(pair, axis=0) for pair in zip(before, blocks)] if before else blocks

    own_terms = shard_terms(own_rows, ())
    weight, own_terms = stage(down_weight[0], own_terms)
    derivs = [deriv_of(tokens[m], weight, m > 0) for m in each]
    derivs = derivs[:1] + [deriv.astype(jnp.float16) for deriv in derivs[1:]]

    other_got, other_picked, derivs = stage(other_got, other_picked, derivs)
    other_rows = spread(other_picked, other_got, experts)
    both_terms = shard_terms(other_rows, own_terms)

    weights = lax.all_to_all(
        after(down_weight, other_twice).reshape(shards, rows, cols),
        "dp",
        split_axis=0,
        concat_axis=0,
        tiled=True,
    )

    grads = [swapped(both_terms[m], "dp", m) for m in range(span)]

    gate_saved, up_saved, _ = stage(gate_saved, up_saved, derivs)
    gate = gate_saved.astype(jnp.float32)
    up = up_saved.astype(jnp.float32)
    sigma = jax.nn.sigmoid(gate)
    deriv = jnp.zeros(gate.shape, jnp.float32)
    for m in each:
        chosen = (routing == (mine ^ m))[:, :, None]
        back = unpacked(swapped(derivs[m], "expert", m), group_tok) if m else derivs[m]
        deriv = jnp.where(chosen, back[:, None, :], deriv)
    d_up = (deriv * gate * sigma).astype(jnp.bfloat16)
    d_gate = (deriv * up * sigma * (1.0 + gate * (1.0 - sigma))).astype(jnp.bfloat16)

    done = ()
    for begin in range(0, span, span // 2):
        some = grads[begin : begin + span // 2]
        done = update(place, begin, span, some, weights, momentum, done)
    new_weight, new_momentum = done
    return (d_gate, d_up, new_weight, new_momentum)


def solution(mesh):
    placed = (
        P(("expert", "dp"), None),
        P("expert", None, "dp"),
        P("expert", None, "dp"),
        P("expert", None),
        P("expert", None, "dp"),
        P("expert", "dp", None),
    )
    return jax.shard_map(
        body,
        mesh=mesh,
        in_specs=placed,
        out_specs=(
            P("expert", None, "dp"),
            P("expert", None, "dp"),
            P("expert", "dp", None),
            P("expert", "dp", None),
        ),
        check_vma=False,
    )
```

```python
import functools

import jax
import jax.numpy as jnp
from jax import lax
from jax.experimental import pallas as pl
from jax.experimental.pallas import tpu as pltpu
from jax.sharding import PartitionSpec as P

beta_first = 0.9
beta_second = 0.99
step_rate = 0.01
decay_rate = 1.0
sign_width = 10.0
MIB = 1024 * 1024
TOP = 14.0
SMALL = pl.CostEstimate(flops=1024, bytes_accessed=1024, transcendentals=0)


def swapped(array, axis, mask):
    if mask == 0:
        return array
    size = lax.axis_size(axis)
    return lax.ppermute(array, axis, [(i, i ^ mask) for i in range(size)])


def after(value, *others):
    return lax.optimization_barrier((value, *others))[0]


def order_kernel(place_ref, mine_ref, theirs_ref, out_ref):
    out_ref[0, place_ref[0]] = mine_ref[0]
    out_ref[0, 1 - place_ref[0]] = theirs_ref[0]


def stage(*values):
    return lax.optimization_barrier(values)


def in_order(mine, theirs, bit):
    count, some, width = mine.shape
    one = pl.BlockSpec((1, some, width), lambda i, place: (i, 0, 0))
    both = pl.pallas_call(
        order_kernel,
        grid_spec=pltpu.PrefetchScalarGridSpec(
            num_scalar_prefetch=1,
            grid=(count,),
            in_specs=[one, one],
            out_specs=pl.BlockSpec((1, 2, some, width), lambda i, place: (i, 0, 0, 0)),
        ),
        out_shape=jax.ShapeDtypeStruct((count, 2, some, width), mine.dtype),
        cost_estimate=SMALL,
        name="side_by_side",
    )(bit.astype(jnp.int32).reshape(1), mine, theirs)
    return both.reshape(2 * count, some, width)


def place_kernel(place_ref, *refs):
    for m, block_ref in enumerate(refs[:-1]):
        refs[-1][place_ref[0] ^ m] = block_ref[...]


def placed_blocks(blocks, place):
    count = len(blocks)
    return pl.pallas_call(
        place_kernel,
        grid_spec=pltpu.PrefetchScalarGridSpec(
            num_scalar_prefetch=1,
            grid=(1,),
            in_specs=[pl.BlockSpec(blocks[0].shape, lambda i, place: (0, 0))] * count,
            out_specs=pl.BlockSpec((count,) + blocks[0].shape, lambda i, place: (0, 0, 0)),
        ),
        out_shape=jax.ShapeDtypeStruct((count,) + blocks[0].shape, blocks[0].dtype),
        compiler_params=pltpu.CompilerParams(vmem_limit_bytes=56 * MIB),
        cost_estimate=SMALL,
        name="placed_blocks",
    )(place.reshape(1), *blocks)


def pick(hidden, named, out_refs):
    count_rows = hidden.shape[0]
    tokens = out_refs[0].shape[1]
    topk = count_rows // tokens
    token = lax.broadcasted_iota(jnp.int32, (tokens, count_rows), 0)
    row = lax.broadcasted_iota(jnp.int32, (tokens, count_rows), 1)
    here = (row >= token * topk) & (row < token * topk + topk)
    m = 0
    for out_ref in out_refs:
        for i in range(out_ref.shape[0]):
            chosen = jnp.where(here & (named == m), 1.0, 0.0).astype(jnp.bfloat16)
            out_ref[i] = jnp.dot(chosen, hidden, preferred_element_type=jnp.float32).astype(
                jnp.bfloat16
            )
            m += 1


def hidden_kernel(place_ref, gate_ref, up_ref, named_ref, twice_ref, *out_refs):
    gate = gate_ref[...].astype(jnp.float32)
    up = up_ref[...].astype(jnp.float32)
    hidden = (gate * jax.nn.sigmoid(gate) * up).astype(jnp.bfloat16)
    twice_ref[0] = hidden
    twice_ref[1] = hidden
    pick(hidden, named_ref[pl.ds(pl.program_id(0), 1), :], out_refs)


def pick_kernel(place_ref, hidden_ref, named_ref, *out_refs):
    pick(hidden_ref[0], named_ref[pl.ds(pl.program_id(0), 1), :], out_refs)


def picked_rows(arrays, named, group_tok, experts, which):
    cols = arrays[0].shape[-1]
    topk = named.shape[1] // group_tok
    steps = 4
    some = group_tok // steps
    fresh = len(arrays) == 2
    sizes = [1] + [1 << b for b in range(experts.bit_length() - 1)]
    out_shape = [jax.ShapeDtypeStruct((n, group_tok, cols), jnp.bfloat16) for n in sizes]
    out_specs = [pl.BlockSpec((n, some, cols), lambda i, which: (0, i, 0)) for n in sizes]
    if fresh:
        in_specs = [pl.BlockSpec((some * topk, cols), lambda i, which: (i, 0))] * 2
        out_shape = [
            jax.ShapeDtypeStruct((2, group_tok * topk, cols), jnp.bfloat16)
        ] + out_shape
        out_specs = [pl.BlockSpec((2, some * topk, cols), lambda i, which: (0, i, 0))] + out_specs
    else:
        in_specs = [pl.BlockSpec((1, some * topk, cols), lambda i, which: (which[0], i, 0))]
    return pl.pallas_call(
        hidden_kernel if fresh else pick_kernel,
        grid_spec=pltpu.PrefetchScalarGridSpec(
            num_scalar_prefetch=1,
            grid=(steps,),
            in_specs=in_specs + [pl.BlockSpec((steps, some * topk), lambda i, which: (0, 0))],
            out_specs=out_specs,
        ),
        out_shape=out_shape,
        compiler_params=pltpu.CompilerParams(vmem_limit_bytes=56 * MIB),
        cost_estimate=SMALL,
        name="hidden_rows",
    )(which.reshape(1), *arrays, named.reshape(steps, some * topk))


def spread(picked, got, experts):
    half = experts // 2
    held = {0: {(1 << i) >> 1: rows for i, rows in enumerate(picked)}}
    bit = half
    while bit:
        for group in list(held):
            rows = got if bit == half else swapped(held[group][bit], "expert", bit)
            held[group ^ bit] = {0: rows[:1]}
            for i in range(bit.bit_length() - 1):
                held[group ^ bit][1 << i] = rows[1 << i : 2 << i]
        bit //= 2
    return [held[m][0][0] for m in range(experts)]


def term_kernel(count, steps, place_ref, *refs):
    tokens, hidden, before = refs[:count], refs[count : 2 * count], refs[2 * count : -steps]
    total = None
    for token_ref, hidden_ref in zip(tokens, hidden):
        one = lax.dot_general(
            token_ref[...],
            hidden_ref[...],
            (((0,), (0,)), ((), ())),
            preferred_element_type=jnp.float32,
        )
        total = one if total is None else total + one
    total = total.astype(jnp.bfloat16)
    for m, out_ref in enumerate(refs[-steps:]):

        @pl.when(pl.program_id(0) == m)
        def _():
            if before:
                out_ref[0] = before[m][0]
            out_ref[out_ref.shape[0] - 1] = total


def terms(tokens, hidden, tall, steps, block_of, place, before=()):
    group_tok, width = tokens[0].shape
    cols = hidden[0].shape[1]
    count = len(tokens)
    deep = 2 if before else 1
    return pl.pallas_call(
        functools.partial(term_kernel, count, steps),
        grid_spec=pltpu.PrefetchScalarGridSpec(
            num_scalar_prefetch=1,
            grid=(steps,),
            in_specs=[
                pl.BlockSpec((group_tok, tall), lambda m, place: (0, block_of(place[0], m)))
            ]
            * count
            + [pl.BlockSpec((group_tok, cols), lambda m, place: (0, 0))] * count
            + [pl.BlockSpec((1, tall, cols), lambda m, place: (0, 0, 0))] * len(before),
            out_specs=[pl.BlockSpec((deep, tall, cols), lambda m, place: (0, 0, 0))] * steps,
        ),
        out_shape=[jax.ShapeDtypeStruct((deep, tall, cols), jnp.bfloat16)] * steps,
        compiler_params=pltpu.CompilerParams(vmem_limit_bytes=56 * MIB),
        cost_estimate=SMALL,
        name="group_terms",
    )(place.reshape(1), *tokens, *hidden, *before)


def deriv_kernel(tokens_ref, weight_ref, out_ref):
    out_ref[...] = jnp.dot(
        tokens_ref[...], weight_ref[...], preferred_element_type=jnp.float32
    )


def packed_kernel(tokens_ref, weight_ref, out_ref):
    deriv = jnp.dot(tokens_ref[...], weight_ref[...], preferred_element_type=jnp.float32)
    group_tok = deriv.shape[0]
    largest = jnp.max(jnp.abs(deriv), axis=0, keepdims=True)
    power = jnp.ceil(jnp.log2(jnp.maximum(largest, 2.0**-100)))
    out_ref[:group_tok, :] = deriv * jnp.exp2(TOP - power)
    rest = out_ref.shape[0] - group_tok
    out_ref[group_tok:, :] = jnp.broadcast_to(power, (rest, deriv.shape[1]))


def unpacked(packed, group_tok):
    power = packed[group_tok : group_tok + 1].astype(jnp.float32)
    return packed[:group_tok].astype(jnp.float32) * jnp.exp2(power - TOP)


def deriv_of(tokens, weight, packed):
    group_tok, width = tokens.shape
    cols = weight.shape[1]
    wide = 256 if cols % 256 == 0 else cols
    tall = group_tok + 16 if packed else group_tok
    return pl.pallas_call(
        packed_kernel if packed else deriv_kernel,
        grid=(cols // wide,),
        in_specs=[
            pl.BlockSpec((group_tok, width), lambda i: (0, 0)),
            pl.BlockSpec((width, wide), lambda i: (0, i)),
        ],
        out_specs=pl.BlockSpec((tall, wide), lambda i: (0, i)),
        out_shape=jax.ShapeDtypeStruct((tall, cols), jnp.float32),
        compiler_params=pltpu.CompilerParams(vmem_limit_bytes=56 * MIB),
        cost_estimate=SMALL,
        name="hidden_deriv",
    )(tokens, weight)


def update_kernel(count, place_ref, weight_ref, momentum_ref, *refs):
    grad_refs = refs[:count]
    new_weight_ref, new_momentum_ref = refs[-2:]
    for m, grad_ref in enumerate(grad_refs):

        @pl.when(pl.program_id(1) == m)
        def _():
            grad = grad_ref[0].astype(jnp.float32)
            moment = momentum_ref[0].astype(jnp.float32)
            weight = weight_ref[0].astype(jnp.float32)
            mix = beta_first * moment + (1.0 - beta_first) * grad
            new_weight_ref[0] = weight * (1.0 - step_rate * decay_rate) - step_rate * jnp.tanh(
                mix / sign_width
            )
            new_momentum_ref[0] = (beta_second * moment + (1.0 - beta_second) * grad).astype(
                jnp.bfloat16
            )


def update(place, begin, span, grads, weight, momentum, done):
    _, rows, cols = weight.shape
    count = len(grads)

    def source(far, m, place):
        return place[0] ^ (begin + m) ^ (far * span)

    wide = pl.BlockSpec((1, rows, cols), lambda far, m, place: (0, 0, source(far, m, place)))
    return pl.pallas_call(
        functools.partial(update_kernel, count),
        grid_spec=pltpu.PrefetchScalarGridSpec(
            num_scalar_prefetch=1,
            grid=(2, count),
            in_specs=[
                pl.BlockSpec((1, rows, cols), lambda far, m, place: (source(far, m, place), 0, 0)),
                wide,
            ]
            + [pl.BlockSpec((1, rows, cols), lambda far, m, place: (far, 0, 0))] * count
            + [pl.BlockSpec(memory_space=pl.ANY)] * len(done),
            out_specs=[wide, wide],
        ),
        out_shape=[
            jax.ShapeDtypeStruct(momentum.shape, jnp.float32),
            jax.ShapeDtypeStruct(momentum.shape, jnp.bfloat16),
        ],
        input_output_aliases={3 + count + i: i for i in range(len(done))},
        compiler_params=pltpu.CompilerParams(vmem_limit_bytes=56 * MIB),
        cost_estimate=SMALL,
        name="lion_step",
    )(place.reshape(1), weight, momentum, *grads, *done)


def body(out_grad, gate_saved, up_saved, routing, down_weight, momentum):
    experts = lax.axis_size("expert")
    shards = lax.axis_size("dp")
    group_tok, topk, cols = gate_saved.shape
    width = out_grad.shape[1]
    rows = momentum.shape[1]
    mine = lax.axis_index("expert")
    place = lax.axis_index("dp")
    span = shards // 2
    each = range(experts)

    half = experts // 2
    others = sorted(range(2, experts, 2), key=lambda m: (bin(m).count("1"), -m))

    blocks = [swapped(out_grad, "dp", m) for m in range(0, shards, 2)]
    named = (routing ^ mine).reshape(1, group_tok * topk)
    upper = place // span
    twice, *own_picked = picked_rows(
        [gate_saved.reshape(-1, cols), up_saved.reshape(-1, cols)],
        named,
        group_tok,
        experts,
        upper,
    )
    blocks, twice, own_picked = stage(blocks, twice, own_picked)

    pairs = [[i, i + span] for i in range(span)]
    other_twice = lax.all_to_all(
        twice, "dp", split_axis=0, concat_axis=0, tiled=True, axis_index_groups=pairs
    )

    held = {0: placed_blocks(blocks, place // 2)}
    for m in others:
        held[m] = swapped(held[m & (m - 1)], "expert", m & -m)
    beside = {0: swapped(held[0], "dp", 1)}
    held, beside, own_picked = stage(held, beside, own_picked)

    last = (place & 1) != 0
    for m in others:
        beside[m] = swapped(held[m], "dp", 1)
    own_got = swapped(own_picked[-1], "expert", half)
    tokens = {}
    for m in [0] + others:
        theirs = after(beside[m], other_twice) if m else beside[m]
        tokens[m] = in_order(held[m], theirs, last).reshape(group_tok, width)
        tokens[m + 1] = swapped(tokens[m], "expert", 1)
    tokens = [tokens[m] for m in each]
    own_rows = spread(own_picked, own_got, experts)
    tokens, own_rows = stage(tokens, own_rows)

    other_picked = picked_rows([other_twice], named, group_tok, experts, 1 - upper)
    other_got = swapped(other_picked[-1], "expert", half)

    def shard_terms(hidden_rows, before):
        if rows % 128 == 0:
            return terms(tokens, hidden_rows, rows, span, lambda place, m: place ^ m, place, before)
        tall = width // 8
        total = terms(
            tokens, hidden_rows, tall, 4, lambda place, m: place // span * 4 + m, place
        )
        total = jnp.concatenate(total, axis=1)
        blocks = [
            lax.dynamic_slice_in_dim(total, (place % span ^ m) * rows, rows, axis=1)
            for m in range(span)
        ]
        return [jnp.concatenate(pair, axis=0) for pair in zip(before, blocks)] if before else blocks

    own_terms = shard_terms(own_rows, ())
    weight, own_terms = stage(down_weight[0], own_terms)
    derivs = [deriv_of(tokens[m], weight, m > 0) for m in each]
    derivs = derivs[:1] + [deriv.astype(jnp.float16) for deriv in derivs[1:]]

    other_got, other_picked, derivs = stage(other_got, other_picked, derivs)
    other_rows = spread(other_picked, other_got, experts)
    both_terms = shard_terms(other_rows, own_terms)

    weights = lax.all_to_all(
        after(down_weight, other_twice).reshape(shards, rows, cols),
        "dp",
        split_axis=0,
        concat_axis=0,
        tiled=True,
    )

    grads = [swapped(both_terms[m], "dp", m) for m in range(span)]

    gate_saved, up_saved, _ = stage(gate_saved, up_saved, derivs)
    gate = gate_saved.astype(jnp.float32)
    up = up_saved.astype(jnp.float32)
    sigma = jax.nn.sigmoid(gate)
    deriv = jnp.zeros(gate.shape, jnp.float32)
    for m in each:
        chosen = (routing == (mine ^ m))[:, :, None]
        back = unpacked(swapped(derivs[m], "expert", m), group_tok) if m else derivs[m]
        deriv = jnp.where(chosen, back[:, None, :], deriv)
    d_up = (deriv * gate * sigma).astype(jnp.bfloat16)
    d_gate = (deriv * up * sigma * (1.0 + gate * (1.0 - sigma))).astype(jnp.bfloat16)

    done = ()
    for begin, end in ((0, span // 2), (span // 2, span * 3 // 4), (span * 3 // 4, span)):
        done = update(place, begin, span, grads[begin:end], weights, momentum, done)
    new_weight, new_momentum = done
    return (d_gate, d_up, new_weight, new_momentum)


def solution(mesh):
    placed = (
        P(("expert", "dp"), None),
        P("expert", None, "dp"),
        P("expert", None, "dp"),
        P("expert", None),
        P("expert", None, "dp"),
        P("expert", "dp", None),
    )
    return jax.shard_map(
        body,
        mesh=mesh,
        in_specs=placed,
        out_specs=(
            P("expert", None, "dp"),
            P("expert", None, "dp"),
            P("expert", "dp", None),
            P("expert", "dp", None),
        ),
        check_vma=False,
    )
```
